256 devices in a mesh: blk: 32 (over z_hi, y, core), op: 8 (over x, z_lo).
Axes of the slice: x: 4, y: 4, z: 8 (z_hi: 4, z_lo: 2; z = z_hi * 2 + z_lo), core: 2. Of those that a mesh axis runs over, the one named last changes fastest.
Arguments:
- initial_state: float32 [8, 6, 96, 32, 128], P('op', None, 'blk'), may hold values from -6 to 6
- target: float32 [8, 6, 96, 32, 128], P('op', None, 'blk'), may hold values from -6 to 6
- features: bfloat16 [8, 16, 96, 32, 128], P('op', None, 'blk'), may hold values from -6 to 6
- coupling: float32 [6, 6], replicated, may hold values from -1 to 1
- in_weight: bfloat16 [16, 256], replicated, may hold values from -1.5 to 1.5
- mid_weight: bfloat16 [256, 256], replicated, may hold values from -0.375 to 0.375
- top_weight: bfloat16 [256, 256], replicated, may hold values from -0.375 to 0.375
- out_weight: bfloat16 [256], replicated, may hold values from -0.375 to 0.375
- biases: float32 [3, 256], replicated, may hold values from -3 to 3
- block_count: int32 [32], P('blk'), may hold values from 1 to 3, as said below
- connectivity: int32 [96, 2], P('blk'), may hold values from 0 to 191, as said below
- orientation: int32 [96, 2], P('blk'), may hold values from 0 to 1
- rotation: int32 [96, 2], P('blk'), may hold values from -1 to 1
Outputs:
- state_final: float32 [8, 6, 96, 32, 128], P('op', None, 'blk')
- grad_in: float32 [16, 256], replicated
- grad_mid: float32 [256, 256], replicated
- grad_top: float32 [256, 256], replicated
- grad_vectors: float32 [4, 256], replicated
The draws below stay inside these ranges and needn't reach their ends.
Inputs may be any that keep to these rules, and one draw needn't show every extreme that they name: `block_count`: every device has at least one live slot, and some device has all 3 live in every draw. `connectivity`: the ghost rows of a live slot name panels of live slots; those of a slot that is not live name panel 0.
All inputs are finite; a program needn't handle non-finite values.
Results may differ from the reference program's by a relative error of at most 0.00066.
Values sent between devices are 32-bit elements; how exact they have to be, the bound alone decides.
A program may use at most 128 MiB of HBM per device.

```python
import math
import jax
import jax.numpy as jnp
from jax import lax

NV = 6
NF = 16
HID = 256
BJ = 128
BI = 32
NB = 3
OWNERS = 32
SLOTS = 96
OPS = 8


def owner_counts(key):
    counts = jax.random.randint(jax.random.fold_in(key, 101), (OWNERS,), 1, NB + 1)
    fullest = jax.random.randint(jax.random.fold_in(key, 102), (), 0, OWNERS)
    return jnp.where(jnp.arange(OWNERS) == fullest, NB, counts).astype(jnp.int32)


def draw_block_count(key, part):
    counts = owner_counts(key)
    return counts


def draw_connectivity(key, part):
    counts = owner_counts(key)
    key = jax.random.fold_in(key, 7)
    owner = jax.random.randint(jax.random.fold_in(key, 1), (SLOTS, 2), 0, OWNERS)
    spread = jax.random.randint(jax.random.fold_in(key, 2), (SLOTS, 2), 0, 1048576)
    picked = spread % counts[owner]
    side = jax.random.randint(jax.random.fold_in(key, 3), (SLOTS, 2), 0, 2)
    source = 2 * (owner * NB + picked) + side
    slot_ids = jnp.arange(SLOTS)
    alive = slot_ids % NB < counts[slot_ids // NB]
    return jnp.where(alive[:, None], source, 0).astype(jnp.int32)


def with_ends(result, key, least, top_value):
    place = [jax.random.randint(jax.random.fold_in(key, axis), (), 0, length) for axis, length in enumerate(result.shape)]
    widest = result.shape.index(max(result.shape))
    beside = place[:widest] + [(place[widest] + 1) % result.shape[widest]] + place[widest + 1:]
    return result.at[tuple(place)].set(least).at[tuple(beside)].set(top_value)


def block_scale(own_key, extent, shards, smallest, high):
    def one(dim, blocks):
        heights = jax.random.uniform(jax.random.fold_in(jax.random.fold_in(own_key, 6), dim), (blocks,), jnp.float32, smallest / len(shards), high / len(shards))
        return jnp.repeat(jnp.exp(heights), extent[dim] // blocks).reshape((-1,) + (1,) * (len(extent) - dim - 1))

    gain = one(*shards[0])
    for cut in shards[1:]:
        gain = gain * one(*cut)
    return gain


def bell_draw(key, extent, scale, reach, split=(), kind=jnp.bfloat16):
    level = block_scale(key, extent, split, -0.22, 0.18) if split else 1.0
    array = jax.random.normal(key, extent, jnp.float32) * scale * level
    return jnp.minimum(jnp.maximum(array, -reach), reach).astype(kind)


def setup_inputs(seed: int = 0) -> dict:
    arg_keys = jax.random.split(jax.random.key(seed), 14)
    initial_state = bell_draw(arg_keys[0], (OPS, NV, SLOTS, BI, BJ), 1.0, 6.0, ((0, 8), (2, 32)), jnp.float32)
    target = bell_draw(arg_keys[1], (OPS, NV, SLOTS, BI, BJ), 1.0, 6.0, ((0, 8), (2, 32)), jnp.float32)
    features = bell_draw(arg_keys[2], (OPS, NF, SLOTS, BI, BJ), 1.0, 6.0, ((0, 8), (2, 32)))
    coupling = bell_draw(arg_keys[3], (NV, NV), 0.3, 1.0, (), jnp.float32)
    in_weight = bell_draw(arg_keys[4], (NF, HID), NF ** -0.5, 1.5)
    mid_weight = bell_draw(arg_keys[5], (HID, HID), HID ** -0.5, 0.375)
    top_weight = bell_draw(arg_keys[6], (HID, HID), HID ** -0.5, 0.375)
    out_weight = bell_draw(arg_keys[7], (HID,), HID ** -0.5, 0.375)
    biases = bell_draw(arg_keys[8], (3, HID), 0.5, 3.0, (), jnp.float32)
    block_count = draw_block_count(jax.random.fold_in(arg_keys[13], 71), 0)
    connectivity = draw_connectivity(jax.random.fold_in(arg_keys[13], 71), 0)
    orientation = with_ends(jax.random.randint(arg_keys[11], (SLOTS, 2), 0, 2), jax.random.fold_in(arg_keys[11], 1), 0, 1).astype(jnp.int32)
    rotation = with_ends(jax.random.randint(arg_keys[12], (SLOTS, 2), -1, 2), jax.random.fold_in(arg_keys[12], 1), -1, 1).astype(jnp.int32)
    return dict(initial_state=initial_state, target=target, features=features, coupling=coupling, in_weight=in_weight, mid_weight=mid_weight, top_weight=top_weight, out_weight=out_weight, biases=biases, block_count=block_count, connectivity=connectivity, orientation=orientation, rotation=rotation)


tau_step = 0.2
passage_angle = 2.0 * math.pi / 36.0
highest = lax.Precision.HIGHEST

def orient_rotate(rows_in, flipped, cosines, sines):
    turned = jnp.where(flipped[None, :, None] == 1, rows_in[:, :, ::-1], rows_in)
    second = turned[2]
    third = turned[3]
    new_second = cosines[:, None] * second - sines[:, None] * third
    new_third = sines[:, None] * second + cosines[:, None] * third
    return jnp.concatenate([turned[:2], new_second[None], new_third[None], turned[4:]], axis=0)

def panel_ghosts(state, connectivity, orientation, rotation):
    panels = jnp.stack([state[:, :, 0, :], state[:, :, -1, :]], axis=2)
    panels = panels.reshape(state.shape[0], -1, state.shape[3])
    picked = jnp.take(panels, connectivity.reshape(-1), axis=1)
    angles = rotation.reshape(-1).astype(jnp.float32) * passage_angle
    ghost = orient_rotate(picked, orientation.reshape(-1), jnp.cos(angles), jnp.sin(angles))
    return (ghost[:, 0::2], ghost[:, 1::2])

def sweep_once(state, low, high, beta, coupling):
    extended = jnp.concatenate([low[:, :, None], state, high[:, :, None]], axis=2)
    row_term = extended[:, :, :-2] + extended[:, :, 2:] - 2.0 * state
    left = jnp.concatenate([state[..., :1], state[..., :-1]], axis=-1)
    right = jnp.concatenate([state[..., 1:], state[..., -1:]], axis=-1)
    laplace = row_term + left + right - 2.0 * state
    coupled = jnp.einsum('vw,wsij->vsij', coupling, state, precision=highest)
    return state + tau_step * (laplace - coupled + beta[None] * jnp.tanh(state))

def contract_lead(left_mat, right_mat):
    return lax.dot_general(left_mat, right_mat, (((0,), (0,)), ((), ())), preferred_element_type=jnp.float32)

def contract_cells(left_mat, right_mat):
    return lax.dot_general(left_mat, right_mat, (((1,), (1,)), ((), ())), preferred_element_type=jnp.float32)

def mlp_forward(inputs, in_weight, mid_weight, top_weight, out_weight, biases):
    first = jnp.tanh(contract_lead(in_weight, inputs) + biases[0][:, None]).astype(jnp.bfloat16)
    second = jnp.tanh(contract_lead(mid_weight, first) + biases[1][:, None]).astype(jnp.bfloat16)
    third = jnp.tanh(contract_lead(top_weight, second) + biases[2][:, None]).astype(jnp.bfloat16)
    beta = 1.0 + jnp.dot(out_weight[None, :], third, preferred_element_type=jnp.float32)[0]
    return (first, second, third, beta)

def mlp_backward(inputs, first, second, third, beta_cot, mid_weight, top_weight, out_weight):
    cot_half = beta_cot.astype(jnp.bfloat16)
    grad_out = jnp.dot(third, cot_half, preferred_element_type=jnp.float32)
    third_wide = third.astype(jnp.float32)
    delta_top = (out_weight.astype(jnp.float32)[:, None] * beta_cot[None, :] * (1.0 - third_wide * third_wide)).astype(jnp.bfloat16)
    grad_top = contract_cells(second, delta_top)
    second_wide = second.astype(jnp.float32)
    delta_mid = (jnp.dot(top_weight, delta_top, preferred_element_type=jnp.float32) * (1.0 - second_wide * second_wide)).astype(jnp.bfloat16)
    grad_mid = contract_cells(first, delta_mid)
    first_wide = first.astype(jnp.float32)
    delta_first = (jnp.dot(mid_weight, delta_mid, preferred_element_type=jnp.float32) * (1.0 - first_wide * first_wide)).astype(jnp.bfloat16)
    grad_in = contract_cells(inputs, delta_first)
    vectors = jnp.stack([grad_out, lax.optimization_barrier(jnp.sum(delta_first.astype(jnp.float32), axis=1)), lax.optimization_barrier(jnp.sum(delta_mid.astype(jnp.float32), axis=1)), lax.optimization_barrier(jnp.sum(delta_top.astype(jnp.float32), axis=1))])
    return (grad_in, grad_mid, grad_top, vectors)

def reference(initial_state, target, features, coupling, in_weight, mid_weight, top_weight, out_weight, biases, block_count, connectivity, orientation, rotation):
    slot_ids = jnp.arange(SLOTS)
    live = (slot_ids % NB < block_count[slot_ids // NB]).astype(jnp.float32)
    loss_scale = 2.0 / math.sqrt(OPS * SLOTS * BI * BJ)
    totals = (jnp.zeros((NF, HID), jnp.float32), jnp.zeros((HID, HID), jnp.float32), jnp.zeros((HID, HID), jnp.float32), jnp.zeros((4, HID), jnp.float32))
    finals = []
    for point in range(OPS):
        inputs = features[point].reshape(NF, SLOTS * BI * BJ)
        first, second, third, beta_flat = mlp_forward(inputs, in_weight, mid_weight, top_weight, out_weight, biases)
        beta = beta_flat.reshape(SLOTS, BI, BJ)
        start = initial_state[point]

        def forward(beta_field):
            state = start
            for sweep in range(2):
                low, high = panel_ghosts(state, connectivity, orientation, rotation)
                state = sweep_once(state, low, high, beta_field, coupling)
            return state
        final, pull = jax.vjp(forward, beta)
        final_cot = loss_scale * live[None, :, None, None] * (final - target[point])
        beta_cot = pull(final_cot)[0]
        grads = mlp_backward(inputs, first, second, third, beta_cot.reshape(-1), mid_weight, top_weight, out_weight)
        totals = tuple((total + part for total, part in zip(totals, grads)))
        finals.append(live[None, :, None, None] * final)
    return (jnp.stack(finals), totals[0], totals[1], totals[2], totals[3])
```

```python
import functools
import math

import jax
import jax.numpy as jnp
from jax import lax
from jax.experimental import pallas as pl
from jax.experimental.pallas import tpu as pltpu
from jax.sharding import PartitionSpec as P

MESH = pl.DeviceIdType.MESH
tau = 0.2
passage_angle = 2.0 * math.pi / 36.0
cos_step = math.cos(passage_angle)
sin_step = math.sin(passage_angle)
highest = lax.Precision.HIGHEST
f32 = jnp.float32
bf16 = jnp.bfloat16

NV, NS, BI, BJ, HID, NF = 6, 3, 32, 128, 256, 16
PL = 8
ZN = 4
ON = 8
NCH = 12
CW = 1024
ROW = NV * BJ


def nt(a, b):
    return lax.dot_general(a, b, (((1,), (1,)), ((), ())), preferred_element_type=f32)


def mm(a, b):
    return jnp.dot(a, b, preferred_element_type=f32)


def lanes_sum(u, lane):
    left = jnp.where(lane == 0, u, pltpu.roll(u, 1, 1))
    right = jnp.where(lane == BJ - 1, u, pltpu.roll(u, BJ - 1, 1))
    return left + right


def kernel(
    loss_scale,
    state, target, feat, coup, in_w, mid_w, top_w, out_w, biases, count, conn, orient, rot,
    out_state, out_in, out_mid, out_top, out_vec,
    x_r, first_r, second_r, third_r,
    win_t, wmid_t, wtop_t, bias_c, ow_c,
    mid_r, ts_r, tm_r, fc_r, beta_r, bc_r,
    plane, zout, zin, inner, tile_r, meta, sel_r, selt_r, ghost_r,
    cz, tbl, ret,
    gtop, gmid, gin, gvec, gout,
    rs1, a1, rs2, rs3, full, sm1, sm2, sm3,
    pl_s, pl_r, me_s, me_r, zz_s, zz_r, cz_s, cz_r, rt_s, rt_r,
    g1_s, g1_r, g2_s, g2_r, g3_s, g3_r, g4_s, g4_r, g5_s, g5_r,
    s1_s, s1_r, s2_s, s2_r, s3_s, s3_r,
):
    b = lax.axis_index("blk")
    o = lax.axis_index("op")
    z = lax.div(b, PL)
    p = lax.rem(b, PL)

    plane_peers = [lax.rem(p + d, PL) for d in range(1, PL)]
    z_peers = [lax.rem(z + d, ZN) for d in range(1, ZN)]
    o_peers = [lax.rem(o + d, ON) for d in range(1, ON)]

    def at_plane(q):
        return {"blk": z * PL + q}

    def at_z(w):
        return {"blk": w * PL + p}

    def at_o(w):
        return {"op": w}

    sent = []

    def send(src, dst, s_sem, r_sem, device):
        copy = pltpu.make_async_remote_copy(
            src_ref=src, dst_ref=dst, send_sem=s_sem, recv_sem=r_sem, device_id=device, device_id_type=MESH
        )
        copy.start()

    def got(dst, s_sem, r_sem, device):
        pltpu.make_async_remote_copy(
            src_ref=dst, dst_ref=dst, send_sem=s_sem, recv_sem=r_sem, device_id=device, device_id_type=MESH
        ).wait_recv()

    def gone(src, s_sem, r_sem, device):
        pltpu.make_async_remote_copy(
            src_ref=src, dst_ref=src, send_sem=s_sem, recv_sem=r_sem, device_id=device, device_id_type=MESH
        ).wait_send()

    barrier = pltpu.get_barrier_semaphore()
    for q in plane_peers:
        pl.semaphore_signal(barrier, inc=1, device_id=at_plane(q), device_id_type=MESH)
    for w in z_peers:
        pl.semaphore_signal(barrier, inc=1, device_id=at_z(w), device_id_type=MESH)
    for w in o_peers:
        pl.semaphore_signal(barrier, inc=1, device_id=at_o(w), device_id_type=MESH)

    rowi = lax.broadcasted_iota(jnp.int32, (8, BJ), 0)
    lane8 = lax.broadcasted_iota(jnp.int32, (8, BJ), 1)
    meta_t = jnp.full((8, BJ), -1.0, f32)
    flip_t = jnp.zeros((8, BJ), f32)
    cos_t = jnp.ones((8, BJ), f32)
    sin_t = jnp.zeros((8, BJ), f32)
    live_t = jnp.zeros((8, BJ), f32)
    live = []
    for s in range(NS):
        live.append(jnp.where(s < count[0], 1.0, 0.0).astype(f32))
        for e in range(2):
            here = rowi == 2 * s + e
            idx = conn[s, e]
            idx = idx + 2 * ((idx * 10923) >> 16)
            meta_t = jnp.where(here, idx.astype(f32), meta_t)
            flip_t = jnp.where(here, orient[s, e].astype(f32), flip_t)
            turn = rot[s, e]
            cos_t = jnp.where(here, jnp.where(turn == 0, 1.0, cos_step).astype(f32), cos_t)
            sin_t = jnp.where(here, turn.astype(f32) * sin_step, sin_t)
            live_t = jnp.where(here, live[s], live_t)
    meta[z] = meta_t
    tile_r[0] = flip_t
    tile_r[1] = cos_t
    tile_r[2] = sin_t
    tile_r[3] = live_t

    def pack(dst, field, rows):
        dst[...] = jnp.zeros((8, ROW), f32)
        for v in range(NV):
            for s in range(NS):
                for e in range(2):
                    dst[2 * s + e:2 * s + e + 1, v * BJ:(v + 1) * BJ] = field[v, s, rows[e]:rows[e] + 1, :]

    def cut(ref):
        return [ref[:, v * BJ:(v + 1) * BJ] for v in range(NV)]

    mine = plane.at[0, p]
    pack(mine, state, (0, BI - 1))

    pl.semaphore_wait(barrier, PL - 1 + ZN - 1 + ON - 1)

    def send_plane(k):
        for q in plane_peers:
            send(plane.at[k, p], plane.at[k, p], pl_s.at[k, q], pl_r.at[k, p], at_plane(q))

    for w in z_peers:
        send(meta.at[z], meta.at[z], me_s.at[w], me_r.at[z], at_z(w))
    send_plane(0)

    def pick(k):
        for q in plane_peers:
            got(plane.at[k, q], pl_s.at[k, q], pl_r.at[k, q], at_plane(q))
        every = plane[k].reshape(PL * 8, ROW)
        chosen = jnp.dot(sel_r[:, :PL * 8], every, preferred_element_type=f32, precision=highest)
        for w in range(ZN):
            zout[k, w] = chosen[8 * w:8 * w + 8]
        zin[k, z] = zout[k, z]
        for w in z_peers:
            send(zout.at[k, w], zin.at[k, z], zz_s.at[k, w], zz_r.at[k, z], at_z(w))

    def make_sel():
        for w in z_peers:
            got(meta.at[w], me_s.at[w], me_r.at[w], at_z(w))
        lane = lax.broadcasted_iota(jnp.int32, (ZN * 8, BJ), 1)
        named = meta[...].reshape(ZN * 8, BJ)
        local = named - (z * (PL * 8)).astype(f32)
        sel = jnp.where((local == lane.astype(f32)) & (lane < PL * 8), 1.0, 0.0).astype(f32)
        sel_r[...] = sel
        selt_r[...] = jnp.concatenate([sel, jnp.zeros((BJ - ZN * 8, BJ), f32)], axis=0).T

    def turned(parts, sign):
        flip, cos, sin = tile_r[0], tile_r[1], tile_r[2] * sign
        whole = jnp.concatenate(parts, axis=0)
        r = lax.broadcasted_iota(jnp.int32, (BJ, BJ), 0)
        c = lax.broadcasted_iota(jnp.int32, (BJ, BJ), 1)
        anti = jnp.where(r + c == BJ - 1, 1.0, 0.0).astype(f32)
        back = jnp.dot(whole, anti, preferred_element_type=f32, precision=highest)
        out = [jnp.where(flip > 0.5, back[8 * v:8 * v + 8], parts[v]) for v in range(NV)]
        c2 = cos * out[2] - sin * out[3]
        c3 = sin * out[2] + cos * out[3]
        return [out[0], out[1], c2, c3, out[4], out[5]]

    def ghosts(k):
        for w in z_peers:
            got(zin.at[k, w], zz_s.at[k, w], zz_r.at[k, w], at_z(w))
        total = (zin[k, 0] + zin[k, 1]) + (zin[k, 2] + zin[k, 3])
        parts = turned([total[:, v * BJ:(v + 1) * BJ] for v in range(NV)], 1.0)
        for v in range(NV):
            ghost_r[k, :, v * BJ:(v + 1) * BJ] = parts[v]

    def edge_beta():
        t = jnp.zeros((8, BJ), f32)
        for s in range(NS):
            for e in range(2):
                row = s * BI + e * (BI - 1)
                t = jnp.where(rowi == 2 * s + e, beta_r[row:row + 1, :], t)
        return t

    def edge_sweep(e, n, gh, beta_e):
        res = []
        for v in range(NV):
            lap = gh[v] + n[v] + lanes_sum(e[v], lane8) - 4.0 * e[v]
            coupled = coup[v, 0] * e[0]
            for w in range(1, NV):
                coupled = coupled + coup[v, w] * e[w]
            res.append(e[v] + tau * (lap - coupled + beta_e * jnp.tanh(e[v])))
        return res

    pad = jnp.zeros((BJ - NF, HID), f32)
    win_t[...] = jnp.concatenate([in_w[...].astype(f32), pad], axis=0).T[:, :NF].astype(bf16)
    wmid_t[...] = mid_w[...].astype(f32).T.astype(bf16)
    wtop_t[...] = top_w[...].astype(f32).T.astype(bf16)
    for k in range(3):
        bias_c[k] = jnp.broadcast_to(biases[k:k + 1, :], (BJ, HID)).T
    ow_c[...] = jnp.broadcast_to(out_w[...].astype(f32), (BJ, HID)).T
    ow_rows = jnp.broadcast_to(out_w[...].astype(f32), (16, HID)).astype(bf16)

    for s in range(NS):
        for h in range(2):
            block = feat[:, s, 16 * h:16 * h + 16, :].astype(f32).reshape(NF * 16, BJ)
            x_t = block.reshape(NF, 16, BJ)
            for r in range(16):
                chunk = 4 * s + 2 * h + r // 8
                x_r[chunk, :, (r % 8) * BJ:(r % 8 + 1) * BJ] = x_t[:, r, :].astype(bf16)

    def chunk_of(k):
        side = lax.rem(k, 2)
        slot = lax.rem(lax.div(k, 2), NS)
        inside = lax.div(k, 6)
        return 4 * slot + 3 * side + inside * (1 - 2 * side)

    SUB = 256

    def forward(k, carry):
        c = chunk_of(k)
        tile = jnp.zeros((8, BJ), f32)
        for j in range(CW // SUB):
            cols = slice(j * SUB, (j + 1) * SUB)
            b0 = jnp.concatenate([bias_c[0]] * (SUB // BJ), axis=1)
            b1 = jnp.concatenate([bias_c[1]] * (SUB // BJ), axis=1)
            b2 = jnp.concatenate([bias_c[2]] * (SUB // BJ), axis=1)
            f1 = jnp.tanh(mm(win_t[...], x_r[c, :, cols]) + b0).astype(bf16)
            first_r[c, :, cols] = f1
            f2 = jnp.tanh(mm(wmid_t[...], f1) + b1).astype(bf16)
            second_r[c, :, cols] = f2
            f3 = jnp.tanh(mm(wtop_t[...], f2) + b2).astype(bf16)
            third_r[c, :, cols] = f3
            bt = mm(ow_rows, f3)[:8] + 1.0
            for i in range(SUB // BJ):
                tile = jnp.where(rowi == j * (SUB // BJ) + i, bt[:, i * BJ:(i + 1) * BJ], tile)
        beta_r[pl.ds(pl.multiple_of(c * 8, 8), 8), :] = tile

        @pl.when(k == 2)
        def _():
            make_sel()
            pick(0)

        @pl.when(k == 5)
        def _():
            ghosts(0)
            pack(inner, state, (1, BI - 2))
            res = edge_sweep(cut(plane.at[0, p]), cut(inner), cut(ghost_r.at[0]), edge_beta())
            for v in range(NV):
                plane[1, p, :, v * BJ:(v + 1) * BJ] = res[v]
            send_plane(1)

        @pl.when(k == 9)
        def _():
            pick(1)

        return carry

    lax.fori_loop(0, NCH, forward, 0)

    rows32 = lax.broadcasted_iota(jnp.int32, (BI, BJ), 0)
    lane32 = lax.broadcasted_iota(jnp.int32, (BI, BJ), 1)

    def stencil(u, low, high):
        up = jnp.where(rows32 == 0, low, pltpu.roll(u, 1, 0))
        down = jnp.where(rows32 == BI - 1, high, pltpu.roll(u, BI - 1, 0))
        return up + down + lanes_sum(u, lane32) - 4.0 * u

    def low_high(k, s, v):
        cols = slice(v * BJ, (v + 1) * BJ)
        return ghost_r[k, 2 * s:2 * s + 1, cols], ghost_r[k, 2 * s + 1:2 * s + 2, cols]

    for s in range(NS):
        us = [state[v, s] for v in range(NV)]
        beta = beta_r[s * BI:(s + 1) * BI, :]
        for v in range(NV):
            t = jnp.tanh(us[v])
            ts_r[v, s] = t
            low, high = low_high(0, s, v)
            coupled = coup[v, 0] * us[0]
            for w in range(1, NV):
                coupled = coupled + coup[v, w] * us[w]
            mid_r[v, s] = us[v] + tau * (stencil(us[v], low, high) - coupled + beta * t)

    ghosts(1)
    pack(inner, mid_r, (1, BI - 2))
    final_e = edge_sweep(cut(plane.at[1, p]), cut(inner), cut(ghost_r.at[1]), edge_beta())
    pack(inner, target, (0, BI - 1))
    goal_e = cut(inner)
    cot_e = [tau * (loss_scale * tile_r[3] * (final_e[v] - goal_e[v])) for v in range(NV)]
    cot_e = turned(cot_e, -1.0)
    for v in range(NV):
        cz[z, :, v * BJ:(v + 1) * BJ] = cot_e[v]
    for w in z_peers:
        send(cz.at[z], cz.at[z], cz_s.at[w], cz_r.at[z], at_z(w))

    for s in range(NS):
        us = [mid_r[v, s] for v in range(NV)]
        beta = beta_r[s * BI:(s + 1) * BI, :]
        for v in range(NV):
            t = jnp.tanh(us[v])
            tm_r[v, s] = t
            low, high = low_high(1, s, v)
            coupled = coup[v, 0] * us[0]
            for w in range(1, NV):
                coupled = coupled + coup[v, w] * us[w]
            final = us[v] + tau * (stencil(us[v], low, high) - coupled + beta * t)
            out_state[v, s] = live[s] * final
            fc_r[v, s] = loss_scale * live[s] * (final - target[v, s])

    for s in range(NS):
        gs = [fc_r[v, s] for v in range(NV)]
        beta = beta_r[s * BI:(s + 1) * BI, :]
        acc = jnp.zeros((BI, BJ), f32)
        for v in range(NV):
            t = tm_r[v, s]
            coupled = coup[0, v] * gs[0]
            for w in range(1, NV):
                coupled = coupled + coup[w, v] * gs[w]
            mc = gs[v] + tau * (stencil(gs[v], 0.0, 0.0) - coupled + beta * (1.0 - t * t) * gs[v])
            acc = acc + (gs[v] * t + mc * ts_r[v, s])
        bc_r[s * BI:(s + 1) * BI, :] = tau * acc

    def table():
        for w in z_peers:
            got(cz.at[w], cz_s.at[w], cz_r.at[w], at_z(w))
        cots = cz[...].reshape(ZN * 8, ROW)
        sums = jnp.dot(selt_r[:PL * 8, :ZN * 8], cots, preferred_element_type=f32, precision=highest)
        for q in range(PL):
            tbl[q] = sums[8 * q:8 * q + 8]
        ret[p] = tbl[p]
        for q in plane_peers:
            send(tbl.at[q], ret.at[p], rt_s.at[q], rt_r.at[p], at_plane(q))

    def returned():
        for q in plane_peers:
            got(ret.at[q], rt_s.at[q], rt_r.at[q], at_plane(q))
        total = ret[0]
        for q in range(1, PL):
            total = total + ret[q]
        start = plane[0, p]
        extra = jnp.zeros((8, BJ), f32)
        for v in range(NV):
            cols = slice(v * BJ, (v + 1) * BJ)
            extra = extra + total[:, cols] * jnp.tanh(start[:, cols])
        for s in range(NS):
            for e in range(2):
                row = s * BI + e * (BI - 1)
                bc_r[row:row + 1, :] = bc_r[row:row + 1, :] + tau * extra[2 * s + e:2 * s + e + 1]

    ones = jnp.ones((16, CW), bf16)
    gout[...] = jnp.zeros((HID, BJ), f32)
    gtop[...] = jnp.zeros((HID + 16, HID), f32)
    gmid[...] = jnp.zeros((HID + 16, HID), f32)
    gin[...] = jnp.zeros((NF + 16, HID), f32)

    def back_top(k, carry):
        c = chunk_of(lax.rem(k + 6, NCH))

        @pl.when(k == 3)
        def _():
            table()

        @pl.when(k == 6)
        def _():
            returned()

        bc = bc_r[pl.ds(pl.multiple_of(c * 8, 8), 8), :]
        ch = bc.astype(bf16).astype(f32)
        RB = 64
        for i in range(HID // RB):
            rows = slice(i * RB, (i + 1) * RB)
            ow = ow_c[rows]
            acc = gout[rows]
            for j in range(CW // BJ):
                cols = slice(j * BJ, (j + 1) * BJ)
                t = third_r[c, rows, cols].astype(f32)
                acc = acc + t * ch[j:j + 1]
                third_r[c, rows, cols] = (ow * bc[j:j + 1] * (1.0 - t * t)).astype(bf16)
            gout[rows] = acc
        gtop[...] += nt(jnp.concatenate([second_r[c], ones], axis=0), third_r[c])
        return carry

    lax.fori_loop(0, NCH, back_top, 0)

    def rs_1(i, g):
        for q in plane_peers:
            part = pl.ds(pl.multiple_of(q * 32, 32), 32)
            send(g.at[part], rs1.at[i, p], g1_s.at[i, q], g1_r.at[i, p], at_plane(q))

    def rs_2(i, g):
        total = g[pl.ds(pl.multiple_of(p * 32, 32), 32), :]
        for q in plane_peers:
            got(rs1.at[i, q], g1_s.at[i, q], g1_r.at[i, q], at_plane(q))
            total = total + rs1[i, q]
        a1[i] = total
        for w in z_peers:
            part = pl.ds(pl.multiple_of(w * 8, 8), 8)
            send(a1.at[i, part], rs2.at[i, z], g2_s.at[i, w], g2_r.at[i, z], at_z(w))

    def rs_3(i):
        total = a1[i, pl.ds(pl.multiple_of(z * 8, 8), 8), :]
        for w in z_peers:
            got(rs2.at[i, w], g2_s.at[i, w], g2_r.at[i, w], at_z(w))
            total = total + rs2[i, w]
        rs3[i, o] = total
        for w in o_peers:
            send(rs3.at[i, o], rs3.at[i, o], g3_s.at[i, w], g3_r.at[i, o], at_o(w))

    def ag_2(i):
        for w in o_peers:
            got(rs3.at[i, w], g3_s.at[i, w], g3_r.at[i, w], at_o(w))
        total = rs3[i, 0]
        for w in range(1, ON):
            total = total + rs3[i, w]
        own = pl.ds(pl.multiple_of(p * 32 + z * 8, 8), 8)
        full[i, own, :] = total
        for w in z_peers:
            send(full.at[i, own], full.at[i, own], g4_s.at[i, w], g4_r.at[i, z], at_z(w))

    def ag_1(i):
        for w in z_peers:
            part = pl.ds(pl.multiple_of(p * 32 + w * 8, 8), 8)
            got(full.at[i, part], g4_s.at[i, w], g4_r.at[i, w], at_z(w))
        own = pl.ds(pl.multiple_of(p * 32, 32), 32)
        for q in plane_peers:
            send(full.at[i, own], full.at[i, own], g5_s.at[i, q], g5_r.at[i, p], at_plane(q))

    def ag_end(i, out):
        for q in plane_peers:
            part = pl.ds(pl.multiple_of(q * 32, 32), 32)
            got(full.at[i, part], g5_s.at[i, q], g5_r.at[i, q], at_plane(q))
        out[...] = full[i]

    def small_1():
        sm1[p, 0:NF] = gin[0:NF]
        sm1[p, NF:NF + 8] = gvec[...]
        for q in plane_peers:
            send(sm1.at[p], sm1.at[p], s1_s.at[q], s1_r.at[p], at_plane(q))

    def small_2():
        for q in plane_peers:
            got(sm1.at[q], s1_s.at[q], s1_r.at[q], at_plane(q))
        total = sm1[0]
        for q in range(1, PL):
            total = total + sm1[q]
        sm2[z] = total
        for w in z_peers:
            send(sm2.at[z], sm2.at[z], s2_s.at[w], s2_r.at[z], at_z(w))

    def small_3():
        for w in z_peers:
            got(sm2.at[w], s2_s.at[w], s2_r.at[w], at_z(w))
        total = (sm2[0] + sm2[1]) + (sm2[2] + sm2[3])
        sm3[o] = total
        for w in o_peers:
            send(sm3.at[o], sm3.at[o], s3_s.at[w], s3_r.at[o], at_o(w))

    def small_end():
        for w in o_peers:
            got(sm3.at[w], s3_s.at[w], s3_r.at[w], at_o(w))
        total = sm3[0]
        for w in range(1, ON):
            total = total + sm3[w]
        out_in[...] = total[0:NF]
        out_vec[...] = total[NF:NF + 4]

    rs_1(0, gtop)

    def back_mid(k, carry):
        for j in range(CW // SUB):
            cols = slice(j * SUB, (j + 1) * SUB)
            s2 = second_r[k, :, cols].astype(f32)
            d = mm(top_w[...], third_r[k, :, cols]) * (1.0 - s2 * s2)
            second_r[k, :, cols] = d.astype(bf16)
        gmid[...] += nt(jnp.concatenate([first_r[k], ones], axis=0), second_r[k])

        @pl.when(k == 6)
        def _():
            rs_2(0, gtop)

        @pl.when(k == 11)
        def _():
            rs_3(0)

        return carry

    lax.fori_loop(0, NCH, back_mid, 0)
    rs_1(1, gmid)

    def back_first(k, carry):
        for j in range(CW // SUB):
            cols = slice(j * SUB, (j + 1) * SUB)
            s1 = first_r[k, :, cols].astype(f32)
            d = mm(mid_w[...], second_r[k, :, cols]) * (1.0 - s1 * s1)
            first_r[k, :, cols] = d.astype(bf16)
        gin[...] += nt(jnp.concatenate([x_r[k], ones], axis=0), first_r[k])

        @pl.when(k == 4)
        def _():
            ag_2(0)

        @pl.when(k == 6)
        def _():
            rs_2(1, gmid)

        @pl.when(k == 9)
        def _():
            ag_1(0)

        @pl.when(k == 11)
        def _():
            rs_3(1)

        return carry

    lax.fori_loop(0, NCH, back_first, 0)

    gvec[...] = jnp.zeros((8, HID), f32)
    gvec[0:1] = jnp.sum(gout[...].T, axis=0, keepdims=True)
    gvec[1:2] = gin[NF:NF + 1]
    gvec[2:3] = gmid[HID:HID + 1]
    gvec[3:4] = gtop[HID:HID + 1]
    small_1()
    ag_2(1)
    small_2()
    ag_1(1)
    small_3()
    ag_end(0, out_top)
    ag_end(1, out_mid)
    small_end()

    for k in range(2):
        for q in plane_peers:
            gone(plane.at[k, p], pl_s.at[k, q], pl_r.at[k, p], at_plane(q))
        for w in z_peers:
            gone(zout.at[k, w], zz_s.at[k, w], zz_r.at[k, z], at_z(w))
    for w in z_peers:
        gone(meta.at[z], me_s.at[w], me_r.at[z], at_z(w))
        gone(cz.at[z], cz_s.at[w], cz_r.at[z], at_z(w))
        gone(sm2.at[z], s2_s.at[w], s2_r.at[z], at_z(w))
    for q in plane_peers:
        gone(tbl.at[q], rt_s.at[q], rt_r.at[p], at_plane(q))
        gone(sm1.at[p], s1_s.at[q], s1_r.at[p], at_plane(q))
    for w in o_peers:
        gone(sm3.at[o], s3_s.at[w], s3_r.at[o], at_o(w))
    for i, g in enumerate((gtop, gmid)):
        for q in plane_peers:
            gone(g.at[pl.ds(pl.multiple_of(q * 32, 32), 32)], g1_s.at[i, q], g1_r.at[i, p], at_plane(q))
            own = pl.ds(pl.multiple_of(p * 32, 32), 32)
            gone(full.at[i, own], g5_s.at[i, q], g5_r.at[i, p], at_plane(q))
        for w in z_peers:
            gone(a1.at[i, pl.ds(pl.multiple_of(w * 8, 8), 8)], g2_s.at[i, w], g2_r.at[i, z], at_z(w))
            own = pl.ds(pl.multiple_of(p * 32 + z * 8, 8), 8)
            gone(full.at[i, own], g4_s.at[i, w], g4_r.at[i, z], at_z(w))
        for w in o_peers:
            gone(rs3.at[i, o], g3_s.at[i, w], g3_r.at[i, o], at_o(w))


def per_device(
    initial_state, target, features, coupling, in_weight, mid_weight, top_weight, out_weight, biases,
    block_count, connectivity, orientation, rotation,
):
    cells = lax.axis_size("op") * lax.axis_size("blk") * NS * BI * BJ
    loss_scale = 2.0 / math.sqrt(cells)
    vmem = pl.BlockSpec(memory_space=pltpu.VMEM)
    smem = pl.BlockSpec(memory_space=pltpu.SMEM)
    dma = pltpu.SemaphoreType.DMA
    field = pltpu.VMEM((NV, NS, BI, BJ), f32)
    outs = pl.pallas_call(
        functools.partial(kernel, loss_scale),
        out_shape=(
            jax.ShapeDtypeStruct((NV, NS, BI, BJ), f32),
            jax.ShapeDtypeStruct((NF, HID), f32),
            jax.ShapeDtypeStruct((HID, HID), f32),
            jax.ShapeDtypeStruct((HID, HID), f32),
            jax.ShapeDtypeStruct((4, HID), f32),
        ),
        in_specs=[vmem, vmem, vmem, smem, vmem, vmem, vmem, vmem, vmem, smem, smem, smem, smem],
        out_specs=(vmem,) * 5,
        scratch_shapes=[
            pltpu.VMEM((NCH, NF, CW), bf16),
            pltpu.VMEM((NCH, HID, CW), bf16),
            pltpu.VMEM((NCH, HID, CW), bf16),
            pltpu.VMEM((NCH, HID, CW), bf16),
            pltpu.VMEM((HID, NF), bf16),
            pltpu.VMEM((HID, HID), bf16),
            pltpu.VMEM((HID, HID), bf16),
            pltpu.VMEM((3, HID, BJ), f32),
            pltpu.VMEM((HID, BJ), f32),
            field, field, field, field,
            pltpu.VMEM((NS * BI, BJ), f32),
            pltpu.VMEM((NS * BI, BJ), f32),
            pltpu.VMEM((2, PL, 8, ROW), f32),
            pltpu.VMEM((2, ZN, 8, ROW), f32),
            pltpu.VMEM((2, ZN, 8, ROW), f32),
            pltpu.VMEM((8, ROW), f32),
            pltpu.VMEM((4, 8, BJ), f32),
            pltpu.VMEM((ZN, 8, BJ), f32),
            pltpu.VMEM((ZN * 8, BJ), f32),
            pltpu.VMEM((BJ, BJ), f32),
            pltpu.VMEM((2, 8, ROW), f32),
            pltpu.VMEM((ZN, 8, ROW), f32),
            pltpu.VMEM((PL, 8, ROW), f32),
            pltpu.VMEM((PL, 8, ROW), f32),
            pltpu.VMEM((HID + 16, HID), f32),
            pltpu.VMEM((HID + 16, HID), f32),
            pltpu.VMEM((NF + 16, HID), f32),
            pltpu.VMEM((8, HID), f32),
            pltpu.VMEM((HID, BJ), f32),
            pltpu.VMEM((2, PL, 32, HID), f32),
            pltpu.VMEM((2, 32, HID), f32),
            pltpu.VMEM((2, ZN, 8, HID), f32),
            pltpu.VMEM((2, ON, 8, HID), f32),
            pltpu.VMEM((2, HID, HID), f32),
            pltpu.VMEM((PL, 24, HID), f32),
            pltpu.VMEM((ZN, 24, HID), f32),
            pltpu.VMEM((ON, 24, HID), f32),
            dma((2, PL)), dma((2, PL)), dma((ZN,)), dma((ZN,)), dma((2, ZN)), dma((2, ZN)),
            dma((ZN,)), dma((ZN,)), dma((PL,)), dma((PL,)),
            dma((2, PL)), dma((2, PL)), dma((2, ZN)), dma((2, ZN)), dma((2, ON)), dma((2, ON)),
            dma((2, ZN)), dma((2, ZN)), dma((2, PL)), dma((2, PL)),
            dma((PL,)), dma((PL,)), dma((ZN,)), dma((ZN,)), dma((ON,)), dma((ON,)),
        ],
        compiler_params=pltpu.CompilerParams(
            collective_id=0, has_side_effects=True, vmem_limit_bytes=56 * 2**20
        ),
    )(
        initial_state[0], target[0], features[0], coupling, in_weight, mid_weight, top_weight,
        out_weight.reshape(1, HID), biases, block_count, connectivity, orientation, rotation,
    )
    return (outs[0][None],) + tuple(outs[1:])


def solution(mesh):
    wide = P("op", None, "blk", None, None)
    return jax.shard_map(
        per_device,
        mesh=mesh,
        in_specs=(wide, wide, wide) + (P(),) * 6 + (P("blk"),) + (P("blk", None),) * 3,
        out_specs=(wide, P(), P(), P(), P()),
        check_vma=False,
    )
```

```python
import functools
import math

import jax
import jax.numpy as jnp
from jax import lax
from jax.experimental import pallas as pl
from jax.experimental.pallas import tpu as pltpu
from jax.sharding import PartitionSpec as P

MESH = pl.DeviceIdType.MESH
tau = 0.2
passage_angle = 2.0 * math.pi / 36.0
cos_step = math.cos(passage_angle)
sin_step = math.sin(passage_angle)
highest = lax.Precision.HIGHEST
f32 = jnp.float32
bf16 = jnp.bfloat16

NV, NS, BI, BJ, HID, NF = 6, 3, 32, 128, 256, 16
PL = 8
ZN = 4
OWN = PL * ZN
NCH = 12
CW = 1024
EDGE = NCH - 1
AN = 32
BN = 8


def row_of(s, i):
    if i == 0 or i == BI - 1:
        return 8 * EDGE + 2 * s + (i != 0)
    inner = (BI - 2) * s + i - 1
    return inner if inner < 8 * EDGE else inner + 2 * NS


def runs(s):
    whole = (BI - 2) * s
    first = min(BI - 2, 8 * EDGE - whole)
    res = [(1, whole, first)]
    if first < BI - 2:
        res.append((1 + first, row_of(s, 1 + first), BI - 2 - first))
    return res


def nt(a, b):
    return lax.dot_general(a, b, (((1,), (1,)), ((), ())), preferred_element_type=f32)


def mm(a, b):
    return jnp.dot(a, b, preferred_element_type=f32)


def lanes_sum(u, lane):
    left = jnp.where(lane == 0, u, pltpu.roll(u, 1, 1))
    right = jnp.where(lane == BJ - 1, u, pltpu.roll(u, BJ - 1, 1))
    return left + right


def kernel(
    loss_scale,
    state, target, feat, coup, in_w, mid_w, top_w, out_w, biases, count, conn, orient, rot,
    out_state, out_in, out_mid, out_top, out_vec,
    x_r, first_r, second_r, third_r,
    xs, win_t, wmid_t, wtop_t, bias_c, ow_c,
    mid_r, ts_r, tm_r, fc_r, beta_r, betan_r, bc_r, bcn_r,
    edge, gath, picked, arr, inner, tile_r, meta, sel_r, selt_r, anti, ghost_r,
    cote, cz, tbl, ret,
    gtop, gmid, gin, gout,
    ra, rb, full, sg, sa, sb, sf,
    pl_s, pl_r, me_s, me_r, zz_s, zz_r, cz_s, cz_r, rt_s, rt_r,
    a1_s, a1_r, a2_s, a2_r, a3_s, a3_r, s1_s, s1_r, s2_s, s2_r, s3_s, s3_r,
):
    b = lax.axis_index("blk")
    o = lax.axis_index("op")
    z = lax.div(b, PL)
    p = lax.rem(b, PL)
    x_at = lax.div(o, 2)
    z_lo = lax.rem(o, 2)
    a = x_at * PL + p
    zz = z * 2 + z_lo

    def at_own(q):
        return {"blk": q}

    def at_a(q):
        return {"blk": z * PL + lax.rem(q, PL), "op": lax.div(q, PL) * 2 + z_lo}

    def at_b(w):
        return {"blk": lax.div(w, 2) * PL + p, "op": x_at * 2 + lax.rem(w, 2)}

    def send(src, dst, s_sem, r_sem, device):
        copy = pltpu.make_async_remote_copy(
            src_ref=src, dst_ref=dst, send_sem=s_sem, recv_sem=r_sem, device_id=device, device_id_type=MESH
        )
        copy.start()

    def got(dst, s_sem, r_sem, device):
        pltpu.make_async_remote_copy(
            src_ref=dst, dst_ref=dst, send_sem=s_sem, recv_sem=r_sem, device_id=device, device_id_type=MESH
        ).wait_recv()

    def gone(src, s_sem, r_sem, device):
        pltpu.make_async_remote_copy(
            src_ref=src, dst_ref=src, send_sem=s_sem, recv_sem=r_sem, device_id=device, device_id_type=MESH
        ).wait_send()

    barrier = pltpu.get_barrier_semaphore()
    def every(first, last, body):
        def step(d, carry):
            body(d)
            return carry

        lax.fori_loop(first, last, step, 0)

    def greet(device):
        pl.semaphore_signal(barrier, inc=1, device_id=device, device_id_type=MESH)

    every(1, OWN, lambda d: greet(at_own(lax.rem(b + d, OWN))))
    every(PL, AN, lambda d: greet(at_a(lax.rem(x_at * PL + d, AN))))
    every(0, ZN, lambda d: greet(at_b(2 * d + 1 - z_lo)))

    rowi = lax.broadcasted_iota(jnp.int32, (8, BJ), 0)
    lane8 = lax.broadcasted_iota(jnp.int32, (8, BJ), 1)
    row1 = lax.broadcasted_iota(jnp.int32, (1, BJ), 1) - lax.rem(b, 16) * 8
    meta_t = jnp.where((row1 >= 6) & (row1 < 8), -1000.0, 0.0).astype(f32)
    flip_t = jnp.zeros((8, BJ), f32)
    cos_t = jnp.ones((8, BJ), f32)
    sin_t = jnp.zeros((8, BJ), f32)
    live_t = jnp.zeros((8, BJ), f32)
    live = []
    for s in range(NS):
        live.append(jnp.where(s < count[0], 1.0, 0.0).astype(f32))
        for e in range(2):
            here = rowi == 2 * s + e
            idx = conn[e, s]
            idx = idx + 2 * ((idx * 10923) >> 16)
            meta_t = jnp.where(row1 == 2 * s + e, idx.astype(f32), meta_t)
            flip_t = jnp.where(here, orient[e, s].astype(f32), flip_t)
            turn = rot[e, s]
            cos_t = jnp.where(here, jnp.where(turn == 0, 1.0, cos_step).astype(f32), cos_t)
            sin_t = jnp.where(here, turn.astype(f32) * sin_step, sin_t)
            live_t = jnp.where(here, live[s], live_t)
    meta[b] = meta_t
    tile_r[0] = flip_t
    tile_r[1] = cos_t
    tile_r[2] = sin_t
    tile_r[3] = live_t

    def pack(dst, field, rows):
        dst[...] = jnp.zeros((NV, 8, BJ), f32)
        for v in range(NV):
            for s in range(NS):
                for e in range(2):
                    dst[v, 2 * s + e:2 * s + e + 1, :] = field[v, s, rows[e]:rows[e] + 1, :]

    def cut(ref):
        return [ref[v] for v in range(NV)]

    def thirds(u):
        u1 = u.astype(bf16)
        u2 = (u - u1.astype(f32)).astype(bf16)
        u3 = (u - u1.astype(f32) - u2.astype(f32)).astype(bf16)
        return u1, u2, u3

    def by_rows(mask, u):
        r = mm(mask, jnp.concatenate(thirds(u), axis=1))
        return r[:, :BJ] + r[:, BJ:2 * BJ] + r[:, 2 * BJ:]

    pack(edge.at[0], state, (0, BI - 1))
    anti_r = lax.broadcasted_iota(jnp.int32, (BJ, BJ), 0)
    anti_c = lax.broadcasted_iota(jnp.int32, (BJ, BJ), 1)
    anti[...] = jnp.where(anti_r + anti_c == BJ - 1, 1.0, 0.0).astype(bf16)

    pad = jnp.zeros((BJ - NF, HID), f32)
    win_t[...] = jnp.concatenate([in_w[...].astype(f32), pad], axis=0).T[:, :NF].astype(bf16)
    wmid_t[...] = mid_w[...].astype(f32).T.astype(bf16)
    wtop_t[...] = top_w[...].astype(f32).T.astype(bf16)
    for k in range(3):
        bias_c[k] = jnp.broadcast_to(biases[k:k + 1, :], (BJ, HID)).T
    ow_c[...] = jnp.broadcast_to(out_w[...].astype(f32).reshape(1, HID), (BJ, HID)).T

    for s in range(NS):
        for h in range(2):
            xs[s, h] = feat[:, s, 16 * h:16 * h + 16, :].astype(f32).reshape(NF * 16, BJ)
    for s in range(NS):
        for h in range(2):
            for r in range(16):
                row = row_of(s, 16 * h + r)
                x_r[row // 8, :, (row % 8) * BJ:(row % 8 + 1) * BJ] = xs[s, h, pl.ds(r, NF, stride=16), :].astype(bf16)

    pl.semaphore_wait(barrier, OWN - 1 + AN - PL + ZN)

    def send_plane(k):
        for v in range(NV):
            @pl.when(p != v)
            def _():
                send(edge.at[k, v], gath.at[k, p], pl_s.at[k], pl_r.at[k], at_own(z * PL + v))

        @pl.when(p < NV)
        def _():
            gath[k, p] = edge[k, p]

    send_plane(0)
    every(1, OWN, lambda d: send(meta.at[b], meta.at[b], me_s, me_r, at_own(lax.rem(b + d, OWN))))

    def make_sel():
        got(meta.at[pl.ds(0, OWN - 1)], me_s, me_r, at_own(b))
        panel = lax.broadcasted_iota(jnp.int32, (BJ, BJ), 0)
        for h in range(2):
            named = jnp.sum(meta[16 * h:16 * h + 16], axis=0) - (z * (PL * 8)).astype(f32)
            sel = jnp.where((named == panel.astype(f32)) & (panel < PL * 8), 1.0, 0.0).astype(f32)
            selt_r[:, h * BJ:(h + 1) * BJ] = sel[:PL * 8].astype(bf16)
            sel_r[h * BJ:(h + 1) * BJ, :] = sel.T[:, :PL * 8].astype(bf16)

    def pick(k):
        @pl.when(p < NV)
        def _():
            got(gath.at[k, pl.ds(0, PL - 1)], pl_s.at[k], pl_r.at[k], at_own(b))
            chosen = by_rows(sel_r[...], gath[k].reshape(PL * 8, BJ))
            picked[k] = chosen.reshape(OWN, 8, BJ)
            arr[k, z * NV + p] = picked[k, b]

            def part(d):
                q = lax.rem(b + d, OWN)
                send(picked.at[k, q], arr.at[k, z * NV + p], zz_s.at[k], zz_r.at[k], at_own(q))

            every(1, OWN, part)

    def turned(parts, sign):
        flip, cos, sin = tile_r[0], tile_r[1], tile_r[2] * sign
        r = mm(jnp.concatenate(thirds(jnp.concatenate(parts, axis=0)), axis=0), anti[...])
        n = 8 * NV
        back = r[:n] + r[n:2 * n] + r[2 * n:]
        out = [jnp.where(flip > 0.5, back[8 * v:8 * v + 8], parts[v]) for v in range(NV)]
        c2 = cos * out[2] - sin * out[3]
        c3 = sin * out[2] + cos * out[3]
        return [out[0], out[1], c2, c3, out[4], out[5]]

    def got_some(ref, few, s_sem, r_sem):
        @pl.when(p < NV)
        def _():
            got(ref.at[pl.ds(0, few)], s_sem, r_sem, at_own(b))

        @pl.when(p >= NV)
        def _():
            got(ref.at[pl.ds(0, few + 1)], s_sem, r_sem, at_own(b))

    def gone_some(ref, few, s_sem, r_sem):
        @pl.when(p < NV)
        def _():
            gone(ref.at[pl.ds(0, few)], s_sem, r_sem, at_own(b))

        @pl.when(p >= NV)
        def _():
            gone(ref.at[pl.ds(0, few + 1)], s_sem, r_sem, at_own(b))

    def ghosts(k):
        got_some(arr.at[k], ZN * NV - 1, zz_s.at[k], zz_r.at[k])
        parts = [
            (arr[k, v] + arr[k, NV + v]) + (arr[k, 2 * NV + v] + arr[k, 3 * NV + v]) for v in range(NV)
        ]
        parts = turned(parts, 1.0)
        for v in range(NV):
            ghost_r[k, v] = parts[v]

    def edge_sweep(e, n, gh):
        res = []
        beta_e = jnp.where(rowi < 2 * NS, beta_r[8 * EDGE:8 * EDGE + 8, :], 0.0)
        for v in range(NV):
            lap = gh[v] + n[v] + lanes_sum(e[v], lane8) - 4.0 * e[v]
            coupled = coup[v, 0] * e[0]
            for w in range(1, NV):
                coupled = coupled + coup[v, w] * e[w]
            res.append(e[v] + tau * (lap - coupled + beta_e * jnp.tanh(e[v])))
        return res

    SUB = 256

    weights = (win_t, wmid_t, wtop_t)
    acts = (x_r, first_r, second_r, third_r)
    SUBS = 2 * CW // SUB

    def forward(k, carry):
        pair = (lax.rem(2 * k + EDGE, NCH), 2 * k)

        def place(j):
            return pair[j // (CW // SUB)], slice((j % (CW // SUB)) * SUB, (j % (CW // SUB) + 1) * SUB)

        def product(layer, j):
            c, cols = place(j)
            return mm(weights[layer][...], acts[layer][c, :, cols])

        tiles = [jnp.zeros((8, BJ), f32), jnp.zeros((8, BJ), f32)]

        def activate(layer, j, d):
            c, cols = place(j)
            bias = bias_c[layer]
            for i in range(SUB // BJ):
                t = jnp.tanh(d[:, i * BJ:(i + 1) * BJ] + bias).astype(bf16)
                acts[layer + 1][c, :, cols.start + i * BJ:cols.start + (i + 1) * BJ] = t
                if layer == 2:
                    bt = jnp.sum(ow_c[...] * t.astype(f32), axis=0, keepdims=True) + 1.0
                    row = (j % (CW // SUB)) * (SUB // BJ) + i
                    half = j // (CW // SUB)
                    tiles[half] = jnp.where(rowi == row, bt, tiles[half])

        tasks = [(layer, j) for layer in range(3) for j in range(SUBS)]
        held = None
        for task in tasks:
            d = product(*task)
            if held is not None:
                activate(*held)
            held = task + (d,)
        activate(*held)
        for half in range(2):
            beta_r[pl.ds(pl.multiple_of(pair[half] * 8, 8), 8), :] = tiles[half]

        @pl.when(k == 0)
        def _():
            make_sel()
            pick(0)

        @pl.when(k == 2)
        def _():
            ghosts(0)
            pack(inner, state, (1, BI - 2))
            res = edge_sweep(cut(edge.at[0]), cut(inner), cut(ghost_r.at[0]))
            for v in range(NV):
                edge[1, v] = res[v]
            send_plane(1)

        @pl.when(k == 3)
        def _():
            pick(1)

        return carry

    lax.fori_loop(0, NCH // 2, forward, 0)

    for s in range(NS):
        for e in range(2):
            g = 8 * EDGE + 2 * s + e
            row = s * BI + e * (BI - 1)
            betan_r[row:row + 1, :] = beta_r[g:g + 1, :]
        for first, place, length in runs(s):
            betan_r[s * BI + first:s * BI + first + length, :] = beta_r[place:place + length, :]

    rows32 = lax.broadcasted_iota(jnp.int32, (BI, BJ), 0)
    lane32 = lax.broadcasted_iota(jnp.int32, (BI, BJ), 1)

    def stencil(u, low, high):
        up = jnp.where(rows32 == 0, low, pltpu.roll(u, 1, 0))
        down = jnp.where(rows32 == BI - 1, high, pltpu.roll(u, BI - 1, 0))
        return up + down + lanes_sum(u, lane32) - 4.0 * u

    def low_high(k, s, v):
        return ghost_r[k, v, 2 * s:2 * s + 1, :], ghost_r[k, v, 2 * s + 1:2 * s + 2, :]

    for s in range(NS):
        us = [state[v, s] for v in range(NV)]
        beta = betan_r[s * BI:(s + 1) * BI, :]
        for v in range(NV):
            t = jnp.tanh(us[v])
            ts_r[v, s] = t
            low, high = low_high(0, s, v)
            coupled = coup[v, 0] * us[0]
            for w in range(1, NV):
                coupled = coupled + coup[v, w] * us[w]
            mid_r[v, s] = us[v] + tau * (stencil(us[v], low, high) - coupled + beta * t)

    ghosts(1)
    pack(inner, mid_r, (1, BI - 2))
    final_e = edge_sweep(cut(edge.at[1]), cut(inner), cut(ghost_r.at[1]))
    pack(inner, target, (0, BI - 1))
    goal_e = cut(inner)
    cot_e = [tau * (loss_scale * tile_r[3] * (final_e[v] - goal_e[v])) for v in range(NV)]
    cot_e = turned(cot_e, -1.0)
    for v in range(NV):
        cote[v] = cot_e[v]
    for w in range(ZN):
        for v in range(NV):
            there = w * PL + v

            @pl.when(b != there)
            def _():
                send(cote.at[v], cz.at[b], cz_s, cz_r, at_own(there))

    @pl.when(p < NV)
    def _():
        cz[b] = cote[p]

    for s in range(NS):
        us = [mid_r[v, s] for v in range(NV)]
        beta = betan_r[s * BI:(s + 1) * BI, :]
        for v in range(NV):
            t = jnp.tanh(us[v])
            tm_r[v, s] = t
            low, high = low_high(1, s, v)
            coupled = coup[v, 0] * us[0]
            for w in range(1, NV):
                coupled = coupled + coup[v, w] * us[w]
            final = us[v] + tau * (stencil(us[v], low, high) - coupled + beta * t)
            out_state[v, s] = live[s] * final
            fc_r[v, s] = loss_scale * live[s] * (final - target[v, s])

    for s in range(NS):
        gs = [fc_r[v, s] for v in range(NV)]
        beta = betan_r[s * BI:(s + 1) * BI, :]
        acc = jnp.zeros((BI, BJ), f32)
        for v in range(NV):
            t = tm_r[v, s]
            coupled = coup[0, v] * gs[0]
            for w in range(1, NV):
                coupled = coupled + coup[w, v] * gs[w]
            mc = gs[v] + tau * (stencil(gs[v], 0.0, 0.0) - coupled + beta * (1.0 - t * t) * gs[v])
            acc = acc + (gs[v] * t + mc * ts_r[v, s])
        bcn_r[s * BI:(s + 1) * BI, :] = tau * acc
        for first, place, length in runs(s):
            bc_r[place:place + length, :] = bcn_r[s * BI + first:s * BI + first + length, :]

    def table():
        @pl.when(p < NV)
        def _():
            got(cz.at[pl.ds(0, OWN - 1)], cz_s, cz_r, at_own(b))
            sums = by_rows(selt_r[...], cz[...].reshape(OWN * 8, BJ))
            tbl[...] = sums.reshape(PL, 8, BJ)
            ret[p] = tbl[p]

            def part(d):
                q = lax.rem(p + d, PL)
                send(tbl.at[q], ret.at[p], rt_s, rt_r, at_own(z * PL + q))

            every(1, PL, part)

    def returned():
        got_some(ret, NV - 1, rt_s, rt_r)
        extra = jnp.zeros((8, BJ), f32)
        for v in range(NV):
            extra = extra + ret[v] * jnp.tanh(edge[0, v])
        for s in range(NS):
            for e in range(2):
                g = 2 * s + e
                row = s * BI + e * (BI - 1)
                bc_r[8 * EDGE + g:8 * EDGE + g + 1, :] = bcn_r[row:row + 1, :] + tau * extra[g:g + 1]

    ones = jnp.ones((16, CW), bf16)
    gout[...] = jnp.zeros((HID, BJ), f32)
    gtop[...] = jnp.zeros((HID + 16, HID), f32)
    gmid[...] = jnp.zeros((HID + 16, HID), f32)
    gin[...] = jnp.zeros((NF + 16, HID), f32)

    def weigh(c, acc, left, right, fresh=None):
        part = nt(jnp.concatenate([left[c], ones], axis=0), right[c])
        if fresh is not None:
            part = jnp.where(fresh, part, 0.0)
        acc[...] = acc[...] + part

    def before(k, half):
        return lax.rem(2 * k + half + NCH - 2, NCH)

    RB = 64

    def top_delta(c):
        bc = bc_r[pl.ds(pl.multiple_of(c * 8, 8), 8), :]
        ch = bc.astype(bf16).astype(f32)
        for i in range(HID // RB):
            rows = slice(i * RB, (i + 1) * RB)
            ow = ow_c[rows]
            acc = gout[rows]
            for j in range(CW // BJ):
                cols = slice(j * BJ, (j + 1) * BJ)
                t = third_r[c, rows, cols].astype(f32)
                acc = acc + t * ch[j:j + 1]
                third_r[c, rows, cols] = (ow * bc[j:j + 1] * (1.0 - t * t)).astype(bf16)
            gout[rows] = acc

    def back_top(k, carry):
        for half in range(2):
            weigh(before(k, half), gtop, second_r, third_r, k > 0)
            top_delta(2 * k + half)
        return carry

    def layer_back(k, weight, source, act, acc, left, fresh=None):
        held = None

        def put(c, cols, d):
            for i in range(SUB // BJ):
                here = slice(cols.start + i * BJ, cols.start + (i + 1) * BJ)
                t = act[c, :, here].astype(f32)
                act[c, :, here] = (d[:, i * BJ:(i + 1) * BJ] * (1.0 - t * t)).astype(bf16)

        for half in range(2):
            c = 2 * k + half
            for j in range(CW // SUB):
                cols = slice(j * SUB, (j + 1) * SUB)
                d = mm(weight[...], source[c, :, cols])
                if held is not None:
                    put(*held)
                held = (c, cols, d)
            if half == 0:
                weigh(before(k, 0), acc, left, act, fresh)
        put(*held)
        weigh(before(k, 1), acc, left, act, fresh)

    def back_mid(k, carry):
        layer_back(k, top_w, third_r, second_r, gmid, first_r, k > 0)
        return carry

    def ar_1(i, g):
        def part(d):
            q = lax.rem(a + d, AN)
            send(g.at[pl.ds(pl.multiple_of(q * 8, 8), 8)], ra.at[i, a], a1_s.at[i], a1_r.at[i], at_a(q))

        every(1, AN, part)
        ra[i, a] = g[pl.ds(pl.multiple_of(a * 8, 8), 8), :]

    def ar_2(i):
        got(ra.at[i, pl.ds(0, AN - 1)], a1_s.at[i], a1_r.at[i], at_a(a))
        total = ra[i, 0]
        for q in range(1, AN):
            total = total + ra[i, q]
        rb[i, zz] = total
        for d in range(1, BN):
            w = lax.rem(zz + d, BN)
            send(rb.at[i, zz], rb.at[i, zz], a2_s.at[i], a2_r.at[i], at_b(w))

    def ar_3(i):
        got(rb.at[i, pl.ds(0, BN - 1)], a2_s.at[i], a2_r.at[i], at_b(zz))
        total = rb[i, 0]
        for w in range(1, BN):
            total = total + rb[i, w]
        full[i, a] = total
        every(1, AN, lambda d: send(full.at[i, a], full.at[i, a], a3_s.at[i], a3_r.at[i], at_a(lax.rem(a + d, AN))))

    def ar_4(i, out):
        got(full.at[i, pl.ds(0, AN - 1)], a3_s.at[i], a3_r.at[i], at_a(a))
        out[...] = full[i].reshape(HID, HID)

    def small_1():
        for r in range(NF):
            sg[r] = gin[r:r + 1]
        sg[NF] = jnp.sum(gout[...].T, axis=0, keepdims=True)
        sg[NF + 1] = gin[NF:NF + 1]
        sg[NF + 2] = gmid[HID:HID + 1]
        sg[NF + 3] = gtop[HID:HID + 1]
        sg[NF + 4:] = jnp.zeros((AN - NF - 4, 1, HID), f32)
        def part(d):
            q = lax.rem(a + d, AN)
            send(sg.at[q], sa.at[a], s1_s, s1_r, at_a(q))

        every(1, AN, part)
        sa[a] = sg[a]

    def small_2():
        got(sa.at[pl.ds(0, AN - 1)], s1_s, s1_r, at_a(a))
        sb[zz] = jnp.sum(sa[...], axis=0)
        for d in range(1, BN):
            w = lax.rem(zz + d, BN)
            send(sb.at[zz], sb.at[zz], s2_s, s2_r, at_b(w))

    def small_3():
        got(sb.at[pl.ds(0, BN - 1)], s2_s, s2_r, at_b(zz))
        sf[a] = jnp.sum(sb[...], axis=0)
        every(1, AN, lambda d: send(sf.at[a], sf.at[a], s3_s, s3_r, at_a(lax.rem(a + d, AN))))

    def small_4():
        got(sf.at[pl.ds(0, AN - 1)], s3_s, s3_r, at_a(a))
        for r in range(NF):
            out_in[r:r + 1] = sf[r]
        for r in range(4):
            out_vec[r:r + 1] = sf[NF + r]

    LAST = NCH // 2 - 1
    lax.fori_loop(0, LAST, back_top, 0)
    weigh(EDGE - 3, gtop, second_r, third_r)
    weigh(EDGE - 2, gtop, second_r, third_r)
    table()
    lax.fori_loop(0, LAST, back_mid, 0)
    top_delta(EDGE - 1)
    weigh(EDGE - 1, gtop, second_r, third_r)
    returned()
    top_delta(EDGE)
    weigh(EDGE, gtop, second_r, third_r)
    ar_1(0, gtop)
    layer_back(LAST, top_w, third_r, second_r, gmid, first_r)
    weigh(EDGE - 1, gmid, first_r, second_r)
    weigh(EDGE, gmid, first_r, second_r)
    ar_1(1, gmid)

    def back_first(k, carry):
        layer_back(k, mid_w, second_r, first_r, gin, x_r, k > 0)

        @pl.when(k == 3)
        def _():
            ar_2(0)

        @pl.when(k == 5)
        def _():
            ar_2(1)

        return carry

    lax.fori_loop(0, LAST + 1, back_first, 0)
    weigh(EDGE - 1, gin, x_r, first_r)
    weigh(EDGE, gin, x_r, first_r)

    small_1()
    ar_3(0)
    ar_3(1)
    small_2()
    ar_4(0, out_top)
    small_3()
    ar_4(1, out_mid)
    small_4()

    gone(meta.at[pl.ds(0, OWN - 1)], me_s, me_r, at_own(b))
    for k in range(2):
        gone_some(edge.at[k], NV - 1, pl_s.at[k], pl_r.at[k])

        @pl.when(p < NV)
        def _():
            gone(picked.at[k, pl.ds(0, OWN - 1)], zz_s.at[k], zz_r.at[k], at_own(b))
    gone_some(cz, ZN * NV - 1, cz_s, cz_r)

    @pl.when(p < NV)
    def _():
        gone(tbl.at[pl.ds(0, PL - 1)], rt_s, rt_r, at_own(b))
    for i in range(2):
        gone(ra.at[i, pl.ds(0, AN - 1)], a1_s.at[i], a1_r.at[i], at_a(a))
        gone(rb.at[i, pl.ds(0, BN - 1)], a2_s.at[i], a2_r.at[i], at_b(zz))
        gone(full.at[i, pl.ds(0, AN - 1)], a3_s.at[i], a3_r.at[i], at_a(a))
    gone(sa.at[pl.ds(0, AN - 1)], s1_s, s1_r, at_a(a))
    gone(sb.at[pl.ds(0, BN - 1)], s2_s, s2_r, at_b(zz))
    gone(sf.at[pl.ds(0, AN - 1)], s3_s, s3_r, at_a(a))


def copy_kernel(*refs):
    ins, outs, sem = refs[:5], refs[5:10], refs[10]
    copies = [pltpu.make_async_copy(ins[i], outs[i], sem.at[i]) for i in range(5)]
    for copy in copies:
        copy.start()
    for copy in copies:
        copy.wait()


def per_device(
    initial_state, target, features, coupling, in_weight, mid_weight, top_weight, out_weight, biases,
    block_count, connectivity, orientation, rotation,
):
    cells = lax.axis_size("op") * lax.axis_size("blk") * NS * BI * BJ
    loss_scale = 2.0 / math.sqrt(cells)
    vmem = pl.BlockSpec(memory_space=pltpu.VMEM)
    smem = pl.BlockSpec(memory_space=pltpu.SMEM)
    dma = pltpu.SemaphoreType.DMA
    field = pltpu.VMEM((NV, NS, BI, BJ), f32)
    outs = pl.pallas_call(
        functools.partial(kernel, loss_scale),
        out_shape=(
            jax.ShapeDtypeStruct((NV, NS, BI, BJ), f32),
            jax.ShapeDtypeStruct((NF, HID), f32),
            jax.ShapeDtypeStruct((HID, HID), f32),
            jax.ShapeDtypeStruct((HID, HID), f32),
            jax.ShapeDtypeStruct((4, HID), f32),
        ),
        in_specs=[vmem, vmem, vmem, smem, vmem, vmem, vmem, vmem, vmem, smem, smem, smem, smem],
        out_specs=(vmem,) * 5,
        scratch_shapes=[
            pltpu.VMEM((NCH, NF, CW), bf16),
            pltpu.VMEM((NCH, HID, CW), bf16),
            pltpu.VMEM((NCH, HID, CW), bf16),
            pltpu.VMEM((NCH, HID, CW), bf16),
            pltpu.VMEM((NS, 2, NF * 16, BJ), f32),
            pltpu.VMEM((HID, NF), bf16),
            pltpu.VMEM((HID, HID), bf16),
            pltpu.VMEM((HID, HID), bf16),
            pltpu.VMEM((3, HID, BJ), f32),
            pltpu.VMEM((HID, BJ), f32),
            field, field, field, field,
            pltpu.VMEM((NS * BI, BJ), f32),
            pltpu.VMEM((NS * BI, BJ), f32),
            pltpu.VMEM((NS * BI, BJ), f32),
            pltpu.VMEM((NS * BI, BJ), f32),
            pltpu.VMEM((2, NV, 8, BJ), f32),
            pltpu.VMEM((2, PL, 8, BJ), f32),
            pltpu.VMEM((2, OWN, 8, BJ), f32),
            pltpu.VMEM((2, ZN * NV, 8, BJ), f32),
            pltpu.VMEM((NV, 8, BJ), f32),
            pltpu.VMEM((4, 8, BJ), f32),
            pltpu.VMEM((OWN, 1, BJ), f32),
            pltpu.VMEM((OWN * 8, PL * 8), bf16),
            pltpu.VMEM((PL * 8, OWN * 8), bf16),
            pltpu.VMEM((BJ, BJ), bf16),
            pltpu.VMEM((2, NV, 8, BJ), f32),
            pltpu.VMEM((NV, 8, BJ), f32),
            pltpu.VMEM((OWN, 8, BJ), f32),
            pltpu.VMEM((PL, 8, BJ), f32),
            pltpu.VMEM((NV, 8, BJ), f32),
            pltpu.VMEM((HID + 16, HID), f32),
            pltpu.VMEM((HID + 16, HID), f32),
            pltpu.VMEM((NF + 16, HID), f32),
            pltpu.VMEM((HID, BJ), f32),
            pltpu.VMEM((2, AN, 8, HID), f32),
            pltpu.VMEM((2, BN, 8, HID), f32),
            pltpu.VMEM((2, AN, 8, HID), f32),
            pltpu.VMEM((AN, 1, HID), f32),
            pltpu.VMEM((AN, 1, HID), f32),
            pltpu.VMEM((BN, 1, HID), f32),
            pltpu.VMEM((AN, 1, HID), f32),
            dma((2,)), dma((2,)), dma, dma, dma((2,)), dma((2,)), dma, dma, dma, dma,
            dma((2,)), dma((2,)), dma((2,)), dma((2,)), dma((2,)), dma((2,)),
            dma, dma, dma, dma, dma, dma,
        ],
        compiler_params=pltpu.CompilerParams(
            collective_id=0, has_side_effects=True, vmem_limit_bytes=56 * 2**20
        ),
    )(
        initial_state[0], target[0], features[0], coupling, in_weight, mid_weight, top_weight,
        out_weight, biases, block_count, connectivity.T, orientation.T, rotation.T,
    )
    outs = pl.pallas_call(
        copy_kernel,
        out_shape=tuple(jax.ShapeDtypeStruct(x.shape, x.dtype) for x in outs),
        in_specs=[vmem] * 5,
        out_specs=(pl.BlockSpec(memory_space=pl.ANY),) * 5,
        scratch_shapes=[dma((5,))],
    )(*outs)
    return (outs[0][None],) + tuple(outs[1:])


def solution(mesh):
    wide = P("op", None, "blk", None, None)
    return jax.shard_map(
        per_device,
        mesh=mesh,
        in_specs=(wide, wide, wide) + (P(),) * 6 + (P("blk"),) + (P("blk", None),) * 3,
        out_specs=(wide, P(), P(), P(), P()),
        check_vma=False,
    )
```

```python
import functools
import math

import jax
import jax.numpy as jnp
from jax import lax
from jax.experimental import pallas as pl
from jax.experimental.pallas import tpu as pltpu
from jax.sharding import PartitionSpec as P

MESH = pl.DeviceIdType.MESH
tau = 0.2
passage_angle = 2.0 * math.pi / 36.0
cos_step = math.cos(passage_angle)
sin_step = math.sin(passage_angle)
highest = lax.Precision.HIGHEST
f32 = jnp.float32
bf16 = jnp.bfloat16

NV, NS, BI, BJ, HID, NF = 6, 3, 32, 128, 256, 16
PL = 8
ZN = 4
NCH = 12
CW = 1024
EDGE = NCH - 1
AN = 16
BN = 8
ROW = NV * BJ


def row_of(s, i):
    if i == 0 or i == BI - 1:
        return 8 * EDGE + 2 * s + (i != 0)
    inner = (BI - 2) * s + i - 1
    return inner if inner < 8 * EDGE else inner + 2 * NS


def runs(s):
    whole = (BI - 2) * s
    first = min(BI - 2, 8 * EDGE - whole)
    res = [(1, whole, first)]
    if first < BI - 2:
        res.append((1 + first, row_of(s, 1 + first), BI - 2 - first))
    return res


def nt(a, b):
    return lax.dot_general(a, b, (((1,), (1,)), ((), ())), preferred_element_type=f32)


def mm(a, b):
    return jnp.dot(a, b, preferred_element_type=f32)


def lanes_sum(u, lane):
    left = jnp.where(lane == 0, u, pltpu.roll(u, 1, 1))
    right = jnp.where(lane == BJ - 1, u, pltpu.roll(u, BJ - 1, 1))
    return left + right


def kernel(
    loss_scale,
    state, target, feat, coup, in_w, mid_w, top_w, out_w, biases, count, conn, orient, rot,
    out_state, out_in, out_mid, out_top, out_vec,
    x_r, first_r, second_r, third_r,
    xs, win_t, wmid_t, wtop_t, bias_c, ow_c,
    mid_r, ts_r, tm_r, fc_r, beta_r, betan_r, bc_r, bcn_r,
    plane, zout, zin, inner, tile_r, meta, sel_r, selt_r, ghost_r,
    cz, tbl, ret,
    gtop, gmid, gin, gout,
    cg, gsum, ra, rb, full, other, sg, sc, sa, sb, sf, st,
    pl_s, pl_r, me_s, me_r, zz_s, zz_r, cz_s, cz_r, rt_s, rt_r,
    c_s, c_r, a1_s, a1_r, a2_s, a2_r, a3_s, a3_r, f_s, f_r, s0_s, s0_r, s1_s, s1_r, s2_s, s2_r, s3_s, s3_r,
):
    b = lax.axis_index("blk")
    o = lax.axis_index("op")
    z = lax.div(b, PL)
    p = lax.rem(b, PL)

    plane_peers = [lax.rem(p + d, PL) for d in range(1, PL)]
    z_peers = [lax.rem(z + d, ZN) for d in range(1, ZN)]
    x_at = lax.div(o, 2)
    z_lo = lax.rem(o, 2)
    core = lax.rem(b, 2)
    a = x_at * ZN + lax.div(p, 2)
    zz = z * 2 + z_lo

    def at_plane(q):
        return {"blk": z * PL + q}

    def at_z(w):
        return {"blk": w * PL + p}

    def at_a(q):
        return {"blk": z * PL + lax.rem(q, 4) * 2 + core, "op": lax.div(q, 4) * 2 + z_lo}

    def partner():
        return {"blk": b + 1 - 2 * core}

    def at_b(w):
        return {"blk": lax.div(w, 2) * PL + p, "op": x_at * 2 + lax.rem(w, 2)}

    def send(src, dst, s_sem, r_sem, device):
        copy = pltpu.make_async_remote_copy(
            src_ref=src, dst_ref=dst, send_sem=s_sem, recv_sem=r_sem, device_id=device, device_id_type=MESH
        )
        copy.start()

    def got(dst, s_sem, r_sem, device):
        pltpu.make_async_remote_copy(
            src_ref=dst, dst_ref=dst, send_sem=s_sem, recv_sem=r_sem, device_id=device, device_id_type=MESH
        ).wait_recv()

    def gone(src, s_sem, r_sem, device):
        pltpu.make_async_remote_copy(
            src_ref=src, dst_ref=src, send_sem=s_sem, recv_sem=r_sem, device_id=device, device_id_type=MESH
        ).wait_send()

    barrier = pltpu.get_barrier_semaphore()
    def greet(device):
        pl.semaphore_signal(barrier, inc=1, device_id=device, device_id_type=MESH)

    for q in plane_peers:
        greet(at_plane(q))
    for d in range(4, AN):
        greet(at_a(lax.rem(x_at * 4 + d, AN)))
    for d in range(1, BN):
        greet(at_b(lax.rem(zz + d, BN)))

    rowi = lax.broadcasted_iota(jnp.int32, (8, BJ), 0)
    lane8 = lax.broadcasted_iota(jnp.int32, (8, BJ), 1)
    meta_t = jnp.full((8, BJ), -1.0, f32)
    flip_t = jnp.zeros((8, BJ), f32)
    cos_t = jnp.ones((8, BJ), f32)
    sin_t = jnp.zeros((8, BJ), f32)
    live_t = jnp.zeros((8, BJ), f32)
    live = []
    for s in range(NS):
        live.append(jnp.where(s < count[0], 1.0, 0.0).astype(f32))
        for e in range(2):
            here = rowi == 2 * s + e
            idx = conn[e, s]
            idx = idx + 2 * ((idx * 10923) >> 16)
            meta_t = jnp.where(here, idx.astype(f32), meta_t)
            flip_t = jnp.where(here, orient[e, s].astype(f32), flip_t)
            turn = rot[e, s]
            cos_t = jnp.where(here, jnp.where(turn == 0, 1.0, cos_step).astype(f32), cos_t)
            sin_t = jnp.where(here, turn.astype(f32) * sin_step, sin_t)
            live_t = jnp.where(here, live[s], live_t)
    meta[z] = meta_t
    tile_r[0] = flip_t
    tile_r[1] = cos_t
    tile_r[2] = sin_t
    tile_r[3] = live_t

    def pack(dst, field, rows):
        dst[...] = jnp.zeros((8, ROW), f32)
        for v in range(NV):
            for s in range(NS):
                for e in range(2):
                    dst[2 * s + e:2 * s + e + 1, v * BJ:(v + 1) * BJ] = field[v, s, rows[e]:rows[e] + 1, :]

    def cut(ref):
        return [ref[:, v * BJ:(v + 1) * BJ] for v in range(NV)]

    mine = plane.at[0, p]
    pack(mine, state, (0, BI - 1))

    pad = jnp.zeros((BJ - NF, HID), f32)
    win_t[...] = jnp.concatenate([in_w[...].astype(f32), pad], axis=0).T[:, :NF].astype(bf16)
    wmid_t[...] = mid_w[...].astype(f32).T.astype(bf16)
    wtop_t[...] = top_w[...].astype(f32).T.astype(bf16)
    for k in range(3):
        bias_c[k] = jnp.broadcast_to(biases[k:k + 1, :], (BJ, HID)).T
    ow_c[...] = jnp.broadcast_to(out_w[...].astype(f32).reshape(1, HID), (BJ, HID)).T

    for s in range(NS):
        for h in range(2):
            xs[s, h] = feat[:, s, 16 * h:16 * h + 16, :].astype(f32).reshape(NF * 16, BJ)
    for s in range(NS):
        for h in range(2):
            for r in range(16):
                row = row_of(s, 16 * h + r)
                x_r[row // 8, :, (row % 8) * BJ:(row % 8 + 1) * BJ] = xs[s, h, pl.ds(r, NF, stride=16), :].astype(bf16)

    pl.semaphore_wait(barrier, PL - 1 + AN - 4 + BN - 1)

    def send_plane(k):
        for q in plane_peers:
            send(plane.at[k, p], plane.at[k, p], pl_s.at[k, q], pl_r.at[k, p], at_plane(q))

    for w in z_peers:
        send(meta.at[z], meta.at[z], me_s.at[w], me_r.at[z], at_z(w))
    send_plane(0)

    def pick(k):
        for q in plane_peers:
            got(plane.at[k, q], pl_s.at[k, q], pl_r.at[k, q], at_plane(q))
        every = plane[k].reshape(PL * 8, ROW)
        chosen = jnp.dot(sel_r[:, :PL * 8], every, preferred_element_type=f32, precision=highest)
        for w in range(ZN):
            zout[k, w] = chosen[8 * w:8 * w + 8]
        zin[k, z] = zout[k, z]
        for w in z_peers:
            send(zout.at[k, w], zin.at[k, z], zz_s.at[k, w], zz_r.at[k, z], at_z(w))

    def make_sel():
        for w in z_peers:
            got(meta.at[w], me_s.at[w], me_r.at[w], at_z(w))
        lane = lax.broadcasted_iota(jnp.int32, (ZN * 8, BJ), 1)
        named = meta[...].reshape(ZN * 8, BJ)
        local = named - (z * (PL * 8)).astype(f32)
        sel = jnp.where((local == lane.astype(f32)) & (lane < PL * 8), 1.0, 0.0).astype(f32)
        sel_r[...] = sel
        selt_r[...] = jnp.concatenate([sel, jnp.zeros((BJ - ZN * 8, BJ), f32)], axis=0).T

    def turned(parts, sign):
        flip, cos, sin = tile_r[0], tile_r[1], tile_r[2] * sign
        whole = jnp.concatenate(parts, axis=0)
        r = lax.broadcasted_iota(jnp.int32, (BJ, BJ), 0)
        c = lax.broadcasted_iota(jnp.int32, (BJ, BJ), 1)
        anti = jnp.where(r + c == BJ - 1, 1.0, 0.0).astype(f32)
        back = jnp.dot(whole, anti, preferred_element_type=f32, precision=highest)
        out = [jnp.where(flip > 0.5, back[8 * v:8 * v + 8], parts[v]) for v in range(NV)]
        c2 = cos * out[2] - sin * out[3]
        c3 = sin * out[2] + cos * out[3]
        return [out[0], out[1], c2, c3, out[4], out[5]]

    def ghosts(k):
        for w in z_peers:
            got(zin.at[k, w], zz_s.at[k, w], zz_r.at[k, w], at_z(w))
        total = (zin[k, 0] + zin[k, 1]) + (zin[k, 2] + zin[k, 3])
        parts = turned([total[:, v * BJ:(v + 1) * BJ] for v in range(NV)], 1.0)
        for v in range(NV):
            ghost_r[k, :, v * BJ:(v + 1) * BJ] = parts[v]

    def edge_sweep(e, n, gh):
        res = []
        beta_e = jnp.where(rowi < 2 * NS, beta_r[8 * EDGE:8 * EDGE + 8, :], 0.0)
        for v in range(NV):
            lap = gh[v] + n[v] + lanes_sum(e[v], lane8) - 4.0 * e[v]
            coupled = coup[v, 0] * e[0]
            for w in range(1, NV):
                coupled = coupled + coup[v, w] * e[w]
            res.append(e[v] + tau * (lap - coupled + beta_e * jnp.tanh(e[v])))
        return res

    SUB = 256

    weights = (win_t, wmid_t, wtop_t)
    acts = (x_r, first_r, second_r, third_r)
    SUBS = 2 * CW // SUB

    def forward(k, carry):
        pair = (lax.rem(2 * k + EDGE, NCH), 2 * k)

        def place(j):
            return pair[j // (CW // SUB)], slice((j % (CW // SUB)) * SUB, (j % (CW // SUB) + 1) * SUB)

        def product(layer, j):
            c, cols = place(j)
            return mm(weights[layer][...], acts[layer][c, :, cols])

        tiles = [jnp.zeros((8, BJ), f32), jnp.zeros((8, BJ), f32)]

        def activate(layer, j, d):
            c, cols = place(j)
            bias = bias_c[layer]
            for i in range(SUB // BJ):
                t = jnp.tanh(d[:, i * BJ:(i + 1) * BJ] + bias).astype(bf16)
                acts[layer + 1][c, :, cols.start + i * BJ:cols.start + (i + 1) * BJ] = t
                if layer == 2:
                    bt = jnp.sum(ow_c[...] * t.astype(f32), axis=0, keepdims=True) + 1.0
                    row = (j % (CW // SUB)) * (SUB // BJ) + i
                    half = j // (CW // SUB)
                    tiles[half] = jnp.where(rowi == row, bt, tiles[half])

        tasks = [(layer, j) for layer in range(3) for j in range(SUBS)]
        held = None
        for task in tasks:
            d = product(*task)
            if held is not None:
                activate(*held)
            held = task + (d,)
        activate(*held)
        for half in range(2):
            beta_r[pl.ds(pl.multiple_of(pair[half] * 8, 8), 8), :] = tiles[half]

        @pl.when(k == 0)
        def _():
            make_sel()
            pick(0)

        @pl.when(k == 2)
        def _():
            ghosts(0)
            pack(inner, state, (1, BI - 2))
            res = edge_sweep(cut(plane.at[0, p]), cut(inner), cut(ghost_r.at[0]))
            for v in range(NV):
                plane[1, p, :, v * BJ:(v + 1) * BJ] = res[v]
            send_plane(1)

        @pl.when(k == 4)
        def _():
            pick(1)

        return carry

    lax.fori_loop(0, NCH // 2, forward, 0)

    for s in range(NS):
        for e in range(2):
            g = 8 * EDGE + 2 * s + e
            row = s * BI + e * (BI - 1)
            betan_r[row:row + 1, :] = beta_r[g:g + 1, :]
        for first, place, length in runs(s):
            betan_r[s * BI + first:s * BI + first + length, :] = beta_r[place:place + length, :]

    rows32 = lax.broadcasted_iota(jnp.int32, (BI, BJ), 0)
    lane32 = lax.broadcasted_iota(jnp.int32, (BI, BJ), 1)

    def stencil(u, low, high):
        up = jnp.where(rows32 == 0, low, pltpu.roll(u, 1, 0))
        down = jnp.where(rows32 == BI - 1, high, pltpu.roll(u, BI - 1, 0))
        return up + down + lanes_sum(u, lane32) - 4.0 * u

    def low_high(k, s, v):
        cols = slice(v * BJ, (v + 1) * BJ)
        return ghost_r[k, 2 * s:2 * s + 1, cols], ghost_r[k, 2 * s + 1:2 * s + 2, cols]

    for s in range(NS):
        us = [state[v, s] for v in range(NV)]
        beta = betan_r[s * BI:(s + 1) * BI, :]
        for v in range(NV):
            t = jnp.tanh(us[v])
            ts_r[v, s] = t
            low, high = low_high(0, s, v)
            coupled = coup[v, 0] * us[0]
            for w in range(1, NV):
                coupled = coupled + coup[v, w] * us[w]
            mid_r[v, s] = us[v] + tau * (stencil(us[v], low, high) - coupled + beta * t)

    ghosts(1)
    pack(inner, mid_r, (1, BI - 2))
    final_e = edge_sweep(cut(plane.at[1, p]), cut(inner), cut(ghost_r.at[1]))
    pack(inner, target, (0, BI - 1))
    goal_e = cut(inner)
    cot_e = [tau * (loss_scale * tile_r[3] * (final_e[v] - goal_e[v])) for v in range(NV)]
    cot_e = turned(cot_e, -1.0)
    for v in range(NV):
        cz[z, :, v * BJ:(v + 1) * BJ] = cot_e[v]
    for w in z_peers:
        send(cz.at[z], cz.at[z], cz_s.at[w], cz_r.at[z], at_z(w))

    for s in range(NS):
        us = [mid_r[v, s] for v in range(NV)]
        beta = betan_r[s * BI:(s + 1) * BI, :]
        for v in range(NV):
            t = jnp.tanh(us[v])
            tm_r[v, s] = t
            low, high = low_high(1, s, v)
            coupled = coup[v, 0] * us[0]
            for w in range(1, NV):
                coupled = coupled + coup[v, w] * us[w]
            final = us[v] + tau * (stencil(us[v], low, high) - coupled + beta * t)
            out_state[v, s] = live[s] * final
            fc_r[v, s] = loss_scale * live[s] * (final - target[v, s])

    for s in range(NS):
        gs = [fc_r[v, s] for v in range(NV)]
        beta = betan_r[s * BI:(s + 1) * BI, :]
        acc = jnp.zeros((BI, BJ), f32)
        for v in range(NV):
            t = tm_r[v, s]
            coupled = coup[0, v] * gs[0]
            for w in range(1, NV):
                coupled = coupled + coup[w, v] * gs[w]
            mc = gs[v] + tau * (stencil(gs[v], 0.0, 0.0) - coupled + beta * (1.0 - t * t) * gs[v])
            acc = acc + (gs[v] * t + mc * ts_r[v, s])
        bcn_r[s * BI:(s + 1) * BI, :] = tau * acc
        for first, place, length in runs(s):
            bc_r[place:place + length, :] = bcn_r[s * BI + first:s * BI + first + length, :]

    def table():
        for w in z_peers:
            got(cz.at[w], cz_s.at[w], cz_r.at[w], at_z(w))
        cots = cz[...].reshape(ZN * 8, ROW)
        sums = jnp.dot(selt_r[:PL * 8, :ZN * 8], cots, preferred_element_type=f32, precision=highest)
        for q in range(PL):
            tbl[q] = sums[8 * q:8 * q + 8]
        ret[p] = tbl[p]
        for q in plane_peers:
            send(tbl.at[q], ret.at[p], rt_s.at[q], rt_r.at[p], at_plane(q))

    def returned():
        for q in plane_peers:
            got(ret.at[q], rt_s.at[q], rt_r.at[q], at_plane(q))
        total = ret[0]
        for q in range(1, PL):
            total = total + ret[q]
        start = plane[0, p]
        extra = jnp.zeros((8, BJ), f32)
        for v in range(NV):
            cols = slice(v * BJ, (v + 1) * BJ)
            extra = extra + total[:, cols] * jnp.tanh(start[:, cols])
        for s in range(NS):
            for e in range(2):
                g = 2 * s + e
                row = s * BI + e * (BI - 1)
                bc_r[8 * EDGE + g:8 * EDGE + g + 1, :] = bcn_r[row:row + 1, :] + tau * extra[g:g + 1]

    ones = jnp.ones((16, CW), bf16)
    gout[...] = jnp.zeros((HID, BJ), f32)
    gtop[...] = jnp.zeros((HID + 16, HID), f32)
    gmid[...] = jnp.zeros((HID + 16, HID), f32)
    gin[...] = jnp.zeros((NF + 16, HID), f32)

    def weigh(c, acc, left, right, fresh=None):
        part = nt(jnp.concatenate([left[c], ones], axis=0), right[c])
        if fresh is not None:
            part = jnp.where(fresh, part, 0.0)
        acc[...] = acc[...] + part

    def before(k, half):
        return lax.rem(2 * k + half + NCH - 2, NCH)

    RB = 64

    def top_delta(c):
        bc = bc_r[pl.ds(pl.multiple_of(c * 8, 8), 8), :]
        ch = bc.astype(bf16).astype(f32)
        for i in range(HID // RB):
            rows = slice(i * RB, (i + 1) * RB)
            ow = ow_c[rows]
            acc = gout[rows]
            for j in range(CW // BJ):
                cols = slice(j * BJ, (j + 1) * BJ)
                t = third_r[c, rows, cols].astype(f32)
                acc = acc + t * ch[j:j + 1]
                third_r[c, rows, cols] = (ow * bc[j:j + 1] * (1.0 - t * t)).astype(bf16)
            gout[rows] = acc

    def back_top(k, carry):
        for half in range(2):
            weigh(before(k, half), gtop, second_r, third_r, k > 0)
            top_delta(2 * k + half)
        return carry

    def layer_back(k, weight, source, act, acc, left, fresh=None):
        held = None

        def put(c, cols, d):
            for i in range(SUB // BJ):
                here = slice(cols.start + i * BJ, cols.start + (i + 1) * BJ)
                t = act[c, :, here].astype(f32)
                act[c, :, here] = (d[:, i * BJ:(i + 1) * BJ] * (1.0 - t * t)).astype(bf16)

        for half in range(2):
            c = 2 * k + half
            for j in range(CW // SUB):
                cols = slice(j * SUB, (j + 1) * SUB)
                d = mm(weight[...], source[c, :, cols])
                if held is not None:
                    put(*held)
                held = (c, cols, d)
            if half == 0:
                weigh(before(k, 0), acc, left, act, fresh)
        put(*held)
        weigh(before(k, 1), acc, left, act, fresh)

    def back_mid(k, carry):
        layer_back(k, top_w, third_r, second_r, gmid, first_r, k > 0)
        return carry

    grads = (gtop, gmid)
    R = HID // AN

    def hand(i):
        @pl.when(core != i)
        def _():
            send(grads[i].at[pl.ds(0, HID)], cg, c_s, c_r, partner())

    def ar_1(i):
        got(cg, c_s, c_r, partner())
        gsum[...] = (grads[i][0:HID] + cg[...]).reshape(AN, R, HID)
        for d in range(1, AN):
            q = lax.rem(a + d, AN)
            send(gsum.at[q], ra.at[a], a1_s, a1_r, at_a(q))
        ra[a] = gsum[a]

    def ar_2():
        got(ra.at[pl.ds(0, AN - 1)], a1_s, a1_r, at_a(a))
        total = ra[0]
        for q in range(1, AN):
            total = total + ra[q]
        rb[zz] = total
        for d in range(1, BN):
            send(rb.at[zz], rb.at[zz], a2_s, a2_r, at_b(lax.rem(zz + d, BN)))

    def ar_3():
        got(rb.at[pl.ds(0, BN - 1)], a2_s, a2_r, at_b(zz))
        total = rb[0]
        for w in range(1, BN):
            total = total + rb[w]
        full[a] = total
        for d in range(1, AN):
            send(full.at[a], full.at[a], a3_s, a3_r, at_a(lax.rem(a + d, AN)))

    def ar_4(out):
        got(full.at[pl.ds(0, AN - 1)], a3_s, a3_r, at_a(a))
        send(full, other, f_s, f_r, partner())
        out[...] = full[...].reshape(HID, HID)

    def ar_5(out):
        got(other, f_s, f_r, partner())
        out[...] = other[...].reshape(HID, HID)

    def small_0():
        sg[0:NF] = gin[0:NF]
        sg[NF:NF + 1] = jnp.sum(gout[...].T, axis=0, keepdims=True)
        sg[NF + 1:NF + 2] = gin[NF:NF + 1]
        sg[NF + 2:NF + 3] = gmid[HID:HID + 1]
        sg[NF + 3:NF + 4] = gtop[HID:HID + 1]
        sg[NF + 4:NF + 8] = jnp.zeros((4, HID), f32)

        @pl.when(core == 1)
        def _():
            send(sg, sc, s0_s, s0_r, partner())

    def small_1():
        got(sc, s0_s, s0_r, partner())
        sa[a] = sg[...] + sc[...]
        for d in range(1, AN):
            send(sa.at[a], sa.at[a], s1_s, s1_r, at_a(lax.rem(a + d, AN)))

    def small_2():
        got(sa.at[pl.ds(0, AN - 1)], s1_s, s1_r, at_a(a))
        total = sa[0]
        for q in range(1, AN):
            total = total + sa[q]
        sb[zz] = total
        for d in range(1, BN):
            send(sb.at[zz], sb.at[zz], s2_s, s2_r, at_b(lax.rem(zz + d, BN)))

    def small_3():
        got(sb.at[pl.ds(0, BN - 1)], s2_s, s2_r, at_b(zz))
        total = sb[0]
        for w in range(1, BN):
            total = total + sb[w]
        sf[...] = total
        send(sf, st, s3_s, s3_r, partner())

    LAST = NCH // 2 - 1
    lax.fori_loop(0, LAST, back_top, 0)
    weigh(EDGE - 3, gtop, second_r, third_r)
    weigh(EDGE - 2, gtop, second_r, third_r)
    table()
    lax.fori_loop(0, LAST, back_mid, 0)
    top_delta(EDGE - 1)
    weigh(EDGE - 1, gtop, second_r, third_r)
    returned()
    top_delta(EDGE)
    weigh(EDGE, gtop, second_r, third_r)
    hand(0)
    layer_back(LAST, top_w, third_r, second_r, gmid, first_r)
    weigh(EDGE - 1, gmid, first_r, second_r)
    weigh(EDGE, gmid, first_r, second_r)
    hand(1)

    @pl.when(core == 0)
    def _():
        ar_1(0)

    def back_first(k, carry):
        layer_back(k, mid_w, second_r, first_r, gin, x_r, k > 0)

        @pl.when((k == 1) & (core == 1))
        def _():
            ar_1(1)

        @pl.when((k == 4) & (core == 0))
        def _():
            ar_2()

        return carry

    lax.fori_loop(0, LAST + 1, back_first, 0)
    weigh(EDGE - 1, gin, x_r, first_r)
    weigh(EDGE, gin, x_r, first_r)

    small_0()

    @pl.when(core == 0)
    def _():
        small_1()
        ar_3()
        small_2()
        ar_4(out_top)
        small_3()
        out_in[...] = sf[0:NF]
        out_vec[...] = sf[NF:NF + 4]
        ar_5(out_mid)

    @pl.when(core == 1)
    def _():
        ar_2()
        ar_3()
        ar_4(out_mid)
        ar_5(out_top)
        got(st, s3_s, s3_r, partner())
        out_in[...] = st[0:NF]
        out_vec[...] = st[NF:NF + 4]

    for k in range(2):
        for q in plane_peers:
            gone(plane.at[k, p], pl_s.at[k, q], pl_r.at[k, p], at_plane(q))
        for w in z_peers:
            gone(zout.at[k, w], zz_s.at[k, w], zz_r.at[k, z], at_z(w))
    for w in z_peers:
        gone(meta.at[z], me_s.at[w], me_r.at[z], at_z(w))
        gone(cz.at[z], cz_s.at[w], cz_r.at[z], at_z(w))
    for q in plane_peers:
        gone(tbl.at[q], rt_s.at[q], rt_r.at[p], at_plane(q))
    gone(cg, c_s, c_r, partner())
    gone(ra.at[pl.ds(0, AN - 1)], a1_s, a1_r, at_a(a))
    gone(rb.at[pl.ds(0, BN - 1)], a2_s, a2_r, at_b(zz))
    gone(full.at[pl.ds(0, AN - 1)], a3_s, a3_r, at_a(a))
    gone(full, f_s, f_r, partner())

    @pl.when(core == 0)
    def _():
        gone(sa.at[pl.ds(0, AN - 1)], s1_s, s1_r, at_a(a))
        gone(sb.at[pl.ds(0, BN - 1)], s2_s, s2_r, at_b(zz))
        gone(sf, s3_s, s3_r, partner())

    @pl.when(core == 1)
    def _():
        gone(sg, s0_s, s0_r, partner())


def copy_kernel(*refs):
    ins, outs, sem = refs[:5], refs[5:10], refs[10]
    copies = [pltpu.make_async_copy(ins[i], outs[i], sem.at[i]) for i in range(5)]
    for copy in copies:
        copy.start()
    for copy in copies:
        copy.wait()


def per_device(
    initial_state, target, features, coupling, in_weight, mid_weight, top_weight, out_weight, biases,
    block_count, connectivity, orientation, rotation,
):
    cells = lax.axis_size("op") * lax.axis_size("blk") * NS * BI * BJ
    loss_scale = 2.0 / math.sqrt(cells)
    vmem = pl.BlockSpec(memory_space=pltpu.VMEM)
    smem = pl.BlockSpec(memory_space=pltpu.SMEM)
    dma = pltpu.SemaphoreType.DMA
    field = pltpu.VMEM((NV, NS, BI, BJ), f32)
    outs = pl.pallas_call(
        functools.partial(kernel, loss_scale),
        out_shape=(
            jax.ShapeDtypeStruct((NV, NS, BI, BJ), f32),
            jax.ShapeDtypeStruct((NF, HID), f32),
            jax.ShapeDtypeStruct((HID, HID), f32),
            jax.ShapeDtypeStruct((HID, HID), f32),
            jax.ShapeDtypeStruct((4, HID), f32),
        ),
        in_specs=[vmem, vmem, vmem, smem, vmem, vmem, vmem, vmem, vmem, smem, smem, smem, smem],
        out_specs=(vmem,) * 5,
        scratch_shapes=[
            pltpu.VMEM((NCH, NF, CW), bf16),
            pltpu.VMEM((NCH, HID, CW), bf16),
            pltpu.VMEM((NCH, HID, CW), bf16),
            pltpu.VMEM((NCH, HID, CW), bf16),
            pltpu.VMEM((NS, 2, NF * 16, BJ), f32),
            pltpu.VMEM((HID, NF), bf16),
            pltpu.VMEM((HID, HID), bf16),
            pltpu.VMEM((HID, HID), bf16),
            pltpu.VMEM((3, HID, BJ), f32),
            pltpu.VMEM((HID, BJ), f32),
            field, field, field, field,
            pltpu.VMEM((NS * BI, BJ), f32),
            pltpu.VMEM((NS * BI, BJ), f32),
            pltpu.VMEM((NS * BI, BJ), f32),
            pltpu.VMEM((NS * BI, BJ), f32),
            pltpu.VMEM((2, PL, 8, ROW), f32),
            pltpu.VMEM((2, ZN, 8, ROW), f32),
            pltpu.VMEM((2, ZN, 8, ROW), f32),
            pltpu.VMEM((8, ROW), f32),
            pltpu.VMEM((4, 8, BJ), f32),
            pltpu.VMEM((ZN, 8, BJ), f32),
            pltpu.VMEM((ZN * 8, BJ), f32),
            pltpu.VMEM((BJ, BJ), f32),
            pltpu.VMEM((2, 8, ROW), f32),
            pltpu.VMEM((ZN, 8, ROW), f32),
            pltpu.VMEM((PL, 8, ROW), f32),
            pltpu.VMEM((PL, 8, ROW), f32),
            pltpu.VMEM((HID + 16, HID), f32),
            pltpu.VMEM((HID + 16, HID), f32),
            pltpu.VMEM((NF + 16, HID), f32),
            pltpu.VMEM((HID, BJ), f32),
            pltpu.VMEM((HID, HID), f32),
            pltpu.VMEM((AN, HID // AN, HID), f32),
            pltpu.VMEM((AN, HID // AN, HID), f32),
            pltpu.VMEM((BN, HID // AN, HID), f32),
            pltpu.VMEM((AN, HID // AN, HID), f32),
            pltpu.VMEM((AN, HID // AN, HID), f32),
            pltpu.VMEM((24, HID), f32),
            pltpu.VMEM((24, HID), f32),
            pltpu.VMEM((AN, 24, HID), f32),
            pltpu.VMEM((BN, 24, HID), f32),
            pltpu.VMEM((24, HID), f32),
            pltpu.VMEM((24, HID), f32),
            dma((2, PL)), dma((2, PL)), dma((ZN,)), dma((ZN,)), dma((2, ZN)), dma((2, ZN)),
            dma((ZN,)), dma((ZN,)), dma((PL,)), dma((PL,)),
            dma, dma, dma, dma, dma, dma, dma, dma, dma, dma, dma, dma, dma, dma, dma, dma, dma, dma,
        ],
        compiler_params=pltpu.CompilerParams(
            collective_id=0, has_side_effects=True, vmem_limit_bytes=56 * 2**20
        ),
    )(
        initial_state[0], target[0], features[0], coupling, in_weight, mid_weight, top_weight,
        out_weight, biases, block_count, connectivity.T, orientation.T, rotation.T,
    )
    outs = pl.pallas_call(
        copy_kernel,
        out_shape=tuple(jax.ShapeDtypeStruct(x.shape, x.dtype) for x in outs),
        in_specs=[vmem] * 5,
        out_specs=(pl.BlockSpec(memory_space=pl.ANY),) * 5,
        scratch_shapes=[dma((5,))],
    )(*outs)
    return (outs[0][None],) + tuple(outs[1:])


def solution(mesh):
    wide = P("op", None, "blk", None, None)
    return jax.shard_map(
        per_device,
        mesh=mesh,
        in_specs=(wide, wide, wide) + (P(),) * 6 + (P("blk"),) + (P("blk", None),) * 3,
        out_specs=(wide, P(), P(), P(), P()),
        check_vma=False,
    )
```

```python
import functools
import math

import jax
import jax.numpy as jnp
from jax import lax
from jax.experimental import pallas as pl
from jax.experimental.pallas import tpu as pltpu
from jax.sharding import PartitionSpec as P

MESH = pl.DeviceIdType.MESH
tau = 0.2
passage_angle = 2.0 * math.pi / 36.0
cos_step = math.cos(passage_angle)
sin_step = math.sin(passage_angle)
highest = lax.Precision.HIGHEST
f32 = jnp.float32
bf16 = jnp.bfloat16

NV, NS, BI, BJ, HID, NF = 6, 3, 32, 128, 256, 16
PL = 8
ZN = 4
NCH = 12
CW = 1024
EDGE = NCH - 1
AN = 16
BN = 8
ROW = NV * BJ


def row_of(s, i):
    if i == 0 or i == BI - 1:
        return 8 * EDGE + 2 * s + (i != 0)
    inner = (BI - 2) * s + i - 1
    return inner if inner < 8 * EDGE else inner + 2 * NS


def runs(s):
    whole = (BI - 2) * s
    first = min(BI - 2, 8 * EDGE - whole)
    res = [(1, whole, first)]
    if first < BI - 2:
        res.append((1 + first, row_of(s, 1 + first), BI - 2 - first))
    return res


def nt(a, b):
    return lax.dot_general(a, b, (((1,), (1,)), ((), ())), preferred_element_type=f32)


def mm(a, b):
    return jnp.dot(a, b, preferred_element_type=f32)


def lanes_sum(u, lane):
    left = jnp.where(lane == 0, u, pltpu.roll(u, 1, 1))
    right = jnp.where(lane == BJ - 1, u, pltpu.roll(u, BJ - 1, 1))
    return left + right


def kernel(
    loss_scale,
    state_h, target_h, feat_h, coup, in_w, mid_w, top_w, out_w, biases, count, conn, orient, rot,
    out_state, out_in, out_mid, out_top, out_vec,
    state, target, feat, x0, x1, first0, first1, second0, second1, third0, third1,
    xs, win_t, wmid_t, wtop_t, bias_c, ow_c,
    mid_r, ts_r, tm_r, fc_r, beta_r, betan_r, bc_r, bcn_r,
    plane, zout, zin, inner, tile_r, meta, sel_r, selt_r, ghost_r,
    cz, tbl, ret,
    gtop, gmid, gin, gout,
    cg, gsum, ra, rb, full, other, sg, sc, sa, sb, sf, st,
    pl_s, pl_r, me_s, me_r, zz_s, zz_r, cz_s, cz_r, rt_s, rt_r,
    in_s, c_s, c_r, a1_s, a1_r, a2_s, a2_r, a3_s, a3_r, f_s, f_r, s0_s, s0_r, s1_s, s1_r, s2_s, s2_r, s3_s, s3_r,
):
    x_r, first_r, second_r, third_r = (x0, x1), (first0, first1), (second0, second1), (third0, third1)
    b = lax.axis_index("blk")
    o = lax.axis_index("op")
    z = lax.div(b, PL)
    p = lax.rem(b, PL)

    plane_peers = [lax.rem(p + d, PL) for d in range(1, PL)]
    z_peers = [lax.rem(z + d, ZN) for d in range(1, ZN)]
    x_at = lax.div(o, 2)
    z_lo = lax.rem(o, 2)
    core = lax.rem(b, 2)
    a = x_at * ZN + lax.div(p, 2)
    zz = z * 2 + z_lo

    def at_plane(q):
        return {"blk": z * PL + q}

    def at_z(w):
        return {"blk": w * PL + p}

    def at_a(q):
        return {"blk": z * PL + lax.rem(q, 4) * 2 + core, "op": lax.div(q, 4) * 2 + z_lo}

    def partner():
        return {"blk": b + 1 - 2 * core}

    def at_b(w):
        return {"blk": lax.div(w, 2) * PL + p, "op": x_at * 2 + lax.rem(w, 2)}

    def send(src, dst, s_sem, r_sem, device):
        copy = pltpu.make_async_remote_copy(
            src_ref=src, dst_ref=dst, send_sem=s_sem, recv_sem=r_sem, device_id=device, device_id_type=MESH
        )
        copy.start()

    def got(dst, s_sem, r_sem, device):
        pltpu.make_async_remote_copy(
            src_ref=dst, dst_ref=dst, send_sem=s_sem, recv_sem=r_sem, device_id=device, device_id_type=MESH
        ).wait_recv()

    def gone(src, s_sem, r_sem, device):
        pltpu.make_async_remote_copy(
            src_ref=src, dst_ref=src, send_sem=s_sem, recv_sem=r_sem, device_id=device, device_id_type=MESH
        ).wait_send()

    barrier = pltpu.get_barrier_semaphore()
    def greet(device):
        pl.semaphore_signal(barrier, inc=1, device_id=device, device_id_type=MESH)

    for q in plane_peers:
        greet(at_plane(q))
    for d in range(4, AN):
        greet(at_a(lax.rem(x_at * 4 + d, AN)))
    for d in range(1, BN):
        greet(at_b(lax.rem(zz + d, BN)))

    loads = [pltpu.make_async_copy(h, v, in_s.at[i]) for i, (h, v) in enumerate(((state_h, state), (feat_h, feat), (target_h, target)))]
    for load in loads:
        load.start()

    rowi = lax.broadcasted_iota(jnp.int32, (8, BJ), 0)
    lane8 = lax.broadcasted_iota(jnp.int32, (8, BJ), 1)
    meta_t = jnp.full((8, BJ), -1.0, f32)
    flip_t = jnp.zeros((8, BJ), f32)
    cos_t = jnp.ones((8, BJ), f32)
    sin_t = jnp.zeros((8, BJ), f32)
    live_t = jnp.zeros((8, BJ), f32)
    live = []
    for s in range(NS):
        live.append(jnp.where(s < count[0], 1.0, 0.0).astype(f32))
        for e in range(2):
            here = rowi == 2 * s + e
            idx = conn[e, s]
            idx = idx + 2 * ((idx * 10923) >> 16)
            meta_t = jnp.where(here, idx.astype(f32), meta_t)
            flip_t = jnp.where(here, orient[e, s].astype(f32), flip_t)
            turn = rot[e, s]
            cos_t = jnp.where(here, jnp.where(turn == 0, 1.0, cos_step).astype(f32), cos_t)
            sin_t = jnp.where(here, turn.astype(f32) * sin_step, sin_t)
            live_t = jnp.where(here, live[s], live_t)
    meta[z] = meta_t
    tile_r[0] = flip_t
    tile_r[1] = cos_t
    tile_r[2] = sin_t
    tile_r[3] = live_t

    def pack(dst, field, rows):
        dst[...] = jnp.zeros((8, ROW), f32)
        for v in range(NV):
            for s in range(NS):
                for e in range(2):
                    dst[2 * s + e:2 * s + e + 1, v * BJ:(v + 1) * BJ] = field[v, s, rows[e]:rows[e] + 1, :]

    def cut(ref):
        return [ref[:, v * BJ:(v + 1) * BJ] for v in range(NV)]

    loads[0].wait()
    mine = plane.at[0, p]
    pack(mine, state, (0, BI - 1))

    pl.semaphore_wait(barrier, PL - 1 + AN - 4 + BN - 1)

    def send_plane(k):
        for q in plane_peers:
            send(plane.at[k, p], plane.at[k, p], pl_s.at[k, q], pl_r.at[k, p], at_plane(q))

    for w in z_peers:
        send(meta.at[z], meta.at[z], me_s.at[w], me_r.at[z], at_z(w))
    send_plane(0)

    def pick(k):
        for q in plane_peers:
            got(plane.at[k, q], pl_s.at[k, q], pl_r.at[k, q], at_plane(q))
        every = plane[k].reshape(PL * 8, ROW)
        chosen = jnp.dot(sel_r[:, :PL * 8], every, preferred_element_type=f32, precision=highest)
        for w in range(ZN):
            zout[k, w] = chosen[8 * w:8 * w + 8]
        zin[k, z] = zout[k, z]
        for w in z_peers:
            send(zout.at[k, w], zin.at[k, z], zz_s.at[k, w], zz_r.at[k, z], at_z(w))

    def make_sel():
        for w in z_peers:
            got(meta.at[w], me_s.at[w], me_r.at[w], at_z(w))
        lane = lax.broadcasted_iota(jnp.int32, (ZN * 8, BJ), 1)
        named = meta[...].reshape(ZN * 8, BJ)
        local = named - (z * (PL * 8)).astype(f32)
        sel = jnp.where((local == lane.astype(f32)) & (lane < PL * 8), 1.0, 0.0).astype(f32)
        sel_r[...] = sel
        selt_r[...] = jnp.concatenate([sel, jnp.zeros((BJ - ZN * 8, BJ), f32)], axis=0).T

    def turned(parts, sign):
        flip, cos, sin = tile_r[0], tile_r[1], tile_r[2] * sign
        whole = jnp.concatenate(parts, axis=0)
        r = lax.broadcasted_iota(jnp.int32, (BJ, BJ), 0)
        c = lax.broadcasted_iota(jnp.int32, (BJ, BJ), 1)
        anti = jnp.where(r + c == BJ - 1, 1.0, 0.0).astype(f32)
        back = jnp.dot(whole, anti, preferred_element_type=f32, precision=highest)
        out = [jnp.where(flip > 0.5, back[8 * v:8 * v + 8], parts[v]) for v in range(NV)]
        c2 = cos * out[2] - sin * out[3]
        c3 = sin * out[2] + cos * out[3]
        return [out[0], out[1], c2, c3, out[4], out[5]]

    def ghosts(k):
        for w in z_peers:
            got(zin.at[k, w], zz_s.at[k, w], zz_r.at[k, w], at_z(w))
        total = (zin[k, 0] + zin[k, 1]) + (zin[k, 2] + zin[k, 3])
        parts = turned([total[:, v * BJ:(v + 1) * BJ] for v in range(NV)], 1.0)
        for v in range(NV):
            ghost_r[k, :, v * BJ:(v + 1) * BJ] = parts[v]

    def edge_sweep(e, n, gh):
        res = []
        beta_e = jnp.where(rowi < 2 * NS, beta_r[8 * EDGE:8 * EDGE + 8, :], 0.0)
        for v in range(NV):
            lap = gh[v] + n[v] + lanes_sum(e[v], lane8) - 4.0 * e[v]
            coupled = coup[v, 0] * e[0]
            for w in range(1, NV):
                coupled = coupled + coup[v, w] * e[w]
            res.append(e[v] + tau * (lap - coupled + beta_e * jnp.tanh(e[v])))
        return res

    pad = jnp.zeros((BJ - NF, HID), f32)
    win_t[...] = jnp.concatenate([in_w[...].astype(f32), pad], axis=0).T[:, :NF].astype(bf16)
    wmid_t[...] = mid_w[...].astype(f32).T.astype(bf16)
    wtop_t[...] = top_w[...].astype(f32).T.astype(bf16)
    for k in range(3):
        bias_c[k] = jnp.broadcast_to(biases[k:k + 1, :], (BJ, HID)).T
    ow_c[...] = jnp.broadcast_to(out_w[...].astype(f32).reshape(1, HID), (BJ, HID)).T

    loads[1].wait()
    for s in range(NS):
        for h in range(2):
            xs[s, h] = feat[:, s, 16 * h:16 * h + 16, :].astype(f32).reshape(NF * 16, BJ)
    for s in range(NS):
        for h in range(2):
            for r in range(16):
                row = row_of(s, 16 * h + r)
                x_r[row // 8 % 2][row // 16, :, (row % 8) * BJ:(row % 8 + 1) * BJ] = xs[s, h, pl.ds(r, NF, stride=16), :].astype(bf16)

    SUB = 256

    weights = (win_t, wmid_t, wtop_t)
    acts = (x_r, first_r, second_r, third_r)
    SUBS = 2 * CW // SUB

    def forward(k, carry):
        pair = (lax.rem(k + EDGE // 2, NCH // 2), k)

        def place(j):
            half = j // (CW // SUB)
            return 1 - half, pair[half], slice((j % (CW // SUB)) * SUB, (j % (CW // SUB) + 1) * SUB)

        def product(layer, j):
            par, c, cols = place(j)
            return mm(weights[layer][...], acts[layer][par][c, :, cols])

        tiles = [jnp.zeros((8, BJ), f32), jnp.zeros((8, BJ), f32)]

        def activate(layer, j, d):
            par, c, cols = place(j)
            bias = bias_c[layer]
            for i in range(SUB // BJ):
                t = jnp.tanh(d[:, i * BJ:(i + 1) * BJ] + bias).astype(bf16)
                acts[layer + 1][par][c, :, cols.start + i * BJ:cols.start + (i + 1) * BJ] = t
                if layer == 2:
                    bt = jnp.sum(ow_c[...] * t.astype(f32), axis=0, keepdims=True) + 1.0
                    row = (j % (CW // SUB)) * (SUB // BJ) + i
                    half = j // (CW // SUB)
                    tiles[half] = jnp.where(rowi == row, bt, tiles[half])

        tasks = [(layer, j) for layer in range(3) for j in range(SUBS)]
        held = None
        for task in tasks:
            d = product(*task)
            if held is not None:
                activate(*held)
            held = task + (d,)
        activate(*held)
        for half in range(2):
            beta_r[pl.ds(pl.multiple_of((2 * pair[half] + 1 - half) * 8, 8), 8), :] = tiles[half]

        @pl.when(k == 0)
        def _():
            make_sel()
            pick(0)

        @pl.when(k == 2)
        def _():
            ghosts(0)
            pack(inner, state, (1, BI - 2))
            res = edge_sweep(cut(plane.at[0, p]), cut(inner), cut(ghost_r.at[0]))
            for v in range(NV):
                plane[1, p, :, v * BJ:(v + 1) * BJ] = res[v]
            send_plane(1)

        @pl.when(k == 4)
        def _():
            pick(1)

        return carry

    lax.fori_loop(0, NCH // 2, forward, 0)

    for s in range(NS):
        for e in range(2):
            g = 8 * EDGE + 2 * s + e
            row = s * BI + e * (BI - 1)
            betan_r[row:row + 1, :] = beta_r[g:g + 1, :]
        for first, place, length in runs(s):
            betan_r[s * BI + first:s * BI + first + length, :] = beta_r[place:place + length, :]

    rows32 = lax.broadcasted_iota(jnp.int32, (BI, BJ), 0)
    lane32 = lax.broadcasted_iota(jnp.int32, (BI, BJ), 1)

    def stencil(u, low, high):
        up = jnp.where(rows32 == 0, low, pltpu.roll(u, 1, 0))
        down = jnp.where(rows32 == BI - 1, high, pltpu.roll(u, BI - 1, 0))
        return up + down + lanes_sum(u, lane32) - 4.0 * u

    def low_high(k, s, v):
        cols = slice(v * BJ, (v + 1) * BJ)
        return ghost_r[k, 2 * s:2 * s + 1, cols], ghost_r[k, 2 * s + 1:2 * s + 2, cols]

    for s in range(NS):
        us = [state[v, s] for v in range(NV)]
        beta = betan_r[s * BI:(s + 1) * BI, :]
        for v in range(NV):
            t = jnp.tanh(us[v])
            ts_r[v, s] = t
            low, high = low_high(0, s, v)
            coupled = coup[v, 0] * us[0]
            for w in range(1, NV):
                coupled = coupled + coup[v, w] * us[w]
            mid_r[v, s] = us[v] + tau * (stencil(us[v], low, high) - coupled + beta * t)

    ghosts(1)
    pack(inner, mid_r, (1, BI - 2))
    final_e = edge_sweep(cut(plane.at[1, p]), cut(inner), cut(ghost_r.at[1]))
    loads[2].wait()
    pack(inner, target, (0, BI - 1))
    goal_e = cut(inner)
    cot_e = [tau * (loss_scale * tile_r[3] * (final_e[v] - goal_e[v])) for v in range(NV)]
    cot_e = turned(cot_e, -1.0)
    for v in range(NV):
        cz[z, :, v * BJ:(v + 1) * BJ] = cot_e[v]
    for w in z_peers:
        send(cz.at[z], cz.at[z], cz_s.at[w], cz_r.at[z], at_z(w))

    for s in range(NS):
        us = [mid_r[v, s] for v in range(NV)]
        beta = betan_r[s * BI:(s + 1) * BI, :]
        for v in range(NV):
            t = jnp.tanh(us[v])
            tm_r[v, s] = t
            low, high = low_high(1, s, v)
            coupled = coup[v, 0] * us[0]
            for w in range(1, NV):
                coupled = coupled + coup[v, w] * us[w]
            final = us[v] + tau * (stencil(us[v], low, high) - coupled + beta * t)
            out_state[v, s] = live[s] * final
            fc_r[v, s] = loss_scale * live[s] * (final - target[v, s])

    for s in range(NS):
        gs = [fc_r[v, s] for v in range(NV)]
        beta = betan_r[s * BI:(s + 1) * BI, :]
        acc = jnp.zeros((BI, BJ), f32)
        for v in range(NV):
            t = tm_r[v, s]
            coupled = coup[0, v] * gs[0]
            for w in range(1, NV):
                coupled = coupled + coup[w, v] * gs[w]
            mc = gs[v] + tau * (stencil(gs[v], 0.0, 0.0) - coupled + beta * (1.0 - t * t) * gs[v])
            acc = acc + (gs[v] * t + mc * ts_r[v, s])
        bcn_r[s * BI:(s + 1) * BI, :] = tau * acc
        for first, place, length in runs(s):
            bc_r[place:place + length, :] = bcn_r[s * BI + first:s * BI + first + length, :]

    def table():
        for w in z_peers:
            got(cz.at[w], cz_s.at[w], cz_r.at[w], at_z(w))
        cots = cz[...].reshape(ZN * 8, ROW)
        sums = jnp.dot(selt_r[:PL * 8, :ZN * 8], cots, preferred_element_type=f32, precision=highest)
        for q in range(PL):
            tbl[q] = sums[8 * q:8 * q + 8]
        ret[p] = tbl[p]
        for q in plane_peers:
            send(tbl.at[q], ret.at[p], rt_s.at[q], rt_r.at[p], at_plane(q))

    def returned():
        for q in plane_peers:
            got(ret.at[q], rt_s.at[q], rt_r.at[q], at_plane(q))
        total = ret[0]
        for q in range(1, PL):
            total = total + ret[q]
        start = plane[0, p]
        extra = jnp.zeros((8, BJ), f32)
        for v in range(NV):
            cols = slice(v * BJ, (v + 1) * BJ)
            extra = extra + total[:, cols] * jnp.tanh(start[:, cols])
        for s in range(NS):
            for e in range(2):
                g = 2 * s + e
                row = s * BI + e * (BI - 1)
                bc_r[8 * EDGE + g:8 * EDGE + g + 1, :] = bcn_r[row:row + 1, :] + tau * extra[g:g + 1]

    ones = jnp.ones((16, CW), bf16)
    gout[...] = jnp.zeros((HID, BJ), f32)
    gtop[...] = jnp.zeros((HID + 16, HID), f32)
    gmid[...] = jnp.zeros((HID + 16, HID), f32)
    gin[...] = jnp.zeros((NF + 16, HID), f32)

    def weigh(par, k, acc, left, right, fresh=None):
        part = nt(jnp.concatenate([left[par][k], ones], axis=0), right[par][k])
        if fresh is not None:
            part = jnp.where(fresh, part, 0.0)
        acc[...] = acc[...] + part

    def before(k):
        return lax.rem(k + NCH // 2 - 1, NCH // 2)

    RB = 64

    def top_delta(par, k):
        third = third_r[par]
        bc = bc_r[pl.ds(pl.multiple_of((2 * k + par) * 8, 8), 8), :]
        ch = bc.astype(bf16).astype(f32)
        for i in range(HID // RB):
            rows = slice(i * RB, (i + 1) * RB)
            ow = ow_c[rows]
            acc = gout[rows]
            for j in range(CW // BJ):
                cols = slice(j * BJ, (j + 1) * BJ)
                t = third[k, rows, cols].astype(f32)
                acc = acc + t * ch[j:j + 1]
                third[k, rows, cols] = (ow * bc[j:j + 1] * (1.0 - t * t)).astype(bf16)
            gout[rows] = acc

    def back_top(k, carry):
        weigh(1, before(k), gtop, second_r, third_r, k > 0)
        top_delta(0, k)
        weigh(0, k, gtop, second_r, third_r)
        top_delta(1, k)
        return carry

    def layer_back(k, weight, source, act, acc, left, fresh=None):
        held = None

        def put(par, cols, d):
            for i in range(SUB // BJ):
                here = slice(cols.start + i * BJ, cols.start + (i + 1) * BJ)
                t = act[par][k, :, here].astype(f32)
                act[par][k, :, here] = (d[:, i * BJ:(i + 1) * BJ] * (1.0 - t * t)).astype(bf16)

        for par in range(2):
            for j in range(CW // SUB):
                cols = slice(j * SUB, (j + 1) * SUB)
                d = mm(weight[...], source[par][k, :, cols])
                if held is not None:
                    put(*held)
                held = (par, cols, d)
                if j == 0:
                    if par == 0:
                        weigh(1, before(k), acc, left, act, fresh)
                    else:
                        put(*held)
                        held = None
                        weigh(0, k, acc, left, act)
        put(*held)

    def back_mid(k, carry):
        layer_back(k, top_w, third_r, second_r, gmid, first_r, k > 0)
        return carry

    grads = (gtop, gmid)
    R = HID // AN

    def hand(i):
        @pl.when(core != i)
        def _():
            send(grads[i].at[pl.ds(0, HID)], cg, c_s, c_r, partner())

    def ar_1(i):
        got(cg, c_s, c_r, partner())
        gsum[...] = (grads[i][0:HID] + cg[...]).reshape(AN, R, HID)
        for d in range(1, AN):
            q = lax.rem(a + d, AN)
            send(gsum.at[q], ra.at[a], a1_s, a1_r, at_a(q))
        ra[a] = gsum[a]

    def ar_2():
        got(ra.at[pl.ds(0, AN - 1)], a1_s, a1_r, at_a(a))
        total = ra[0]
        for q in range(1, AN):
            total = total + ra[q]
        rb[zz] = total
        for d in range(1, BN):
            send(rb.at[zz], rb.at[zz], a2_s, a2_r, at_b(lax.rem(zz + d, BN)))

    def ar_3():
        got(rb.at[pl.ds(0, BN - 1)], a2_s, a2_r, at_b(zz))
        total = rb[0]
        for w in range(1, BN):
            total = total + rb[w]
        full[a] = total
        for d in range(1, AN):
            send(full.at[a], full.at[a], a3_s, a3_r, at_a(lax.rem(a + d, AN)))

    def ar_4(out):
        got(full.at[pl.ds(0, AN - 1)], a3_s, a3_r, at_a(a))
        send(full, other, f_s, f_r, partner())
        out[...] = full[...].reshape(HID, HID)

    def ar_5(out):
        got(other, f_s, f_r, partner())
        out[...] = other[...].reshape(HID, HID)

    def small_0():
        sg[0:NF] = gin[0:NF]
        sg[NF:NF + 1] = jnp.sum(gout[...].T, axis=0, keepdims=True)
        sg[NF + 1:NF + 2] = gin[NF:NF + 1]
        sg[NF + 2:NF + 3] = gmid[HID:HID + 1]
        sg[NF + 3:NF + 4] = gtop[HID:HID + 1]
        sg[NF + 4:NF + 8] = jnp.zeros((4, HID), f32)

        @pl.when(core == 1)
        def _():
            send(sg, sc, s0_s, s0_r, partner())

    def small_1():
        got(sc, s0_s, s0_r, partner())
        sa[a] = sg[...] + sc[...]
        for d in range(1, AN):
            send(sa.at[a], sa.at[a], s1_s, s1_r, at_a(lax.rem(a + d, AN)))

    def small_2():
        got(sa.at[pl.ds(0, AN - 1)], s1_s, s1_r, at_a(a))
        total = sa[0]
        for q in range(1, AN):
            total = total + sa[q]
        sb[zz] = total
        for d in range(1, BN):
            send(sb.at[zz], sb.at[zz], s2_s, s2_r, at_b(lax.rem(zz + d, BN)))

    def small_3():
        got(sb.at[pl.ds(0, BN - 1)], s2_s, s2_r, at_b(zz))
        total = sb[0]
        for w in range(1, BN):
            total = total + sb[w]
        sf[...] = total
        send(sf, st, s3_s, s3_r, partner())

    LAST = NCH // 2 - 1
    lax.fori_loop(0, LAST, back_top, 0)
    weigh(1, LAST - 1, gtop, second_r, third_r)
    table()
    top_delta(0, LAST)
    weigh(0, LAST, gtop, second_r, third_r)
    lax.fori_loop(0, LAST, back_mid, 0)
    returned()
    top_delta(1, LAST)
    weigh(1, LAST, gtop, second_r, third_r)
    hand(0)
    layer_back(LAST, top_w, third_r, second_r, gmid, first_r)
    weigh(1, LAST, gmid, first_r, second_r)
    hand(1)

    @pl.when(core == 0)
    def _():
        ar_1(0)

    def back_first(k, carry):
        layer_back(k, mid_w, second_r, first_r, gin, x_r, k > 0)

        @pl.when((k == 1) & (core == 1))
        def _():
            ar_1(1)

        @pl.when((k == 4) & (core == 0))
        def _():
            ar_2()

        return carry

    lax.fori_loop(0, LAST + 1, back_first, 0)
    weigh(1, LAST, gin, x_r, first_r)

    small_0()

    @pl.when(core == 0)
    def _():
        small_1()
        ar_3()
        small_2()
        ar_4(out_top)
        small_3()
        out_in[...] = sf[0:NF]
        out_vec[...] = sf[NF:NF + 4]
        ar_5(out_mid)

    @pl.when(core == 1)
    def _():
        ar_2()
        ar_3()
        ar_4(out_mid)
        ar_5(out_top)
        got(st, s3_s, s3_r, partner())
        out_in[...] = st[0:NF]
        out_vec[...] = st[NF:NF + 4]

    for k in range(2):
        for q in plane_peers:
            gone(plane.at[k, p], pl_s.at[k, q], pl_r.at[k, p], at_plane(q))
        for w in z_peers:
            gone(zout.at[k, w], zz_s.at[k, w], zz_r.at[k, z], at_z(w))
    for w in z_peers:
        gone(meta.at[z], me_s.at[w], me_r.at[z], at_z(w))
        gone(cz.at[z], cz_s.at[w], cz_r.at[z], at_z(w))
    for q in plane_peers:
        gone(tbl.at[q], rt_s.at[q], rt_r.at[p], at_plane(q))
    gone(cg, c_s, c_r, partner())
    gone(ra.at[pl.ds(0, AN - 1)], a1_s, a1_r, at_a(a))
    gone(rb.at[pl.ds(0, BN - 1)], a2_s, a2_r, at_b(zz))
    gone(full.at[pl.ds(0, AN - 1)], a3_s, a3_r, at_a(a))
    gone(full, f_s, f_r, partner())

    @pl.when(core == 0)
    def _():
        gone(sa.at[pl.ds(0, AN - 1)], s1_s, s1_r, at_a(a))
        gone(sb.at[pl.ds(0, BN - 1)], s2_s, s2_r, at_b(zz))
        gone(sf, s3_s, s3_r, partner())

    @pl.when(core == 1)
    def _():
        gone(sg, s0_s, s0_r, partner())


def copy_kernel(*refs):
    ins, outs, sem = refs[:5], refs[5:10], refs[10]
    copies = [pltpu.make_async_copy(ins[i], outs[i], sem.at[i]) for i in range(5)]
    for copy in copies:
        copy.start()
    for copy in copies:
        copy.wait()


def per_device(
    initial_state, target, features, coupling, in_weight, mid_weight, top_weight, out_weight, biases,
    block_count, connectivity, orientation, rotation,
):
    cells = lax.axis_size("op") * lax.axis_size("blk") * NS * BI * BJ
    loss_scale = 2.0 / math.sqrt(cells)
    vmem = pl.BlockSpec(memory_space=pltpu.VMEM)
    smem = pl.BlockSpec(memory_space=pltpu.SMEM)
    anywhere = pl.BlockSpec(memory_space=pl.ANY)
    dma = pltpu.SemaphoreType.DMA
    field = pltpu.VMEM((NV, NS, BI, BJ), f32)
    outs = pl.pallas_call(
        functools.partial(kernel, loss_scale),
        out_shape=(
            jax.ShapeDtypeStruct((NV, NS, BI, BJ), f32),
            jax.ShapeDtypeStruct((NF, HID), f32),
            jax.ShapeDtypeStruct((HID, HID), f32),
            jax.ShapeDtypeStruct((HID, HID), f32),
            jax.ShapeDtypeStruct((4, HID), f32),
        ),
        in_specs=[anywhere, anywhere, anywhere, smem, vmem, vmem, vmem, vmem, vmem, smem, smem, smem, smem],
        out_specs=(vmem,) * 5,
        scratch_shapes=[
            field, field, pltpu.VMEM((NF, NS, BI, BJ), bf16),
            pltpu.VMEM((NCH // 2, NF, CW), bf16),
            pltpu.VMEM((NCH // 2, NF, CW), bf16),
            pltpu.VMEM((NCH // 2, HID, CW), bf16),
            pltpu.VMEM((NCH // 2, HID, CW), bf16),
            pltpu.VMEM((NCH // 2, HID, CW), bf16),
            pltpu.VMEM((NCH // 2, HID, CW), bf16),
            pltpu.VMEM((NCH // 2, HID, CW), bf16),
            pltpu.VMEM((NCH // 2, HID, CW), bf16),
            pltpu.VMEM((NS, 2, NF * 16, BJ), f32),
            pltpu.VMEM((HID, NF), bf16),
            pltpu.VMEM((HID, HID), bf16),
            pltpu.VMEM((HID, HID), bf16),
            pltpu.VMEM((3, HID, BJ), f32),
            pltpu.VMEM((HID, BJ), f32),
            field, field, field, field,
            pltpu.VMEM((NS * BI, BJ), f32),
            pltpu.VMEM((NS * BI, BJ), f32),
            pltpu.VMEM((NS * BI, BJ), f32),
            pltpu.VMEM((NS * BI, BJ), f32),
            pltpu.VMEM((2, PL, 8, ROW), f32),
            pltpu.VMEM((2, ZN, 8, ROW), f32),
            pltpu.VMEM((2, ZN, 8, ROW), f32),
            pltpu.VMEM((8, ROW), f32),
            pltpu.VMEM((4, 8, BJ), f32),
            pltpu.VMEM((ZN, 8, BJ), f32),
            pltpu.VMEM((ZN * 8, BJ), f32),
            pltpu.VMEM((BJ, BJ), f32),
            pltpu.VMEM((2, 8, ROW), f32),
            pltpu.VMEM((ZN, 8, ROW), f32),
            pltpu.VMEM((PL, 8, ROW), f32),
            pltpu.VMEM((PL, 8, ROW), f32),
            pltpu.VMEM((HID + 16, HID), f32),
            pltpu.VMEM((HID + 16, HID), f32),
            pltpu.VMEM((NF + 16, HID), f32),
            pltpu.VMEM((HID, BJ), f32),
            pltpu.VMEM((HID, HID), f32),
            pltpu.VMEM((AN, HID // AN, HID), f32),
            pltpu.VMEM((AN, HID // AN, HID), f32),
            pltpu.VMEM((BN, HID // AN, HID), f32),
            pltpu.VMEM((AN, HID // AN, HID), f32),
            pltpu.VMEM((AN, HID // AN, HID), f32),
            pltpu.VMEM((24, HID), f32),
            pltpu.VMEM((24, HID), f32),
            pltpu.VMEM((AN, 24, HID), f32),
            pltpu.VMEM((BN, 24, HID), f32),
            pltpu.VMEM((24, HID), f32),
            pltpu.VMEM((24, HID), f32),
            dma((2, PL)), dma((2, PL)), dma((ZN,)), dma((ZN,)), dma((2, ZN)), dma((2, ZN)),
            dma((ZN,)), dma((ZN,)), dma((PL,)), dma((PL,)),
            dma((3,)), dma, dma, dma, dma, dma, dma, dma, dma, dma, dma, dma, dma, dma, dma, dma, dma, dma, dma,
        ],
        compiler_params=pltpu.CompilerParams(
            collective_id=0, has_side_effects=True, vmem_limit_bytes=56 * 2**20
        ),
    )(
        initial_state[0], target[0], features[0], coupling, in_weight, mid_weight, top_weight,
        out_weight, biases, block_count, connectivity.T, orientation.T, rotation.T,
    )
    outs = pl.pallas_call(
        copy_kernel,
        out_shape=tuple(jax.ShapeDtypeStruct(x.shape, x.dtype) for x in outs),
        in_specs=[vmem] * 5,
        out_specs=(pl.BlockSpec(memory_space=pl.ANY),) * 5,
        scratch_shapes=[dma((5,))],
    )(*outs)
    return (outs[0][None],) + tuple(outs[1:])


def solution(mesh):
    wide = P("op", None, "blk", None, None)
    return jax.shard_map(
        per_device,
        mesh=mesh,
        in_specs=(wide, wide, wide) + (P(),) * 6 + (P("blk"),) + (P("blk", None),) * 3,
        out_specs=(wide, P(), P(), P(), P()),
        check_vma=False,
    )
```

```python
import functools
import math

import jax
import jax.numpy as jnp
from jax import lax
from jax.experimental import pallas as pl
from jax.experimental.pallas import tpu as pltpu
from jax.sharding import PartitionSpec as P

MESH = pl.DeviceIdType.MESH
tau = 0.2
passage_angle = 2.0 * math.pi / 36.0
cos_step = math.cos(passage_angle)
sin_step = math.sin(passage_angle)
f32 = jnp.float32
bf16 = jnp.bfloat16

NV, NS, BI, BJ, HID, NF = 6, 3, 32, 128, 256, 16
PL = 8
ZN = 4
NCH = 12
CW = 1024
EDGE = NCH - 1
AN = 16
BN = 8
HV = NV // 2
HALF = HV * BJ


def row_of(s, i):
    if i == 0 or i == BI - 1:
        return 8 * EDGE + 2 * s + (i != 0)
    inner = (BI - 2) * s + i - 1
    return inner if inner < 8 * EDGE else inner + 2 * NS


def runs(s):
    whole = (BI - 2) * s
    first = min(BI - 2, 8 * EDGE - whole)
    res = [(1, whole, first)]
    if first < BI - 2:
        res.append((1 + first, row_of(s, 1 + first), BI - 2 - first))
    return res


def nt(a, b):
    return lax.dot_general(a, b, (((1,), (1,)), ((), ())), preferred_element_type=f32)


def mm(a, b):
    return jnp.dot(a, b, preferred_element_type=f32)


def lanes_sum(u, lane):
    left = jnp.where(lane == 0, u, pltpu.roll(u, 1, 1))
    right = jnp.where(lane == BJ - 1, u, pltpu.roll(u, BJ - 1, 1))
    return left + right


def kernel(
    loss_scale,
    state_h, target_h, feat_h, coup, in_w, mid_w, top_w, out_w, biases, count, conn, orient, rot,
    out_state, out_in, out_mid, out_top, out_vec,
    state, target, feat, x0, x1, first0, first1, second0, second1, third0, third1,
    xs, win_t, wmid_t, wtop_t, bias_c, ow_c,
    mid_r, ts_r, tm_r, fc_r, beta_r, betan_r, bc_r, bcn_r,
    edge, gath, picked, arr, inner, tile_r, meta, sel_r, selt_r, ghost_r,
    cote, cz, tbl, ret,
    gtop, gmid, gin, gout,
    cg, gsum, ra, rb, full, other, sg, sc, sa, sb, sf, st,
    pl_s, pl_r, me_s, me_r, zz_s, zz_r, cz_s, cz_r, rt_s, rt_r,
    in_s, c_s, c_r, a1_s, a1_r, a2_s, a2_r, a3_s, a3_r, f_s, f_r, s0_s, s0_r, s1_s, s1_r, s2_s, s2_r, s3_s, s3_r,
):
    x_r, first_r, second_r, third_r = (x0, x1), (first0, first1), (second0, second1), (third0, third1)
    b = lax.axis_index("blk")
    o = lax.axis_index("op")
    z = lax.div(b, PL)
    p = lax.rem(b, PL)

    plane_peers = [lax.rem(p + d, PL) for d in range(1, PL)]
    x_at = lax.div(o, 2)
    z_lo = lax.rem(o, 2)
    core = lax.rem(b, 2)
    mine = z * 2 + core
    tower = [lax.rem(mine + d, 2 * ZN) for d in range(1, 2 * ZN)]
    a = x_at * ZN + lax.div(p, 2)
    zz = z * 2 + z_lo

    def at_plane(q):
        return {"blk": z * PL + q}

    def at_tower(w):
        return {"blk": lax.div(w, 2) * PL + p - core + lax.rem(w, 2)}

    def at_a(q):
        return {"blk": z * PL + lax.rem(q, 4) * 2 + core, "op": lax.div(q, 4) * 2 + z_lo}

    def partner():
        return {"blk": b + 1 - 2 * core}

    def at_b(w):
        return {"blk": lax.div(w, 2) * PL + p, "op": x_at * 2 + lax.rem(w, 2)}

    def send(src, dst, s_sem, r_sem, device):
        copy = pltpu.make_async_remote_copy(
            src_ref=src, dst_ref=dst, send_sem=s_sem, recv_sem=r_sem, device_id=device, device_id_type=MESH
        )
        copy.start()

    def got(dst, s_sem, r_sem, device):
        pltpu.make_async_remote_copy(
            src_ref=dst, dst_ref=dst, send_sem=s_sem, recv_sem=r_sem, device_id=device, device_id_type=MESH
        ).wait_recv()

    def gone(src, s_sem, r_sem, device):
        pltpu.make_async_remote_copy(
            src_ref=src, dst_ref=src, send_sem=s_sem, recv_sem=r_sem, device_id=device, device_id_type=MESH
        ).wait_send()

    barrier = pltpu.get_barrier_semaphore()
    def greet(device):
        pl.semaphore_signal(barrier, inc=1, device_id=device, device_id_type=MESH)

    for q in plane_peers:
        greet(at_plane(q))
    for d in range(4, AN):
        greet(at_a(lax.rem(x_at * 4 + d, AN)))
    for d in range(1, BN):
        greet(at_b(lax.rem(zz + d, BN)))
    for d in range(1, ZN):
        greet(at_tower(lax.rem(mine + 2 * d, 2 * ZN) + 1 - 2 * core))

    loads = [pltpu.make_async_copy(h, v, in_s.at[i]) for i, (h, v) in enumerate(((state_h, state), (feat_h, feat), (target_h, target)))]
    for load in loads:
        load.start()

    rowi = lax.broadcasted_iota(jnp.int32, (8, BJ), 0)
    lane8 = lax.broadcasted_iota(jnp.int32, (8, BJ), 1)
    meta_t = jnp.full((8, BJ), -1.0, f32)
    flip_t = jnp.zeros((8, BJ), f32)
    cos_t = jnp.ones((8, BJ), f32)
    sin_t = jnp.zeros((8, BJ), f32)
    live_t = jnp.zeros((8, BJ), f32)
    live = []
    for s in range(NS):
        live.append(jnp.where(s < count[0], 1.0, 0.0).astype(f32))
        for e in range(2):
            here = rowi == 2 * s + e
            idx = conn[e, s]
            idx = idx + 2 * ((idx * 10923) >> 16)
            meta_t = jnp.where(here, idx.astype(f32), meta_t)
            flip_t = jnp.where(here, orient[e, s].astype(f32), flip_t)
            turn = rot[e, s]
            cos_t = jnp.where(here, jnp.where(turn == 0, 1.0, cos_step).astype(f32), cos_t)
            sin_t = jnp.where(here, turn.astype(f32) * sin_step, sin_t)
            live_t = jnp.where(here, live[s], live_t)
    meta[mine] = meta_t
    tile_r[0] = flip_t
    tile_r[1] = cos_t
    tile_r[2] = sin_t
    tile_r[3] = live_t

    def part(ref, v):
        return ref.at[v // HV, :, v % HV * BJ:(v % HV + 1) * BJ]

    def pack(dst, field, rows):
        dst[...] = jnp.zeros((2, 8, HALF), f32)
        for v in range(NV):
            for s in range(NS):
                for e in range(2):
                    part(dst, v)[2 * s + e:2 * s + e + 1, :] = field[v, s, rows[e]:rows[e] + 1, :]

    def cut(ref):
        return [part(ref, v)[...] for v in range(NV)]

    def thirds(u):
        u1 = u.astype(bf16)
        u2 = (u - u1.astype(f32)).astype(bf16)
        u3 = (u - u1.astype(f32) - u2.astype(f32)).astype(bf16)
        return u1, u2, u3

    def by_rows(mask, u):
        r = mm(mask, jnp.concatenate(thirds(u), axis=1))
        return r[:, :HALF] + r[:, HALF:2 * HALF] + r[:, 2 * HALF:]

    loads[0].wait()
    pack(edge.at[0], state, (0, BI - 1))

    pl.semaphore_wait(barrier, PL - 1 + AN - 4 + BN - 1 + ZN - 1)

    def send_plane(k):
        for q in plane_peers:
            send(edge.at[k, lax.rem(q, 2)], gath.at[k, p], pl_s.at[k, q], pl_r.at[k, p], at_plane(q))
        gath[k, p] = edge[k, core]

    for w in tower:
        send(meta.at[mine], meta.at[mine], me_s.at[w], me_r.at[mine], at_tower(w))
    send_plane(0)

    def pick(k):
        for q in plane_peers:
            got(gath.at[k, q], pl_s.at[k, q], pl_r.at[k, q], at_plane(q))
        chosen = by_rows(sel_r[...], gath[k].reshape(PL * 8, HALF))
        picked[k] = chosen.reshape(2 * ZN, 8, HALF)
        arr[k, mine] = picked[k, mine]
        for w in tower:
            send(picked.at[k, w], arr.at[k, mine], zz_s.at[k, w], zz_r.at[k, mine], at_tower(w))

    def make_sel():
        for w in tower:
            got(meta.at[w], me_s.at[w], me_r.at[w], at_tower(w))
        n = 2 * ZN * 8
        lane = lax.broadcasted_iota(jnp.int32, (n, BJ), 1)
        named = meta[...].reshape(n, BJ)
        local = named - (z * (PL * 8)).astype(f32)
        sel = jnp.where((local == lane.astype(f32)) & (lane < PL * 8), 1.0, 0.0).astype(f32)
        sel_r[...] = sel[:, :PL * 8].astype(bf16)
        wide = jnp.concatenate([sel, jnp.zeros((BJ - n, BJ), f32)], axis=0).T
        selt_r[...] = wide[:PL * 8, :n].astype(bf16)

    def turned(parts, sign):
        flip, cos, sin = tile_r[0], tile_r[1], tile_r[2] * sign
        r = lax.broadcasted_iota(jnp.int32, (BJ, BJ), 0)
        c = lax.broadcasted_iota(jnp.int32, (BJ, BJ), 1)
        anti = jnp.where(r + c == BJ - 1, 1.0, 0.0).astype(bf16)
        n = 8 * NV
        back = mm(jnp.concatenate(thirds(jnp.concatenate(parts, axis=0)), axis=0), anti)
        back = back[:n] + back[n:2 * n] + back[2 * n:]
        out = [jnp.where(flip > 0.5, back[8 * v:8 * v + 8], parts[v]) for v in range(NV)]
        c2 = cos * out[2] - sin * out[3]
        c3 = sin * out[2] + cos * out[3]
        return [out[0], out[1], c2, c3, out[4], out[5]]

    def ghosts(k):
        for w in tower:
            got(arr.at[k, w], zz_s.at[k, w], zz_r.at[k, w], at_tower(w))
        total = [(arr[k, h] + arr[k, 2 + h]) + (arr[k, 4 + h] + arr[k, 6 + h]) for h in range(2)]
        parts = turned([total[v // HV][:, v % HV * BJ:(v % HV + 1) * BJ] for v in range(NV)], 1.0)
        for v in range(NV):
            ghost_r[k, v] = parts[v]

    def edge_sweep(e, n, gh):
        res = []
        beta_e = jnp.where(rowi < 2 * NS, beta_r[8 * EDGE:8 * EDGE + 8, :], 0.0)
        for v in range(NV):
            lap = gh[v] + n[v] + lanes_sum(e[v], lane8) - 4.0 * e[v]
            coupled = coup[v, 0] * e[0]
            for w in range(1, NV):
                coupled = coupled + coup[v, w] * e[w]
            res.append(e[v] + tau * (lap - coupled + beta_e * jnp.tanh(e[v])))
        return res

    pad = jnp.zeros((BJ - NF, HID), f32)
    win_t[...] = jnp.concatenate([in_w[...].astype(f32), pad], axis=0).T[:, :NF].astype(bf16)
    wmid_t[...] = mid_w[...].astype(f32).T.astype(bf16)
    wtop_t[...] = top_w[...].astype(f32).T.astype(bf16)
    for k in range(3):
        bias_c[k] = jnp.broadcast_to(biases[k:k + 1, :], (BJ, HID)).T
    ow_c[...] = jnp.broadcast_to(out_w[...].astype(f32).reshape(1, HID), (BJ, HID)).T

    loads[1].wait()
    for s in range(NS):
        for h in range(2):
            xs[s, h] = feat[:, s, 16 * h:16 * h + 16, :].astype(f32).reshape(NF * 16, BJ)
    for s in range(NS):
        for h in range(2):
            for r in range(16):
                row = row_of(s, 16 * h + r)
                x_r[row // 8 % 2][row // 16, :, (row % 8) * BJ:(row % 8 + 1) * BJ] = xs[s, h, pl.ds(r, NF, stride=16), :].astype(bf16)

    SUB = 256

    weights = (win_t, wmid_t, wtop_t)
    acts = (x_r, first_r, second_r, third_r)
    SUBS = 2 * CW // SUB

    def forward(k, carry):
        pair = (lax.rem(k + EDGE // 2, NCH // 2), k)

        def place(j):
            half = j // (CW // SUB)
            return 1 - half, pair[half], slice((j % (CW // SUB)) * SUB, (j % (CW // SUB) + 1) * SUB)

        def product(layer, j):
            par, c, cols = place(j)
            return mm(weights[layer][...], acts[layer][par][c, :, cols])

        tiles = [jnp.zeros((8, BJ), f32), jnp.zeros((8, BJ), f32)]

        def activate(layer, j, d):
            par, c, cols = place(j)
            bias = bias_c[layer]
            for i in range(SUB // BJ):
                t = jnp.tanh(d[:, i * BJ:(i + 1) * BJ] + bias).astype(bf16)
                acts[layer + 1][par][c, :, cols.start + i * BJ:cols.start + (i + 1) * BJ] = t
                if layer == 2:
                    bt = jnp.sum(ow_c[...] * t.astype(f32), axis=0, keepdims=True) + 1.0
                    row = (j % (CW // SUB)) * (SUB // BJ) + i
                    half = j // (CW // SUB)
                    tiles[half] = jnp.where(rowi == row, bt, tiles[half])

        tasks = [(layer, j) for layer in range(3) for j in range(SUBS)]
        held = None
        for task in tasks:
            d = product(*task)
            if held is not None:
                activate(*held)
            held = task + (d,)
        activate(*held)
        for half in range(2):
            beta_r[pl.ds(pl.multiple_of((2 * pair[half] + 1 - half) * 8, 8), 8), :] = tiles[half]

        @pl.when(k == 0)
        def _():
            make_sel()
            pick(0)

        @pl.when(k == 2)
        def _():
            ghosts(0)
            pack(inner, state, (1, BI - 2))
            res = edge_sweep(cut(edge.at[0]), cut(inner), [ghost_r[0, v] for v in range(NV)])
            for v in range(NV):
                part(edge.at[1], v)[...] = res[v]
            send_plane(1)

        @pl.when(k == 4)
        def _():
            pick(1)

        return carry

    lax.fori_loop(0, NCH // 2, forward, 0)

    for s in range(NS):
        for e in range(2):
            g = 8 * EDGE + 2 * s + e
            row = s * BI + e * (BI - 1)
            betan_r[row:row + 1, :] = beta_r[g:g + 1, :]
        for first, place, length in runs(s):
            betan_r[s * BI + first:s * BI + first + length, :] = beta_r[place:place + length, :]

    rows32 = lax.broadcasted_iota(jnp.int32, (BI, BJ), 0)
    lane32 = lax.broadcasted_iota(jnp.int32, (BI, BJ), 1)

    def stencil(u, low, high):
        up = jnp.where(rows32 == 0, low, pltpu.roll(u, 1, 0))
        down = jnp.where(rows32 == BI - 1, high, pltpu.roll(u, BI - 1, 0))
        return up + down + lanes_sum(u, lane32) - 4.0 * u

    def low_high(k, s, v):
        return ghost_r[k, v, 2 * s:2 * s + 1, :], ghost_r[k, v, 2 * s + 1:2 * s + 2, :]

    for s in range(NS):
        us = [state[v, s] for v in range(NV)]
        beta = betan_r[s * BI:(s + 1) * BI, :]
        for v in range(NV):
            t = jnp.tanh(us[v])
            ts_r[v, s] = t
            low, high = low_high(0, s, v)
            coupled = coup[v, 0] * us[0]
            for w in range(1, NV):
                coupled = coupled + coup[v, w] * us[w]
            mid_r[v, s] = us[v] + tau * (stencil(us[v], low, high) - coupled + beta * t)

    ghosts(1)
    pack(inner, mid_r, (1, BI - 2))
    final_e = edge_sweep(cut(edge.at[1]), cut(inner), [ghost_r[1, v] for v in range(NV)])
    loads[2].wait()
    pack(inner, target, (0, BI - 1))
    goal_e = cut(inner)
    cot_e = [tau * (loss_scale * tile_r[3] * (final_e[v] - goal_e[v])) for v in range(NV)]
    cot_e = turned(cot_e, -1.0)
    for v in range(NV):
        part(cote, v)[...] = cot_e[v]
    cz[mine] = cote[core]
    for w in tower:
        send(cote.at[lax.rem(w, 2)], cz.at[mine], cz_s.at[w], cz_r.at[mine], at_tower(w))

    for s in range(NS):
        us = [mid_r[v, s] for v in range(NV)]
        beta = betan_r[s * BI:(s + 1) * BI, :]
        for v in range(NV):
            t = jnp.tanh(us[v])
            tm_r[v, s] = t
            low, high = low_high(1, s, v)
            coupled = coup[v, 0] * us[0]
            for w in range(1, NV):
                coupled = coupled + coup[v, w] * us[w]
            final = us[v] + tau * (stencil(us[v], low, high) - coupled + beta * t)
            out_state[v, s] = live[s] * final
            fc_r[v, s] = loss_scale * live[s] * (final - target[v, s])

    for s in range(NS):
        gs = [fc_r[v, s] for v in range(NV)]
        beta = betan_r[s * BI:(s + 1) * BI, :]
        acc = jnp.zeros((BI, BJ), f32)
        for v in range(NV):
            t = tm_r[v, s]
            coupled = coup[0, v] * gs[0]
            for w in range(1, NV):
                coupled = coupled + coup[w, v] * gs[w]
            mc = gs[v] + tau * (stencil(gs[v], 0.0, 0.0) - coupled + beta * (1.0 - t * t) * gs[v])
            acc = acc + (gs[v] * t + mc * ts_r[v, s])
        bcn_r[s * BI:(s + 1) * BI, :] = tau * acc
        for first, place, length in runs(s):
            bc_r[place:place + length, :] = bcn_r[s * BI + first:s * BI + first + length, :]

    def table():
        for w in tower:
            got(cz.at[w], cz_s.at[w], cz_r.at[w], at_tower(w))
        sums = by_rows(selt_r[...], cz[...].reshape(2 * ZN * 8, HALF))
        tbl[...] = sums.reshape(PL, 8, HALF)
        ret[p] = tbl[p]
        for q in plane_peers:
            send(tbl.at[q], ret.at[p], rt_s.at[q], rt_r.at[p], at_plane(q))

    def returned():
        for q in plane_peers:
            got(ret.at[q], rt_s.at[q], rt_r.at[q], at_plane(q))
        extra = jnp.zeros((8, BJ), f32)
        for h in range(2):
            total = (ret[h] + ret[2 + h]) + (ret[4 + h] + ret[6 + h])
            for v in range(HV):
                cols = slice(v * BJ, (v + 1) * BJ)
                extra = extra + total[:, cols] * jnp.tanh(edge[0, h, :, cols])
        for s in range(NS):
            for e in range(2):
                g = 2 * s + e
                row = s * BI + e * (BI - 1)
                bc_r[8 * EDGE + g:8 * EDGE + g + 1, :] = bcn_r[row:row + 1, :] + tau * extra[g:g + 1]

    ones = jnp.ones((16, CW), bf16)
    gout[...] = jnp.zeros((HID, BJ), f32)
    gtop[...] = jnp.zeros((HID + 16, HID), f32)
    gmid[...] = jnp.zeros((HID + 16, HID), f32)
    gin[...] = jnp.zeros((NF + 16, HID), f32)

    def weigh(par, k, acc, left, right, fresh=None):
        part = nt(jnp.concatenate([left[par][k], ones], axis=0), right[par][k])
        if fresh is not None:
            part = jnp.where(fresh, part, 0.0)
        acc[...] = acc[...] + part

    def before(k):
        return lax.rem(k + NCH // 2 - 1, NCH // 2)

    RB = 64

    def top_delta(par, k):
        third = third_r[par]
        bc = bc_r[pl.ds(pl.multiple_of((2 * k + par) * 8, 8), 8), :]
        ch = bc.astype(bf16).astype(f32)
        for i in range(HID // RB):
            rows = slice(i * RB, (i + 1) * RB)
            ow = ow_c[rows]
            acc = gout[rows]
            for j in range(CW // BJ):
                cols = slice(j * BJ, (j + 1) * BJ)
                t = third[k, rows, cols].astype(f32)
                acc = acc + t * ch[j:j + 1]
                third[k, rows, cols] = (ow * bc[j:j + 1] * (1.0 - t * t)).astype(bf16)
            gout[rows] = acc

    def back_top(k, carry):
        weigh(1, before(k), gtop, second_r, third_r, k > 0)
        top_delta(0, k)
        weigh(0, k, gtop, second_r, third_r)
        top_delta(1, k)
        return carry

    def layer_back(k, weight, source, act, acc, left, fresh=None):
        held = None

        def put(par, cols, d):
            for i in range(SUB // BJ):
                here = slice(cols.start + i * BJ, cols.start + (i + 1) * BJ)
                t = act[par][k, :, here].astype(f32)
                act[par][k, :, here] = (d[:, i * BJ:(i + 1) * BJ] * (1.0 - t * t)).astype(bf16)

        for par in range(2):
            for j in range(CW // SUB):
                cols = slice(j * SUB, (j + 1) * SUB)
                d = mm(weight[...], source[par][k, :, cols])
                if held is not None:
                    put(*held)
                held = (par, cols, d)
                if j == 0:
                    if par == 0:
                        weigh(1, before(k), acc, left, act, fresh)
                    else:
                        put(*held)
                        held = None
                        weigh(0, k, acc, left, act)
        put(*held)

    def back_mid(k, carry):
        layer_back(k, top_w, third_r, second_r, gmid, first_r, k > 0)
        return carry

    grads = (gtop, gmid)
    R = HID // AN

    def hand(i):
        @pl.when(core != i)
        def _():
            send(grads[i].at[pl.ds(0, HID)], cg, c_s, c_r, partner())

    def ar_1(i):
        got(cg, c_s, c_r, partner())
        gsum[...] = (grads[i][0:HID] + cg[...]).reshape(AN, R, HID)
        for d in range(1, AN):
            q = lax.rem(a + d, AN)
            send(gsum.at[q], ra.at[a], a1_s, a1_r, at_a(q))
        ra[a] = gsum[a]

    def ar_2():
        got(ra.at[pl.ds(0, AN - 1)], a1_s, a1_r, at_a(a))
        total = ra[0]
        for q in range(1, AN):
            total = total + ra[q]
        rb[zz] = total
        for d in range(1, BN):
            send(rb.at[zz], rb.at[zz], a2_s, a2_r, at_b(lax.rem(zz + d, BN)))

    def ar_3():
        got(rb.at[pl.ds(0, BN - 1)], a2_s, a2_r, at_b(zz))
        total = rb[0]
        for w in range(1, BN):
            total = total + rb[w]
        full[a] = total
        for d in range(1, AN):
            send(full.at[a], full.at[a], a3_s, a3_r, at_a(lax.rem(a + d, AN)))

    def ar_4(out):
        got(full.at[pl.ds(0, AN - 1)], a3_s, a3_r, at_a(a))
        send(full, other, f_s, f_r, partner())
        out[...] = full[...].reshape(HID, HID)

    def ar_5(out):
        got(other, f_s, f_r, partner())
        out[...] = other[...].reshape(HID, HID)

    def small_0():
        sg[0:NF] = gin[0:NF]
        sg[NF:NF + 1] = jnp.sum(gout[...].T, axis=0, keepdims=True)
        sg[NF + 1:NF + 2] = gin[NF:NF + 1]
        sg[NF + 2:NF + 3] = gmid[HID:HID + 1]
        sg[NF + 3:NF + 4] = gtop[HID:HID + 1]
        sg[NF + 4:NF + 8] = jnp.zeros((4, HID), f32)

        @pl.when(core == 1)
        def _():
            send(sg, sc, s0_s, s0_r, partner())

    def small_1():
        got(sc, s0_s, s0_r, partner())
        sa[a] = sg[...] + sc[...]
        for d in range(1, AN):
            send(sa.at[a], sa.at[a], s1_s, s1_r, at_a(lax.rem(a + d, AN)))

    def small_2():
        got(sa.at[pl.ds(0, AN - 1)], s1_s, s1_r, at_a(a))
        total = sa[0]
        for q in range(1, AN):
            total = total + sa[q]
        sb[zz] = total
        for d in range(1, BN):
            send(sb.at[zz], sb.at[zz], s2_s, s2_r, at_b(lax.rem(zz + d, BN)))

    def small_3():
        got(sb.at[pl.ds(0, BN - 1)], s2_s, s2_r, at_b(zz))
        total = sb[0]
        for w in range(1, BN):
            total = total + sb[w]
        sf[...] = total
        send(sf, st, s3_s, s3_r, partner())

    LAST = NCH // 2 - 1
    lax.fori_loop(0, LAST, back_top, 0)
    weigh(1, LAST - 1, gtop, second_r, third_r)
    table()
    top_delta(0, LAST)
    weigh(0, LAST, gtop, second_r, third_r)
    lax.fori_loop(0, LAST, back_mid, 0)
    returned()
    top_delta(1, LAST)
    weigh(1, LAST, gtop, second_r, third_r)
    hand(0)
    layer_back(LAST, top_w, third_r, second_r, gmid, first_r)
    weigh(1, LAST, gmid, first_r, second_r)
    hand(1)

    @pl.when(core == 0)
    def _():
        ar_1(0)

    def back_first(k, carry):
        layer_back(k, mid_w, second_r, first_r, gin, x_r, k > 0)

        @pl.when((k == 1) & (core == 1))
        def _():
            ar_1(1)

        @pl.when((k == 4) & (core == 0))
        def _():
            ar_2()

        return carry

    lax.fori_loop(0, LAST + 1, back_first, 0)
    weigh(1, LAST, gin, x_r, first_r)

    small_0()

    @pl.when(core == 0)
    def _():
        small_1()
        ar_3()
        small_2()
        ar_4(out_top)
        small_3()
        out_in[...] = sf[0:NF]
        out_vec[...] = sf[NF:NF + 4]
        ar_5(out_mid)

    @pl.when(core == 1)
    def _():
        ar_2()
        ar_3()
        ar_4(out_mid)
        ar_5(out_top)
        got(st, s3_s, s3_r, partner())
        out_in[...] = st[0:NF]
        out_vec[...] = st[NF:NF + 4]

    for k in range(2):
        for q in plane_peers:
            gone(edge.at[k, core], pl_s.at[k, q], pl_r.at[k, p], at_plane(q))
        for w in tower:
            gone(picked.at[k, w], zz_s.at[k, w], zz_r.at[k, mine], at_tower(w))
    for w in tower:
        gone(meta.at[mine], me_s.at[w], me_r.at[mine], at_tower(w))
        gone(cote.at[core], cz_s.at[w], cz_r.at[mine], at_tower(w))
    for q in plane_peers:
        gone(tbl.at[q], rt_s.at[q], rt_r.at[p], at_plane(q))
    gone(cg, c_s, c_r, partner())
    gone(ra.at[pl.ds(0, AN - 1)], a1_s, a1_r, at_a(a))
    gone(rb.at[pl.ds(0, BN - 1)], a2_s, a2_r, at_b(zz))
    gone(full.at[pl.ds(0, AN - 1)], a3_s, a3_r, at_a(a))
    gone(full, f_s, f_r, partner())

    @pl.when(core == 0)
    def _():
        gone(sa.at[pl.ds(0, AN - 1)], s1_s, s1_r, at_a(a))
        gone(sb.at[pl.ds(0, BN - 1)], s2_s, s2_r, at_b(zz))
        gone(sf, s3_s, s3_r, partner())

    @pl.when(core == 1)
    def _():
        gone(sg, s0_s, s0_r, partner())


def copy_kernel(*refs):
    ins, outs, sem = refs[:5], refs[5:10], refs[10]
    copies = [pltpu.make_async_copy(ins[i], outs[i], sem.at[i]) for i in range(5)]
    for copy in copies:
        copy.start()
    for copy in copies:
        copy.wait()


def per_device(
    initial_state, target, features, coupling, in_weight, mid_weight, top_weight, out_weight, biases,
    block_count, connectivity, orientation, rotation,
):
    cells = lax.axis_size("op") * lax.axis_size("blk") * NS * BI * BJ
    loss_scale = 2.0 / math.sqrt(cells)
    vmem = pl.BlockSpec(memory_space=pltpu.VMEM)
    smem = pl.BlockSpec(memory_space=pltpu.SMEM)
    anywhere = pl.BlockSpec(memory_space=pl.ANY)
    dma = pltpu.SemaphoreType.DMA
    field = pltpu.VMEM((NV, NS, BI, BJ), f32)
    outs = pl.pallas_call(
        functools.partial(kernel, loss_scale),
        out_shape=(
            jax.ShapeDtypeStruct((NV, NS, BI, BJ), f32),
            jax.ShapeDtypeStruct((NF, HID), f32),
            jax.ShapeDtypeStruct((HID, HID), f32),
            jax.ShapeDtypeStruct((HID, HID), f32),
            jax.ShapeDtypeStruct((4, HID), f32),
        ),
        in_specs=[anywhere, anywhere, anywhere, smem, vmem, vmem, vmem, vmem, vmem, smem, smem, smem, smem],
        out_specs=(vmem,) * 5,
        scratch_shapes=[
            field, field, pltpu.VMEM((NF, NS, BI, BJ), bf16),
            pltpu.VMEM((NCH // 2, NF, CW), bf16),
            pltpu.VMEM((NCH // 2, NF, CW), bf16),
            pltpu.VMEM((NCH // 2, HID, CW), bf16),
            pltpu.VMEM((NCH // 2, HID, CW), bf16),
            pltpu.VMEM((NCH // 2, HID, CW), bf16),
            pltpu.VMEM((NCH // 2, HID, CW), bf16),
            pltpu.VMEM((NCH // 2, HID, CW), bf16),
            pltpu.VMEM((NCH // 2, HID, CW), bf16),
            pltpu.VMEM((NS, 2, NF * 16, BJ), f32),
            pltpu.VMEM((HID, NF), bf16),
            pltpu.VMEM((HID, HID), bf16),
            pltpu.VMEM((HID, HID), bf16),
            pltpu.VMEM((3, HID, BJ), f32),
            pltpu.VMEM((HID, BJ), f32),
            field, field, field, field,
            pltpu.VMEM((NS * BI, BJ), f32),
            pltpu.VMEM((NS * BI, BJ), f32),
            pltpu.VMEM((NS * BI, BJ), f32),
            pltpu.VMEM((NS * BI, BJ), f32),
            pltpu.VMEM((2, 2, 8, HALF), f32),
            pltpu.VMEM((2, PL, 8, HALF), f32),
            pltpu.VMEM((2, 2 * ZN, 8, HALF), f32),
            pltpu.VMEM((2, 2 * ZN, 8, HALF), f32),
            pltpu.VMEM((2, 8, HALF), f32),
            pltpu.VMEM((4, 8, BJ), f32),
            pltpu.VMEM((2 * ZN, 8, BJ), f32),
            pltpu.VMEM((2 * ZN * 8, PL * 8), bf16),
            pltpu.VMEM((PL * 8, 2 * ZN * 8), bf16),
            pltpu.VMEM((2, NV, 8, BJ), f32),
            pltpu.VMEM((2, 8, HALF), f32),
            pltpu.VMEM((2 * ZN, 8, HALF), f32),
            pltpu.VMEM((PL, 8, HALF), f32),
            pltpu.VMEM((PL, 8, HALF), f32),
            pltpu.VMEM((HID + 16, HID), f32),
            pltpu.VMEM((HID + 16, HID), f32),
            pltpu.VMEM((NF + 16, HID), f32),
            pltpu.VMEM((HID, BJ), f32),
            pltpu.VMEM((HID, HID), f32),
            pltpu.VMEM((AN, HID // AN, HID), f32),
            pltpu.VMEM((AN, HID // AN, HID), f32),
            pltpu.VMEM((BN, HID // AN, HID), f32),
            pltpu.VMEM((AN, HID // AN, HID), f32),
            pltpu.VMEM((AN, HID // AN, HID), f32),
            pltpu.VMEM((24, HID), f32),
            pltpu.VMEM((24, HID), f32),
            pltpu.VMEM((AN, 24, HID), f32),
            pltpu.VMEM((BN, 24, HID), f32),
            pltpu.VMEM((24, HID), f32),
            pltpu.VMEM((24, HID), f32),
            dma((2, PL)), dma((2, PL)), dma((2 * ZN,)), dma((2 * ZN,)), dma((2, 2 * ZN)), dma((2, 2 * ZN)),
            dma((2 * ZN,)), dma((2 * ZN,)), dma((PL,)), dma((PL,)),
            dma((3,)), dma, dma, dma, dma, dma, dma, dma, dma, dma, dma, dma, dma, dma, dma, dma, dma, dma, dma,
        ],
        compiler_params=pltpu.CompilerParams(
            collective_id=0, has_side_effects=True, vmem_limit_bytes=56 * 2**20
        ),
    )(
        initial_state[0], target[0], features[0], coupling, in_weight, mid_weight, top_weight,
        out_weight, biases, block_count, connectivity.T, orientation.T, rotation.T,
    )
    outs = pl.pallas_call(
        copy_kernel,
        out_shape=tuple(jax.ShapeDtypeStruct(x.shape, x.dtype) for x in outs),
        in_specs=[vmem] * 5,
        out_specs=(pl.BlockSpec(memory_space=pl.ANY),) * 5,
        scratch_shapes=[dma((5,))],
    )(*outs)
    return (outs[0][None],) + tuple(outs[1:])


def solution(mesh):
    wide = P("op", None, "blk", None, None)
    return jax.shard_map(
        per_device,
        mesh=mesh,
        in_specs=(wide, wide, wide) + (P(),) * 6 + (P("blk"),) + (P("blk", None),) * 3,
        out_specs=(wide, P(), P(), P(), P()),
        check_vma=False,
    )
```

```python
import functools
import math

import jax
import jax.numpy as jnp
from jax import lax
from jax.experimental import pallas as pl
from jax.experimental.pallas import tpu as pltpu
from jax.sharding import PartitionSpec as P

MESH = pl.DeviceIdType.MESH
tau = 0.2
passage_angle = 2.0 * math.pi / 36.0
cos_step = math.cos(passage_angle)
sin_step = math.sin(passage_angle)
f32 = jnp.float32
bf16 = jnp.bfloat16

NV, NS, BI, BJ, HID, NF = 6, 3, 32, 128, 256, 16
PL = 8
ZN = 4
NCH = 12
CW = 1024
EDGE = NCH - 1
AN = 16
BN = 8
HV = NV // 2
HALF = HV * BJ


def row_of(s, i):
    if i == 0 or i == BI - 1:
        return 8 * EDGE + 2 * s + (i != 0)
    inner = (BI - 2) * s + i - 1
    return inner if inner < 8 * EDGE else inner + 2 * NS


def runs(s):
    whole = (BI - 2) * s
    first = min(BI - 2, 8 * EDGE - whole)
    res = [(1, whole, first)]
    if first < BI - 2:
        res.append((1 + first, row_of(s, 1 + first), BI - 2 - first))
    return res


def nt(a, b):
    return lax.dot_general(a, b, (((1,), (1,)), ((), ())), preferred_element_type=f32)


def mm(a, b):
    return jnp.dot(a, b, preferred_element_type=f32)


def lanes_sum(u, lane):
    left = jnp.where(lane == 0, u, pltpu.roll(u, 1, 1))
    right = jnp.where(lane == BJ - 1, u, pltpu.roll(u, BJ - 1, 1))
    return left + right


def kernel(
    loss_scale,
    state_h, target_h, feat_h, coup, in_w, mid_w, top_w, out_w, biases, count, conn, orient, rot,
    out_state, out_in, out_mid, out_top, out_vec,
    state, target, feat, x0, x1, first0, first1, second0, second1, third0, third1,
    xs, win_t, wmid_t, wtop_t, bias_c, ow_c,
    mid_r, ts_r, tm_r, fc_r, beta_r, betan_r, bc_r, bcn_r,
    edge, gath, picked, arr, inner, tile_r, meta, sel_r, selt_r, ghost_r,
    cote, cz, tbl, ret,
    gtop, gmid, gin, gout,
    cg, gsum, ra, rb, full, sg, sa, sb, sf,
    pl_s, pl_r, me_s, me_r, zz_s, zz_r, cz_s, cz_r, rt_s, rt_r,
    in_s, c_s, c_r, a1_s, a1_r, a2_s, a2_r, a3_s, a3_r, f_s, f_r, s1_s, s1_r, s2_s, s2_r, s3_s, s3_r,
):
    x_r, first_r, second_r, third_r = (x0, x1), (first0, first1), (second0, second1), (third0, third1)
    b = lax.axis_index("blk")
    o = lax.axis_index("op")
    z = lax.div(b, PL)
    p = lax.rem(b, PL)

    plane_peers = [lax.rem(p + d, PL) for d in range(1, PL)]
    x_at = lax.div(o, 2)
    z_lo = lax.rem(o, 2)
    core = lax.rem(b, 2)
    mine = z * 2 + core
    tower = [lax.rem(mine + d, 2 * ZN) for d in range(1, 2 * ZN)]
    a = x_at * ZN + lax.div(p, 2)
    zz = z * 2 + z_lo

    def at_plane(q):
        return {"blk": z * PL + q}

    def at_tower(w):
        return {"blk": lax.div(w, 2) * PL + p - core + lax.rem(w, 2)}

    def at_a(q):
        return {"blk": z * PL + lax.rem(q, 4) * 2 + core, "op": lax.div(q, 4) * 2 + z_lo}

    def at_zc(w, c):
        return {"blk": lax.div(w, 2) * PL + p - core + c, "op": x_at * 2 + lax.rem(w, 2)}

    def partner():
        return {"blk": b + 1 - 2 * core}

    def at_b(w):
        return {"blk": lax.div(w, 2) * PL + p, "op": x_at * 2 + lax.rem(w, 2)}

    def send(src, dst, s_sem, r_sem, device):
        copy = pltpu.make_async_remote_copy(
            src_ref=src, dst_ref=dst, send_sem=s_sem, recv_sem=r_sem, device_id=device, device_id_type=MESH
        )
        copy.start()

    def got(dst, s_sem, r_sem, device):
        pltpu.make_async_remote_copy(
            src_ref=dst, dst_ref=dst, send_sem=s_sem, recv_sem=r_sem, device_id=device, device_id_type=MESH
        ).wait_recv()

    def gone(src, s_sem, r_sem, device):
        pltpu.make_async_remote_copy(
            src_ref=src, dst_ref=src, send_sem=s_sem, recv_sem=r_sem, device_id=device, device_id_type=MESH
        ).wait_send()

    barrier = pltpu.get_barrier_semaphore()
    def greet(device):
        pl.semaphore_signal(barrier, inc=1, device_id=device, device_id_type=MESH)

    for q in plane_peers:
        greet(at_plane(q))
    for d in range(4, AN):
        greet(at_a(lax.rem(x_at * 4 + d, AN)))
    for d in range(1, BN):
        for c in range(2):
            greet(at_zc(lax.rem(zz + d, BN), c))

    loads = [pltpu.make_async_copy(h, v, in_s.at[i]) for i, (h, v) in enumerate(((state_h, state), (feat_h, feat), (target_h, target)))]
    for load in loads:
        load.start()

    rowi = lax.broadcasted_iota(jnp.int32, (8, BJ), 0)
    lane8 = lax.broadcasted_iota(jnp.int32, (8, BJ), 1)
    meta_t = jnp.full((8, BJ), -1.0, f32)
    flip_t = jnp.zeros((8, BJ), f32)
    cos_t = jnp.ones((8, BJ), f32)
    sin_t = jnp.zeros((8, BJ), f32)
    live_t = jnp.zeros((8, BJ), f32)
    live = []
    for s in range(NS):
        live.append(jnp.where(s < count[0], 1.0, 0.0).astype(f32))
        for e in range(2):
            here = rowi == 2 * s + e
            idx = conn[e, s]
            idx = idx + 2 * ((idx * 10923) >> 16)
            meta_t = jnp.where(here, idx.astype(f32), meta_t)
            flip_t = jnp.where(here, orient[e, s].astype(f32), flip_t)
            turn = rot[e, s]
            cos_t = jnp.where(here, jnp.where(turn == 0, 1.0, cos_step).astype(f32), cos_t)
            sin_t = jnp.where(here, turn.astype(f32) * sin_step, sin_t)
            live_t = jnp.where(here, live[s], live_t)
    meta[mine] = meta_t
    tile_r[0] = flip_t
    tile_r[1] = cos_t
    tile_r[2] = sin_t
    tile_r[3] = live_t

    def part(ref, v):
        return ref.at[v // HV, :, v % HV * BJ:(v % HV + 1) * BJ]

    def pack(dst, field, rows):
        dst[...] = jnp.zeros((2, 8, HALF), f32)
        for v in range(NV):
            for s in range(NS):
                for e in range(2):
                    part(dst, v)[2 * s + e:2 * s + e + 1, :] = field[v, s, rows[e]:rows[e] + 1, :]

    def cut(ref):
        return [part(ref, v)[...] for v in range(NV)]

    def thirds(u):
        u1 = u.astype(bf16)
        u2 = (u - u1.astype(f32)).astype(bf16)
        u3 = (u - u1.astype(f32) - u2.astype(f32)).astype(bf16)
        return u1, u2, u3

    def by_rows(mask, u):
        r = mm(mask, jnp.concatenate(thirds(u), axis=1))
        return r[:, :HALF] + r[:, HALF:2 * HALF] + r[:, 2 * HALF:]

    loads[0].wait()
    pack(edge.at[0], state, (0, BI - 1))

    pl.semaphore_wait(barrier, PL - 1 + AN - 4 + 2 * (BN - 1))

    def send_plane(k):
        for q in plane_peers:
            send(edge.at[k, lax.rem(q, 2)], gath.at[k, p], pl_s.at[k, q], pl_r.at[k, p], at_plane(q))
        gath[k, p] = edge[k, core]

    for w in tower:
        send(meta.at[mine], meta.at[mine], me_s.at[w], me_r.at[mine], at_tower(w))
    send_plane(0)

    def pick(k):
        for q in plane_peers:
            got(gath.at[k, q], pl_s.at[k, q], pl_r.at[k, q], at_plane(q))
        chosen = by_rows(sel_r[...], gath[k].reshape(PL * 8, HALF))
        picked[k] = chosen.reshape(2 * ZN, 8, HALF)
        arr[k, mine] = picked[k, mine]
        for w in tower:
            send(picked.at[k, w], arr.at[k, mine], zz_s.at[k, w], zz_r.at[k, mine], at_tower(w))

    def make_sel():
        for w in tower:
            got(meta.at[w], me_s.at[w], me_r.at[w], at_tower(w))
        n = 2 * ZN * 8
        lane = lax.broadcasted_iota(jnp.int32, (n, BJ), 1)
        named = meta[...].reshape(n, BJ)
        local = named - (z * (PL * 8)).astype(f32)
        sel = jnp.where((local == lane.astype(f32)) & (lane < PL * 8), 1.0, 0.0).astype(f32)
        sel_r[...] = sel[:, :PL * 8].astype(bf16)
        wide = jnp.concatenate([sel, jnp.zeros((BJ - n, BJ), f32)], axis=0).T
        selt_r[...] = wide[:PL * 8, :n].astype(bf16)

    def turned(parts, sign):
        flip, cos, sin = tile_r[0], tile_r[1], tile_r[2] * sign
        r = lax.broadcasted_iota(jnp.int32, (BJ, BJ), 0)
        c = lax.broadcasted_iota(jnp.int32, (BJ, BJ), 1)
        anti = jnp.where(r + c == BJ - 1, 1.0, 0.0).astype(bf16)
        n = 8 * NV
        back = mm(jnp.concatenate(thirds(jnp.concatenate(parts, axis=0)), axis=0), anti)
        back = back[:n] + back[n:2 * n] + back[2 * n:]
        out = [jnp.where(flip > 0.5, back[8 * v:8 * v + 8], parts[v]) for v in range(NV)]
        c2 = cos * out[2] - sin * out[3]
        c3 = sin * out[2] + cos * out[3]
        return [out[0], out[1], c2, c3, out[4], out[5]]

    def ghosts(k):
        for w in tower:
            got(arr.at[k, w], zz_s.at[k, w], zz_r.at[k, w], at_tower(w))
        total = [(arr[k, h] + arr[k, 2 + h]) + (arr[k, 4 + h] + arr[k, 6 + h]) for h in range(2)]
        parts = turned([total[v // HV][:, v % HV * BJ:(v % HV + 1) * BJ] for v in range(NV)], 1.0)
        for v in range(NV):
            ghost_r[k, v] = parts[v]

    def edge_sweep(e, n, gh):
        res = []
        beta_e = jnp.where(rowi < 2 * NS, beta_r[8 * EDGE:8 * EDGE + 8, :], 0.0)
        for v in range(NV):
            lap = gh[v] + n[v] + lanes_sum(e[v], lane8) - 4.0 * e[v]
            coupled = coup[v, 0] * e[0]
            for w in range(1, NV):
                coupled = coupled + coup[v, w] * e[w]
            res.append(e[v] + tau * (lap - coupled + beta_e * jnp.tanh(e[v])))
        return res

    pad = jnp.zeros((BJ - NF, HID), f32)
    win_t[...] = jnp.concatenate([in_w[...].astype(f32), pad], axis=0).T[:, :NF].astype(bf16)
    wmid_t[...] = mid_w[...].astype(f32).T.astype(bf16)
    wtop_t[...] = top_w[...].astype(f32).T.astype(bf16)
    for k in range(3):
        bias_c[k] = jnp.broadcast_to(biases[k:k + 1, :], (BJ, HID)).T
    ow_c[...] = jnp.broadcast_to(out_w[...].astype(f32).reshape(1, HID), (BJ, HID)).T

    loads[1].wait()
    for s in range(NS):
        for h in range(2):
            xs[s, h] = feat[:, s, 16 * h:16 * h + 16, :].astype(f32).reshape(NF * 16, BJ)
    for s in range(NS):
        for h in range(2):
            for r in range(16):
                row = row_of(s, 16 * h + r)
                x_r[row // 8 % 2][row // 16, :, (row % 8) * BJ:(row % 8 + 1) * BJ] = xs[s, h, pl.ds(r, NF, stride=16), :].astype(bf16)

    SUB = 256

    weights = (win_t, wmid_t, wtop_t)
    acts = (x_r, first_r, second_r, third_r)
    SUBS = 2 * CW // SUB

    def forward(k, carry):
        pair = (lax.rem(k + EDGE // 2, NCH // 2), k)

        def place(j):
            half = j // (CW // SUB)
            return 1 - half, pair[half], slice((j % (CW // SUB)) * SUB, (j % (CW // SUB) + 1) * SUB)

        def product(layer, j):
            par, c, cols = place(j)
            return mm(weights[layer][...], acts[layer][par][c, :, cols])

        tiles = [jnp.zeros((8, BJ), f32), jnp.zeros((8, BJ), f32)]

        def activate(layer, j, d):
            par, c, cols = place(j)
            bias = bias_c[layer]
            for i in range(SUB // BJ):
                t = jnp.tanh(d[:, i * BJ:(i + 1) * BJ] + bias).astype(bf16)
                acts[layer + 1][par][c, :, cols.start + i * BJ:cols.start + (i + 1) * BJ] = t
                if layer == 2:
                    bt = jnp.sum(ow_c[...] * t.astype(f32), axis=0, keepdims=True) + 1.0
                    row = (j % (CW // SUB)) * (SUB // BJ) + i
                    half = j // (CW // SUB)
                    tiles[half] = jnp.where(rowi == row, bt, tiles[half])

        tasks = [(layer, j) for layer in range(3) for j in range(SUBS)]
        held = None
        for task in tasks:
            d = product(*task)
            if held is not None:
                activate(*held)
            held = task + (d,)
        activate(*held)
        for half in range(2):
            beta_r[pl.ds(pl.multiple_of((2 * pair[half] + 1 - half) * 8, 8), 8), :] = tiles[half]

        @pl.when(k == 0)
        def _():
            make_sel()
            pick(0)

        @pl.when(k == 2)
        def _():
            ghosts(0)
            pack(inner, state, (1, BI - 2))
            res = edge_sweep(cut(edge.at[0]), cut(inner), [ghost_r[0, v] for v in range(NV)])
            for v in range(NV):
                part(edge.at[1], v)[...] = res[v]
            send_plane(1)

        @pl.when(k == 4)
        def _():
            pick(1)

        return carry

    lax.fori_loop(0, NCH // 2, forward, 0)

    for s in range(NS):
        for e in range(2):
            g = 8 * EDGE + 2 * s + e
            row = s * BI + e * (BI - 1)
            betan_r[row:row + 1, :] = beta_r[g:g + 1, :]
        for first, place, length in runs(s):
            betan_r[s * BI + first:s * BI + first + length, :] = beta_r[place:place + length, :]

    rows32 = lax.broadcasted_iota(jnp.int32, (BI, BJ), 0)
    lane32 = lax.broadcasted_iota(jnp.int32, (BI, BJ), 1)

    def stencil(u, low, high):
        up = jnp.where(rows32 == 0, low, pltpu.roll(u, 1, 0))
        down = jnp.where(rows32 == BI - 1, high, pltpu.roll(u, BI - 1, 0))
        return up + down + lanes_sum(u, lane32) - 4.0 * u

    def low_high(k, s, v):
        return ghost_r[k, v, 2 * s:2 * s + 1, :], ghost_r[k, v, 2 * s + 1:2 * s + 2, :]

    for s in range(NS):
        us = [state[v, s] for v in range(NV)]
        beta = betan_r[s * BI:(s + 1) * BI, :]
        for v in range(NV):
            t = jnp.tanh(us[v])
            ts_r[v, s] = t
            low, high = low_high(0, s, v)
            coupled = coup[v, 0] * us[0]
            for w in range(1, NV):
                coupled = coupled + coup[v, w] * us[w]
            mid_r[v, s] = us[v] + tau * (stencil(us[v], low, high) - coupled + beta * t)

    ghosts(1)
    pack(inner, mid_r, (1, BI - 2))
    final_e = edge_sweep(cut(edge.at[1]), cut(inner), [ghost_r[1, v] for v in range(NV)])
    loads[2].wait()
    pack(inner, target, (0, BI - 1))
    goal_e = cut(inner)
    cot_e = [tau * (loss_scale * tile_r[3] * (final_e[v] - goal_e[v])) for v in range(NV)]
    cot_e = turned(cot_e, -1.0)
    for v in range(NV):
        part(cote, v)[...] = cot_e[v]
    cz[mine] = cote[core]
    for w in tower:
        send(cote.at[lax.rem(w, 2)], cz.at[mine], cz_s.at[w], cz_r.at[mine], at_tower(w))

    for s in range(NS):
        us = [mid_r[v, s] for v in range(NV)]
        beta = betan_r[s * BI:(s + 1) * BI, :]
        for v in range(NV):
            t = jnp.tanh(us[v])
            tm_r[v, s] = t
            low, high = low_high(1, s, v)
            coupled = coup[v, 0] * us[0]
            for w in range(1, NV):
                coupled = coupled + coup[v, w] * us[w]
            final = us[v] + tau * (stencil(us[v], low, high) - coupled + beta * t)
            out_state[v, s] = live[s] * final
            fc_r[v, s] = loss_scale * live[s] * (final - target[v, s])

    for s in range(NS):
        gs = [fc_r[v, s] for v in range(NV)]
        beta = betan_r[s * BI:(s + 1) * BI, :]
        acc = jnp.zeros((BI, BJ), f32)
        for v in range(NV):
            t = tm_r[v, s]
            coupled = coup[0, v] * gs[0]
            for w in range(1, NV):
                coupled = coupled + coup[w, v] * gs[w]
            mc = gs[v] + tau * (stencil(gs[v], 0.0, 0.0) - coupled + beta * (1.0 - t * t) * gs[v])
            acc = acc + (gs[v] * t + mc * ts_r[v, s])
        bcn_r[s * BI:(s + 1) * BI, :] = tau * acc
        for first, place, length in runs(s):
            bc_r[place:place + length, :] = bcn_r[s * BI + first:s * BI + first + length, :]

    def table():
        for w in tower:
            got(cz.at[w], cz_s.at[w], cz_r.at[w], at_tower(w))
        sums = by_rows(selt_r[...], cz[...].reshape(2 * ZN * 8, HALF))
        tbl[...] = sums.reshape(PL, 8, HALF)
        ret[p] = tbl[p]
        for q in plane_peers:
            send(tbl.at[q], ret.at[p], rt_s.at[q], rt_r.at[p], at_plane(q))

    def returned():
        for q in plane_peers:
            got(ret.at[q], rt_s.at[q], rt_r.at[q], at_plane(q))
        extra = jnp.zeros((8, BJ), f32)
        for h in range(2):
            total = (ret[h] + ret[2 + h]) + (ret[4 + h] + ret[6 + h])
            for v in range(HV):
                cols = slice(v * BJ, (v + 1) * BJ)
                extra = extra + total[:, cols] * jnp.tanh(edge[0, h, :, cols])
        for s in range(NS):
            for e in range(2):
                g = 2 * s + e
                row = s * BI + e * (BI - 1)
                bc_r[8 * EDGE + g:8 * EDGE + g + 1, :] = bcn_r[row:row + 1, :] + tau * extra[g:g + 1]

    ones = jnp.ones((16, CW), bf16)
    gout[...] = jnp.zeros((HID, BJ), f32)
    gtop[...] = jnp.zeros((HID + 16, HID), f32)
    gmid[...] = jnp.zeros((HID + 16, HID), f32)
    gin[...] = jnp.zeros((NF + 16, HID), f32)

    def weigh(par, k, acc, left, right, fresh=None):
        part = nt(jnp.concatenate([left[par][k], ones], axis=0), right[par][k])
        if fresh is not None:
            part = jnp.where(fresh, part, 0.0)
        acc[...] = acc[...] + part

    def before(k):
        return lax.rem(k + NCH // 2 - 1, NCH // 2)

    RB = 64

    def top_delta(par, k):
        third = third_r[par]
        bc = bc_r[pl.ds(pl.multiple_of((2 * k + par) * 8, 8), 8), :]
        ch = bc.astype(bf16).astype(f32)
        for i in range(HID // RB):
            rows = slice(i * RB, (i + 1) * RB)
            ow = ow_c[rows]
            acc = gout[rows]
            for j in range(CW // BJ):
                cols = slice(j * BJ, (j + 1) * BJ)
                t = third[k, rows, cols].astype(f32)
                acc = acc + t * ch[j:j + 1]
                third[k, rows, cols] = (ow * bc[j:j + 1] * (1.0 - t * t)).astype(bf16)
            gout[rows] = acc

    def back_top(k, carry):
        weigh(1, before(k), gtop, second_r, third_r, k > 0)
        top_delta(0, k)
        weigh(0, k, gtop, second_r, third_r)
        top_delta(1, k)
        return carry

    def layer_back(k, weight, source, act, acc, left, fresh=None):
        held = None

        def put(par, cols, d):
            for i in range(SUB // BJ):
                here = slice(cols.start + i * BJ, cols.start + (i + 1) * BJ)
                t = act[par][k, :, here].astype(f32)
                act[par][k, :, here] = (d[:, i * BJ:(i + 1) * BJ] * (1.0 - t * t)).astype(bf16)

        for par in range(2):
            for j in range(CW // SUB):
                cols = slice(j * SUB, (j + 1) * SUB)
                d = mm(weight[...], source[par][k, :, cols])
                if held is not None:
                    put(*held)
                held = (par, cols, d)
                if j == 0:
                    if par == 0:
                        weigh(1, before(k), acc, left, act, fresh)
                    else:
                        put(*held)
                        held = None
                        weigh(0, k, acc, left, act)
        put(*held)

    def back_mid(k, carry):
        layer_back(k, top_w, third_r, second_r, gmid, first_r, k > 0)
        return carry

    grads = (gtop, gmid)
    HR = HID // 2
    R = HR // AN

    def hand(i):
        other = pl.ds(pl.multiple_of((1 - core) * HR, HR), HR)
        send(grads[i].at[other], cg.at[i], c_s.at[i], c_r.at[i], partner())

    def ar_1(i):
        got(cg.at[i], c_s.at[i], c_r.at[i], partner())
        half = grads[i][pl.ds(pl.multiple_of(core * HR, HR), HR), :] + cg[i]
        gsum[i] = half.reshape(AN, R, HID)
        for d in range(1, AN):
            q = lax.rem(a + d, AN)
            send(gsum.at[i, q], ra.at[i, a], a1_s.at[i], a1_r.at[i], at_a(q))
        ra[i, a] = gsum[i, a]

    def ar_2(i):
        got(ra.at[i, pl.ds(0, AN - 1)], a1_s.at[i], a1_r.at[i], at_b(zz))
        total = ra[i, 0]
        for q in range(1, AN):
            total = total + ra[i, q]
        rb[i, zz] = total
        for d in range(1, BN):
            send(rb.at[i, zz], rb.at[i, zz], a2_s.at[i], a2_r.at[i], at_b(lax.rem(zz + d, BN)))

    def ar_3(i):
        got(rb.at[i, pl.ds(0, BN - 1)], a2_s.at[i], a2_r.at[i], at_b(zz))
        total = rb[i, 0]
        for w in range(1, BN):
            total = total + rb[i, w]
        full[i, core, a] = total
        for d in range(1, AN):
            send(full.at[i, core, a], full.at[i, core, a], a3_s.at[i], a3_r.at[i], at_a(lax.rem(a + d, AN)))

    def ar_4(i):
        got(full.at[i, core, pl.ds(0, AN - 1)], a3_s.at[i], a3_r.at[i], at_b(zz))
        send(full.at[i, core], full.at[i, core], f_s.at[i], f_r.at[i], partner())

    def ar_5(i, out):
        got(full.at[i, 1 - core], f_s.at[i], f_r.at[i], partner())
        out[...] = full[i].reshape(HID, HID)

    def small_1():
        for r in range(NF):
            sg[r // 2, r % 2:r % 2 + 1] = gin[r:r + 1]
        sg[NF // 2, 0:1] = jnp.sum(gout[...].T, axis=0, keepdims=True)
        sg[NF // 2, 1:2] = gin[NF:NF + 1]
        sg[NF // 2 + 1, 0:1] = gmid[HID:HID + 1]
        sg[NF // 2 + 1, 1:2] = gtop[HID:HID + 1]
        sg[NF // 2 + 2:] = jnp.zeros((AN - NF // 2 - 2, 2, HID), f32)
        for d in range(1, AN):
            q = lax.rem(a + d, AN)
            send(sg.at[q], sa.at[a], s1_s, s1_r, at_a(q))
        sa[a] = sg[a]

    def small_2():
        got(sa.at[pl.ds(0, AN - 1)], s1_s, s1_r, at_a(a))
        total = sa[0]
        for q in range(1, AN):
            total = total + sa[q]
        own = 2 * zz + core
        sb[own] = total
        send(sb.at[own], sb.at[own], s2_s, s2_r, partner())
        for d in range(1, BN):
            for c in range(2):
                send(sb.at[own], sb.at[own], s2_s, s2_r, at_zc(lax.rem(zz + d, BN), c))

    def small_3():
        got(sb.at[pl.ds(0, 2 * BN - 1)], s2_s, s2_r, at_b(zz))
        total = sb[0]
        for w in range(1, 2 * BN):
            total = total + sb[w]
        sf[a] = total
        for d in range(1, AN):
            send(sf.at[a], sf.at[a], s3_s, s3_r, at_a(lax.rem(a + d, AN)))

    def small_4():
        got(sf.at[pl.ds(0, AN - 1)], s3_s, s3_r, at_a(a))
        for r in range(NF):
            out_in[r:r + 1] = sf[r // 2, r % 2:r % 2 + 1]
        for r in range(4):
            out_vec[r:r + 1] = sf[(NF + r) // 2, r % 2:r % 2 + 1]

    LAST = NCH // 2 - 1
    lax.fori_loop(0, LAST, back_top, 0)
    weigh(1, LAST - 1, gtop, second_r, third_r)
    table()
    top_delta(0, LAST)
    weigh(0, LAST, gtop, second_r, third_r)
    lax.fori_loop(0, LAST, back_mid, 0)
    returned()
    top_delta(1, LAST)
    weigh(1, LAST, gtop, second_r, third_r)
    hand(0)
    layer_back(LAST, top_w, third_r, second_r, gmid, first_r)
    weigh(1, LAST, gmid, first_r, second_r)
    hand(1)
    ar_1(0)

    def back_first(k, carry):
        layer_back(k, mid_w, second_r, first_r, gin, x_r, k > 0)

        @pl.when(k == 1)
        def _():
            ar_1(1)

        @pl.when(k == 3)
        def _():
            ar_2(0)

        @pl.when(k == 5)
        def _():
            ar_2(1)

        return carry

    lax.fori_loop(0, LAST + 1, back_first, 0)
    weigh(1, LAST, gin, x_r, first_r)

    small_1()
    ar_3(0)
    ar_3(1)
    small_2()
    ar_4(0)
    ar_4(1)
    small_3()
    ar_5(0, out_top)
    ar_5(1, out_mid)
    small_4()

    for k in range(2):
        for q in plane_peers:
            gone(edge.at[k, core], pl_s.at[k, q], pl_r.at[k, p], at_plane(q))
        for w in tower:
            gone(picked.at[k, w], zz_s.at[k, w], zz_r.at[k, mine], at_tower(w))
    for w in tower:
        gone(meta.at[mine], me_s.at[w], me_r.at[mine], at_tower(w))
        gone(cote.at[core], cz_s.at[w], cz_r.at[mine], at_tower(w))
    for q in plane_peers:
        gone(tbl.at[q], rt_s.at[q], rt_r.at[p], at_plane(q))
    for i in range(2):
        gone(cg.at[i], c_s.at[i], c_r.at[i], partner())
        gone(ra.at[i, pl.ds(0, AN - 1)], a1_s.at[i], a1_r.at[i], at_b(zz))
        gone(rb.at[i, pl.ds(0, BN - 1)], a2_s.at[i], a2_r.at[i], at_b(zz))
        gone(ra.at[i, pl.ds(0, AN - 1)], a3_s.at[i], a3_r.at[i], at_b(zz))
        gone(cg.at[i], f_s.at[i], f_r.at[i], partner())
    gone(sa.at[pl.ds(0, AN - 1)], s1_s, s1_r, at_a(a))
    gone(sb.at[pl.ds(0, 2 * BN - 1)], s2_s, s2_r, at_b(zz))
    gone(sf.at[pl.ds(0, AN - 1)], s3_s, s3_r, at_a(a))


def copy_kernel(*refs):
    ins, outs, sem = refs[:5], refs[5:10], refs[10]
    copies = [pltpu.make_async_copy(ins[i], outs[i], sem.at[i]) for i in range(5)]
    for copy in copies:
        copy.start()
    for copy in copies:
        copy.wait()


def per_device(
    initial_state, target, features, coupling, in_weight, mid_weight, top_weight, out_weight, biases,
    block_count, connectivity, orientation, rotation,
):
    cells = lax.axis_size("op") * lax.axis_size("blk") * NS * BI * BJ
    loss_scale = 2.0 / math.sqrt(cells)
    vmem = pl.BlockSpec(memory_space=pltpu.VMEM)
    smem = pl.BlockSpec(memory_space=pltpu.SMEM)
    anywhere = pl.BlockSpec(memory_space=pl.ANY)
    dma = pltpu.SemaphoreType.DMA
    field = pltpu.VMEM((NV, NS, BI, BJ), f32)
    outs = pl.pallas_call(
        functools.partial(kernel, loss_scale),
        out_shape=(
            jax.ShapeDtypeStruct((NV, NS, BI, BJ), f32),
            jax.ShapeDtypeStruct((NF, HID), f32),
            jax.ShapeDtypeStruct((HID, HID), f32),
            jax.ShapeDtypeStruct((HID, HID), f32),
            jax.ShapeDtypeStruct((4, HID), f32),
        ),
        in_specs=[anywhere, anywhere, anywhere, smem, vmem, vmem, vmem, vmem, vmem, smem, smem, smem, smem],
        out_specs=(vmem,) * 5,
        scratch_shapes=[
            field, field, pltpu.VMEM((NF, NS, BI, BJ), bf16),
            pltpu.VMEM((NCH // 2, NF, CW), bf16),
            pltpu.VMEM((NCH // 2, NF, CW), bf16),
            pltpu.VMEM((NCH // 2, HID, CW), bf16),
            pltpu.VMEM((NCH // 2, HID, CW), bf16),
            pltpu.VMEM((NCH // 2, HID, CW), bf16),
            pltpu.VMEM((NCH // 2, HID, CW), bf16),
            pltpu.VMEM((NCH // 2, HID, CW), bf16),
            pltpu.VMEM((NCH // 2, HID, CW), bf16),
            pltpu.VMEM((NS, 2, NF * 16, BJ), f32),
            pltpu.VMEM((HID, NF), bf16),
            pltpu.VMEM((HID, HID), bf16),
            pltpu.VMEM((HID, HID), bf16),
            pltpu.VMEM((3, HID, BJ), f32),
            pltpu.VMEM((HID, BJ), f32),
            field, field, field, field,
            pltpu.VMEM((NS * BI, BJ), f32),
            pltpu.VMEM((NS * BI, BJ), f32),
            pltpu.VMEM((NS * BI, BJ), f32),
            pltpu.VMEM((NS * BI, BJ), f32),
            pltpu.VMEM((2, 2, 8, HALF), f32),
            pltpu.VMEM((2, PL, 8, HALF), f32),
            pltpu.VMEM((2, 2 * ZN, 8, HALF), f32),
            pltpu.VMEM((2, 2 * ZN, 8, HALF), f32),
            pltpu.VMEM((2, 8, HALF), f32),
            pltpu.VMEM((4, 8, BJ), f32),
            pltpu.VMEM((2 * ZN, 8, BJ), f32),
            pltpu.VMEM((2 * ZN * 8, PL * 8), bf16),
            pltpu.VMEM((PL * 8, 2 * ZN * 8), bf16),
            pltpu.VMEM((2, NV, 8, BJ), f32),
            pltpu.VMEM((2, 8, HALF), f32),
            pltpu.VMEM((2 * ZN, 8, HALF), f32),
            pltpu.VMEM((PL, 8, HALF), f32),
            pltpu.VMEM((PL, 8, HALF), f32),
            pltpu.VMEM((HID + 16, HID), f32),
            pltpu.VMEM((HID + 16, HID), f32),
            pltpu.VMEM((NF + 16, HID), f32),
            pltpu.VMEM((HID, BJ), f32),
            pltpu.VMEM((2, HID // 2, HID), f32),
            pltpu.VMEM((2, AN, HID // 2 // AN, HID), f32),
            pltpu.VMEM((2, AN, HID // 2 // AN, HID), f32),
            pltpu.VMEM((2, BN, HID // 2 // AN, HID), f32),
            pltpu.VMEM((2, 2, AN, HID // 2 // AN, HID), f32),
            pltpu.VMEM((AN, 2, HID), f32),
            pltpu.VMEM((AN, 2, HID), f32),
            pltpu.VMEM((2 * BN, 2, HID), f32),
            pltpu.VMEM((AN, 2, HID), f32),
            dma((2, PL)), dma((2, PL)), dma((2 * ZN,)), dma((2 * ZN,)), dma((2, 2 * ZN)), dma((2, 2 * ZN)),
            dma((2 * ZN,)), dma((2 * ZN,)), dma((PL,)), dma((PL,)),
            dma((3,)), dma((2,)), dma((2,)), dma((2,)), dma((2,)), dma((2,)), dma((2,)), dma((2,)), dma((2,)), dma((2,)), dma((2,)),
            dma, dma, dma, dma, dma, dma,
        ],
        compiler_params=pltpu.CompilerParams(
            collective_id=0, has_side_effects=True, vmem_limit_bytes=56 * 2**20
        ),
    )(
        initial_state[0], target[0], features[0], coupling, in_weight, mid_weight, top_weight,
        out_weight, biases, block_count, connectivity.T, orientation.T, rotation.T,
    )
    outs = pl.pallas_call(
        copy_kernel,
        out_shape=tuple(jax.ShapeDtypeStruct(x.shape, x.dtype) for x in outs),
        in_specs=[vmem] * 5,
        out_specs=(pl.BlockSpec(memory_space=pl.ANY),) * 5,
        scratch_shapes=[dma((5,))],
    )(*outs)
    return (outs[0][None],) + tuple(outs[1:])


def solution(mesh):
    wide = P("op", None, "blk", None, None)
    return jax.shard_map(
        per_device,
        mesh=mesh,
        in_specs=(wide, wide, wide) + (P(),) * 6 + (P("blk"),) + (P("blk", None),) * 3,
        out_specs=(wide, P(), P(), P(), P()),
        check_vma=False,
    )
```

```python
import functools
import math

import jax
import jax.numpy as jnp
from jax import lax
from jax.experimental import pallas as pl
from jax.experimental.pallas import tpu as pltpu
from jax.sharding import PartitionSpec as P

MESH = pl.DeviceIdType.MESH
tau = 0.2
passage_angle = 2.0 * math.pi / 36.0
cos_step = math.cos(passage_angle)
sin_step = math.sin(passage_angle)
f32 = jnp.float32
bf16 = jnp.bfloat16

NV, NS, BI, BJ, HID, NF = 6, 3, 32, 128, 256, 16
PL = 8
ZN = 4
NCH = 12
CW = 1024
EDGE = NCH - 1
AN = 16
BN = 8
HV = NV // 2
HALF = HV * BJ


def row_of(s, i):
    if i == 0 or i == BI - 1:
        return 8 * EDGE + 2 * s + (i != 0)
    inner = (BI - 2) * s + i - 1
    return inner if inner < 8 * EDGE else inner + 2 * NS


def runs(s):
    whole = (BI - 2) * s
    first = min(BI - 2, 8 * EDGE - whole)
    res = [(1, whole, first)]
    if first < BI - 2:
        res.append((1 + first, row_of(s, 1 + first), BI - 2 - first))
    return res


def nt(a, b):
    return lax.dot_general(a, b, (((1,), (1,)), ((), ())), preferred_element_type=f32)


def mm(a, b):
    return jnp.dot(a, b, preferred_element_type=f32)


def lanes_sum(u, lane):
    left = jnp.where(lane == 0, u, pltpu.roll(u, 1, 1))
    right = jnp.where(lane == BJ - 1, u, pltpu.roll(u, BJ - 1, 1))
    return left + right


def kernel(
    loss_scale,
    state_h, target_h, feat_h, coup, in_w, mid_w, top_w, out_w, biases, count, conn, orient, rot,
    out_h, out_in, out_mid, out_top, out_vec,
    out_state, state, target, feat, x0, x1, first0, first1, second0, second1, third0, third1,
    xs, win_t, wmid_t, wtop_t, bias_c, ow_c,
    mid_r, ts_r, tm_r, fc_r, beta_r, betan_r, bc_r, bcn_r,
    edge, gath, picked, arr, inner, tile_r, meta, sel_r, selt_r, ghost_r,
    cote, cz, tbl, ret,
    gtop, gmid, gin, gout,
    cg, gsum, ra, rb, full, sg, sa, sb, sf,
    pl_s, pl_r, me_s, me_r, zz_s, zz_r, cz_s, cz_r, rt_s, rt_r,
    in_s, c_s, c_r, a1_s, a1_r, a2_s, a2_r, a3_s, a3_r, f_s, f_r, s1_s, s1_r, s2_s, s2_r, s3_s, s3_r,
):
    x_r, first_r, second_r, third_r = (x0, x1), (first0, first1), (second0, second1), (third0, third1)
    b = lax.axis_index("blk")
    o = lax.axis_index("op")
    z = lax.div(b, PL)
    p = lax.rem(b, PL)

    plane_peers = [lax.rem(p + d, PL) for d in range(1, PL)]
    x_at = lax.div(o, 2)
    z_lo = lax.rem(o, 2)
    core = lax.rem(b, 2)
    mine = z * 2 + core
    tower = [lax.rem(mine + d, 2 * ZN) for d in range(1, 2 * ZN)]
    a = x_at * ZN + lax.div(p, 2)
    zz = z * 2 + z_lo

    def at_plane(q):
        return {"blk": z * PL + q}

    def at_tower(w):
        return {"blk": lax.div(w, 2) * PL + p - core + lax.rem(w, 2)}

    def at_a(q):
        return {"blk": z * PL + lax.rem(q, 4) * 2 + core, "op": lax.div(q, 4) * 2 + z_lo}

    def at_zc(w, c):
        return {"blk": lax.div(w, 2) * PL + p - core + c, "op": x_at * 2 + lax.rem(w, 2)}

    def partner():
        return {"blk": b + 1 - 2 * core}

    def at_b(w):
        return {"blk": lax.div(w, 2) * PL + p, "op": x_at * 2 + lax.rem(w, 2)}

    def send(src, dst, s_sem, r_sem, device):
        copy = pltpu.make_async_remote_copy(
            src_ref=src, dst_ref=dst, send_sem=s_sem, recv_sem=r_sem, device_id=device, device_id_type=MESH
        )
        copy.start()

    def got(dst, s_sem, r_sem, device):
        pltpu.make_async_remote_copy(
            src_ref=dst, dst_ref=dst, send_sem=s_sem, recv_sem=r_sem, device_id=device, device_id_type=MESH
        ).wait_recv()

    def gone(src, s_sem, r_sem, device):
        pltpu.make_async_remote_copy(
            src_ref=src, dst_ref=src, send_sem=s_sem, recv_sem=r_sem, device_id=device, device_id_type=MESH
        ).wait_send()

    barrier = pltpu.get_barrier_semaphore()
    def greet(device):
        pl.semaphore_signal(barrier, inc=1, device_id=device, device_id_type=MESH)

    for q in plane_peers:
        greet(at_plane(q))
    for d in range(4, AN):
        greet(at_a(lax.rem(x_at * 4 + d, AN)))
    for d in range(1, BN):
        for c in range(2):
            greet(at_zc(lax.rem(zz + d, BN), c))

    loads = [pltpu.make_async_copy(h, v, in_s.at[i]) for i, (h, v) in enumerate(((state_h, state), (feat_h, feat), (target_h, target)))]
    for load in loads:
        load.start()

    rowi = lax.broadcasted_iota(jnp.int32, (8, BJ), 0)
    lane8 = lax.broadcasted_iota(jnp.int32, (8, BJ), 1)
    meta_t = jnp.full((8, BJ), -1.0, f32)
    flip_t = jnp.zeros((8, BJ), f32)
    cos_t = jnp.ones((8, BJ), f32)
    sin_t = jnp.zeros((8, BJ), f32)
    live_t = jnp.zeros((8, BJ), f32)
    live = []
    for s in range(NS):
        live.append(jnp.where(s < count[0], 1.0, 0.0).astype(f32))
        for e in range(2):
            here = rowi == 2 * s + e
            idx = conn[e, s]
            idx = idx + 2 * ((idx * 10923) >> 16)
            meta_t = jnp.where(here, idx.astype(f32), meta_t)
            flip_t = jnp.where(here, orient[e, s].astype(f32), flip_t)
            turn = rot[e, s]
            cos_t = jnp.where(here, jnp.where(turn == 0, 1.0, cos_step).astype(f32), cos_t)
            sin_t = jnp.where(here, turn.astype(f32) * sin_step, sin_t)
            live_t = jnp.where(here, live[s], live_t)
    meta[mine] = meta_t
    tile_r[0] = flip_t
    tile_r[1] = cos_t
    tile_r[2] = sin_t
    tile_r[3] = live_t

    def part(ref, v):
        return ref.at[v // HV, :, v % HV * BJ:(v % HV + 1) * BJ]

    def pack(dst, field, rows):
        dst[...] = jnp.zeros((2, 8, HALF), f32)
        for v in range(NV):
            for s in range(NS):
                for e in range(2):
                    part(dst, v)[2 * s + e:2 * s + e + 1, :] = field[v, s, rows[e]:rows[e] + 1, :]

    def cut(ref):
        return [part(ref, v)[...] for v in range(NV)]

    def thirds(u):
        u1 = u.astype(bf16)
        u2 = (u - u1.astype(f32)).astype(bf16)
        u3 = (u - u1.astype(f32) - u2.astype(f32)).astype(bf16)
        return u1, u2, u3

    def by_rows(mask, u):
        r = mm(mask, jnp.concatenate(thirds(u), axis=1))
        return r[:, :HALF] + r[:, HALF:2 * HALF] + r[:, 2 * HALF:]

    loads[0].wait()
    pack(edge.at[0], state, (0, BI - 1))

    pl.semaphore_wait(barrier, PL - 1 + AN - 4 + 2 * (BN - 1))

    def send_plane(k):
        for q in plane_peers:
            send(edge.at[k, lax.rem(q, 2)], gath.at[k, p], pl_s.at[k, q], pl_r.at[k, p], at_plane(q))
        gath[k, p] = edge[k, core]

    for w in tower:
        send(meta.at[mine], meta.at[mine], me_s.at[w], me_r.at[mine], at_tower(w))
    send_plane(0)

    def pick(k):
        for q in plane_peers:
            got(gath.at[k, q], pl_s.at[k, q], pl_r.at[k, q], at_plane(q))
        chosen = by_rows(sel_r[...], gath[k].reshape(PL * 8, HALF))
        picked[k] = chosen.reshape(2 * ZN, 8, HALF)
        arr[k, mine] = picked[k, mine]
        for w in tower:
            send(picked.at[k, w], arr.at[k, mine], zz_s.at[k, w], zz_r.at[k, mine], at_tower(w))

    def make_sel():
        for w in tower:
            got(meta.at[w], me_s.at[w], me_r.at[w], at_tower(w))
        n = 2 * ZN * 8
        lane = lax.broadcasted_iota(jnp.int32, (n, BJ), 1)
        named = meta[...].reshape(n, BJ)
        local = named - (z * (PL * 8)).astype(f32)
        sel = jnp.where((local == lane.astype(f32)) & (lane < PL * 8), 1.0, 0.0).astype(f32)
        sel_r[...] = sel[:, :PL * 8].astype(bf16)
        wide = jnp.concatenate([sel, jnp.zeros((BJ - n, BJ), f32)], axis=0).T
        selt_r[...] = wide[:PL * 8, :n].astype(bf16)

    def turned(parts, sign):
        flip, cos, sin = tile_r[0], tile_r[1], tile_r[2] * sign
        r = lax.broadcasted_iota(jnp.int32, (BJ, BJ), 0)
        c = lax.broadcasted_iota(jnp.int32, (BJ, BJ), 1)
        anti = jnp.where(r + c == BJ - 1, 1.0, 0.0).astype(bf16)
        n = 8 * NV
        back = mm(jnp.concatenate(thirds(jnp.concatenate(parts, axis=0)), axis=0), anti)
        back = back[:n] + back[n:2 * n] + back[2 * n:]
        out = [jnp.where(flip > 0.5, back[8 * v:8 * v + 8], parts[v]) for v in range(NV)]
        c2 = cos * out[2] - sin * out[3]
        c3 = sin * out[2] + cos * out[3]
        return [out[0], out[1], c2, c3, out[4], out[5]]

    def ghosts(k):
        for w in tower:
            got(arr.at[k, w], zz_s.at[k, w], zz_r.at[k, w], at_tower(w))
        total = [(arr[k, h] + arr[k, 2 + h]) + (arr[k, 4 + h] + arr[k, 6 + h]) for h in range(2)]
        parts = turned([total[v // HV][:, v % HV * BJ:(v % HV + 1) * BJ] for v in range(NV)], 1.0)
        for v in range(NV):
            ghost_r[k, v] = parts[v]

    def edge_sweep(e, n, gh):
        res = []
        beta_e = jnp.where(rowi < 2 * NS, beta_r[8 * EDGE:8 * EDGE + 8, :], 0.0)
        for v in range(NV):
            lap = gh[v] + n[v] + lanes_sum(e[v], lane8) - 4.0 * e[v]
            coupled = coup[v, 0] * e[0]
            for w in range(1, NV):
                coupled = coupled + coup[v, w] * e[w]
            res.append(e[v] + tau * (lap - coupled + beta_e * jnp.tanh(e[v])))
        return res

    pad = jnp.zeros((BJ - NF, HID), f32)
    win_t[...] = jnp.concatenate([in_w[...].astype(f32), pad], axis=0).T[:, :NF].astype(bf16)
    wmid_t[...] = mid_w[...].astype(f32).T.astype(bf16)
    wtop_t[...] = top_w[...].astype(f32).T.astype(bf16)
    for k in range(3):
        bias_c[k] = jnp.broadcast_to(biases[k:k + 1, :], (BJ, HID)).T
    ow_c[...] = jnp.broadcast_to(out_w[...].astype(f32).reshape(1, HID), (BJ, HID)).T

    loads[1].wait()
    for s in range(NS):
        for h in range(2):
            xs[s, h] = feat[:, s, 16 * h:16 * h + 16, :].astype(f32).reshape(NF * 16, BJ)
    for s in range(NS):
        for h in range(2):
            for r in range(16):
                row = row_of(s, 16 * h + r)
                x_r[row // 8 % 2][row // 16, :, (row % 8) * BJ:(row % 8 + 1) * BJ] = xs[s, h, pl.ds(r, NF, stride=16), :].astype(bf16)

    SUB = 512

    weights = (win_t, wmid_t, wtop_t)
    acts = (x_r, first_r, second_r, third_r)
    SUBS = 2 * CW // SUB

    def forward(k, carry):
        pair = (lax.rem(k + EDGE // 2, NCH // 2), k)

        def place(j):
            half = j // (CW // SUB)
            return 1 - half, pair[half], slice((j % (CW // SUB)) * SUB, (j % (CW // SUB) + 1) * SUB)

        def product(layer, j):
            par, c, cols = place(j)
            return mm(weights[layer][...], acts[layer][par][c, :, cols])

        tiles = [jnp.zeros((8, BJ), f32), jnp.zeros((8, BJ), f32)]

        def activate(layer, j, d):
            par, c, cols = place(j)
            bias = bias_c[layer]
            for i in range(SUB // BJ):
                t = jnp.tanh(d[:, i * BJ:(i + 1) * BJ] + bias).astype(bf16)
                acts[layer + 1][par][c, :, cols.start + i * BJ:cols.start + (i + 1) * BJ] = t
                if layer == 2:
                    bt = jnp.sum(ow_c[...] * t.astype(f32), axis=0, keepdims=True) + 1.0
                    row = (j % (CW // SUB)) * (SUB // BJ) + i
                    half = j // (CW // SUB)
                    tiles[half] = jnp.where(rowi == row, bt, tiles[half])

        tasks = [(layer, j) for layer in range(3) for j in range(SUBS)]
        held = None
        for task in tasks:
            d = product(*task)
            if held is not None:
                activate(*held)
            held = task + (d,)
        activate(*held)
        for half in range(2):
            beta_r[pl.ds(pl.multiple_of((2 * pair[half] + 1 - half) * 8, 8), 8), :] = tiles[half]

        @pl.when(k == 0)
        def _():
            make_sel()
            pick(0)

        @pl.when(k == 2)
        def _():
            ghosts(0)
            pack(inner, state, (1, BI - 2))
            res = edge_sweep(cut(edge.at[0]), cut(inner), [ghost_r[0, v] for v in range(NV)])
            for v in range(NV):
                part(edge.at[1], v)[...] = res[v]
            send_plane(1)

        @pl.when(k == 4)
        def _():
            pick(1)

        return carry

    lax.fori_loop(0, NCH // 2, forward, 0)

    for s in range(NS):
        for e in range(2):
            g = 8 * EDGE + 2 * s + e
            row = s * BI + e * (BI - 1)
            betan_r[row:row + 1, :] = beta_r[g:g + 1, :]
        for first, place, length in runs(s):
            betan_r[s * BI + first:s * BI + first + length, :] = beta_r[place:place + length, :]

    rows32 = lax.broadcasted_iota(jnp.int32, (BI, BJ), 0)
    lane32 = lax.broadcasted_iota(jnp.int32, (BI, BJ), 1)

    def stencil(u, low, high):
        up = jnp.where(rows32 == 0, low, pltpu.roll(u, 1, 0))
        down = jnp.where(rows32 == BI - 1, high, pltpu.roll(u, BI - 1, 0))
        return up + down + lanes_sum(u, lane32) - 4.0 * u

    def low_high(k, s, v):
        return ghost_r[k, v, 2 * s:2 * s + 1, :], ghost_r[k, v, 2 * s + 1:2 * s + 2, :]

    for s in range(NS):
        us = [state[v, s] for v in range(NV)]
        beta = betan_r[s * BI:(s + 1) * BI, :]
        for v in range(NV):
            t = jnp.tanh(us[v])
            ts_r[v, s] = t
            low, high = low_high(0, s, v)
            coupled = coup[v, 0] * us[0]
            for w in range(1, NV):
                coupled = coupled + coup[v, w] * us[w]
            mid_r[v, s] = us[v] + tau * (stencil(us[v], low, high) - coupled + beta * t)

    ghosts(1)
    pack(inner, mid_r, (1, BI - 2))
    final_e = edge_sweep(cut(edge.at[1]), cut(inner), [ghost_r[1, v] for v in range(NV)])
    loads[2].wait()
    pack(inner, target, (0, BI - 1))
    goal_e = cut(inner)
    cot_e = [tau * (loss_scale * tile_r[3] * (final_e[v] - goal_e[v])) for v in range(NV)]
    cot_e = turned(cot_e, -1.0)
    for v in range(NV):
        part(cote, v)[...] = cot_e[v]
    cz[mine] = cote[core]
    for w in tower:
        send(cote.at[lax.rem(w, 2)], cz.at[mine], cz_s.at[w], cz_r.at[mine], at_tower(w))

    for s in range(NS):
        us = [mid_r[v, s] for v in range(NV)]
        beta = betan_r[s * BI:(s + 1) * BI, :]
        for v in range(NV):
            t = jnp.tanh(us[v])
            tm_r[v, s] = t
            low, high = low_high(1, s, v)
            coupled = coup[v, 0] * us[0]
            for w in range(1, NV):
                coupled = coupled + coup[v, w] * us[w]
            final = us[v] + tau * (stencil(us[v], low, high) - coupled + beta * t)
            out_state[v, s] = live[s] * final
            fc_r[v, s] = loss_scale * live[s] * (final - target[v, s])

    for s in range(NS):
        gs = [fc_r[v, s] for v in range(NV)]
        beta = betan_r[s * BI:(s + 1) * BI, :]
        acc = jnp.zeros((BI, BJ), f32)
        for v in range(NV):
            t = tm_r[v, s]
            coupled = coup[0, v] * gs[0]
            for w in range(1, NV):
                coupled = coupled + coup[w, v] * gs[w]
            mc = gs[v] + tau * (stencil(gs[v], 0.0, 0.0) - coupled + beta * (1.0 - t * t) * gs[v])
            acc = acc + (gs[v] * t + mc * ts_r[v, s])
        bcn_r[s * BI:(s + 1) * BI, :] = tau * acc
        for first, place, length in runs(s):
            bc_r[place:place + length, :] = bcn_r[s * BI + first:s * BI + first + length, :]

    leave = pltpu.make_async_copy(out_state, out_h, in_s.at[3])
    leave.start()

    def table():
        for w in tower:
            got(cz.at[w], cz_s.at[w], cz_r.at[w], at_tower(w))
        sums = by_rows(selt_r[...], cz[...].reshape(2 * ZN * 8, HALF))
        tbl[...] = sums.reshape(PL, 8, HALF)
        ret[p] = tbl[p]
        for q in plane_peers:
            send(tbl.at[q], ret.at[p], rt_s.at[q], rt_r.at[p], at_plane(q))

    def returned():
        for q in plane_peers:
            got(ret.at[q], rt_s.at[q], rt_r.at[q], at_plane(q))
        extra = jnp.zeros((8, BJ), f32)
        for h in range(2):
            total = (ret[h] + ret[2 + h]) + (ret[4 + h] + ret[6 + h])
            for v in range(HV):
                cols = slice(v * BJ, (v + 1) * BJ)
                extra = extra + total[:, cols] * jnp.tanh(edge[0, h, :, cols])
        for s in range(NS):
            for e in range(2):
                g = 2 * s + e
                row = s * BI + e * (BI - 1)
                bc_r[8 * EDGE + g:8 * EDGE + g + 1, :] = bcn_r[row:row + 1, :] + tau * extra[g:g + 1]

    ones = jnp.ones((16, CW), bf16)
    gout[...] = jnp.zeros((HID, BJ), f32)
    gtop[...] = jnp.zeros((HID + 16, HID), f32)
    gmid[...] = jnp.zeros((HID + 16, HID), f32)
    gin[...] = jnp.zeros((NF + 16, HID), f32)

    def weigh(par, k, acc, left, right, fresh=None):
        part = nt(jnp.concatenate([left[par][k], ones], axis=0), right[par][k])
        if fresh is not None:
            part = jnp.where(fresh, part, 0.0)
        acc[...] = acc[...] + part

    def before(k):
        return lax.rem(k + NCH // 2 - 1, NCH // 2)

    RB = 64

    def top_delta(par, k):
        third = third_r[par]
        bc = bc_r[pl.ds(pl.multiple_of((2 * k + par) * 8, 8), 8), :]
        ch = bc.astype(bf16).astype(f32)
        for i in range(HID // RB):
            rows = slice(i * RB, (i + 1) * RB)
            ow = ow_c[rows]
            acc = gout[rows]
            for j in range(CW // BJ):
                cols = slice(j * BJ, (j + 1) * BJ)
                t = third[k, rows, cols].astype(f32)
                acc = acc + t * ch[j:j + 1]
                third[k, rows, cols] = (ow * bc[j:j + 1] * (1.0 - t * t)).astype(bf16)
            gout[rows] = acc

    def back_top(k, carry):
        weigh(1, before(k), gtop, second_r, third_r, k > 0)
        top_delta(0, k)
        weigh(0, k, gtop, second_r, third_r)
        top_delta(1, k)
        return carry

    def layer_back(k, weight, source, act, acc, left, fresh=None):
        held = None

        def put(par, cols, d):
            for i in range(SUB // BJ):
                here = slice(cols.start + i * BJ, cols.start + (i + 1) * BJ)
                t = act[par][k, :, here].astype(f32)
                act[par][k, :, here] = (d[:, i * BJ:(i + 1) * BJ] * (1.0 - t * t)).astype(bf16)

        for par in range(2):
            for j in range(CW // SUB):
                cols = slice(j * SUB, (j + 1) * SUB)
                d = mm(weight[...], source[par][k, :, cols])
                if held is not None:
                    put(*held)
                held = (par, cols, d)
                if j == 0:
                    if par == 0:
                        weigh(1, before(k), acc, left, act, fresh)
                    else:
                        put(*held)
                        held = None
                        weigh(0, k, acc, left, act)
        put(*held)

    def back_mid(k, carry):
        layer_back(k, top_w, third_r, second_r, gmid, first_r, k > 0)
        return carry

    grads = (gtop, gmid)
    HR = HID // 2
    R = HR // AN

    def hand(i):
        other = pl.ds(pl.multiple_of((1 - core) * HR, HR), HR)
        send(grads[i].at[other], cg.at[i], c_s.at[i], c_r.at[i], partner())

    def ar_1(i):
        got(cg.at[i], c_s.at[i], c_r.at[i], partner())
        half = grads[i][pl.ds(pl.multiple_of(core * HR, HR), HR), :] + cg[i]
        gsum[i] = half.reshape(AN, R, HID)
        for d in range(1, AN):
            q = lax.rem(a + d, AN)
            send(gsum.at[i, q], ra.at[i, a], a1_s.at[i], a1_r.at[i], at_a(q))
        ra[i, a] = gsum[i, a]

    def ar_2(i):
        got(ra.at[i, pl.ds(0, AN - 1)], a1_s.at[i], a1_r.at[i], at_b(zz))
        total = ra[i, 0]
        for q in range(1, AN):
            total = total + ra[i, q]
        rb[i, zz] = total
        for d in range(1, BN):
            send(rb.at[i, zz], rb.at[i, zz], a2_s.at[i], a2_r.at[i], at_b(lax.rem(zz + d, BN)))

    def ar_3(i):
        got(rb.at[i, pl.ds(0, BN - 1)], a2_s.at[i], a2_r.at[i], at_b(zz))
        total = rb[i, 0]
        for w in range(1, BN):
            total = total + rb[i, w]
        full[i, core, a] = total
        for d in range(1, AN):
            send(full.at[i, core, a], full.at[i, core, a], a3_s.at[i], a3_r.at[i], at_a(lax.rem(a + d, AN)))

    def ar_4(i):
        got(full.at[i, core, pl.ds(0, AN - 1)], a3_s.at[i], a3_r.at[i], at_b(zz))
        send(full.at[i, core], full.at[i, core], f_s.at[i], f_r.at[i], partner())

    def ar_5(i, out):
        got(full.at[i, 1 - core], f_s.at[i], f_r.at[i], partner())
        out[...] = full[i].reshape(HID, HID)

    def small_1():
        for r in range(NF):
            sg[r // 2, r % 2:r % 2 + 1] = gin[r:r + 1]
        sg[NF // 2, 0:1] = jnp.sum(gout[...].T, axis=0, keepdims=True)
        sg[NF // 2, 1:2] = gin[NF:NF + 1]
        sg[NF // 2 + 1, 0:1] = gmid[HID:HID + 1]
        sg[NF // 2 + 1, 1:2] = gtop[HID:HID + 1]
        sg[NF // 2 + 2:] = jnp.zeros((AN - NF // 2 - 2, 2, HID), f32)
        for d in range(1, AN):
            q = lax.rem(a + d, AN)
            send(sg.at[q], sa.at[a], s1_s, s1_r, at_a(q))
        sa[a] = sg[a]

    def small_2():
        got(sa.at[pl.ds(0, AN - 1)], s1_s, s1_r, at_a(a))
        total = sa[0]
        for q in range(1, AN):
            total = total + sa[q]
        own = 2 * zz + core
        sb[own] = total
        send(sb.at[own], sb.at[own], s2_s, s2_r, partner())
        for d in range(1, BN):
            for c in range(2):
                send(sb.at[own], sb.at[own], s2_s, s2_r, at_zc(lax.rem(zz + d, BN), c))

    def small_3():
        got(sb.at[pl.ds(0, 2 * BN - 1)], s2_s, s2_r, at_b(zz))
        total = sb[0]
        for w in range(1, 2 * BN):
            total = total + sb[w]
        sf[a] = total
        for d in range(1, AN):
            send(sf.at[a], sf.at[a], s3_s, s3_r, at_a(lax.rem(a + d, AN)))

    def small_4():
        got(sf.at[pl.ds(0, AN - 1)], s3_s, s3_r, at_a(a))
        for r in range(NF):
            out_in[r:r + 1] = sf[r // 2, r % 2:r % 2 + 1]
        for r in range(4):
            out_vec[r:r + 1] = sf[(NF + r) // 2, r % 2:r % 2 + 1]

    LAST = NCH // 2 - 1
    lax.fori_loop(0, LAST, back_top, 0)
    weigh(1, LAST - 1, gtop, second_r, third_r)
    table()
    top_delta(0, LAST)
    weigh(0, LAST, gtop, second_r, third_r)
    lax.fori_loop(0, LAST, back_mid, 0)
    returned()
    top_delta(1, LAST)
    weigh(1, LAST, gtop, second_r, third_r)
    hand(0)
    layer_back(LAST, top_w, third_r, second_r, gmid, first_r)
    weigh(1, LAST, gmid, first_r, second_r)
    hand(1)
    ar_1(0)

    def back_first(k, carry):
        layer_back(k, mid_w, second_r, first_r, gin, x_r, k > 0)

        @pl.when(k == 1)
        def _():
            ar_1(1)

        @pl.when(k == 3)
        def _():
            ar_2(0)

        @pl.when(k == 5)
        def _():
            ar_2(1)

        return carry

    lax.fori_loop(0, LAST + 1, back_first, 0)
    weigh(1, LAST, gin, x_r, first_r)

    small_1()
    ar_3(0)
    ar_3(1)
    small_2()
    ar_4(0)
    ar_4(1)
    small_3()
    ar_5(0, out_top)
    ar_5(1, out_mid)
    small_4()

    leave.wait()
    for k in range(2):
        for q in plane_peers:
            gone(edge.at[k, core], pl_s.at[k, q], pl_r.at[k, p], at_plane(q))
        for w in tower:
            gone(picked.at[k, w], zz_s.at[k, w], zz_r.at[k, mine], at_tower(w))
    for w in tower:
        gone(meta.at[mine], me_s.at[w], me_r.at[mine], at_tower(w))
        gone(cote.at[core], cz_s.at[w], cz_r.at[mine], at_tower(w))
    for q in plane_peers:
        gone(tbl.at[q], rt_s.at[q], rt_r.at[p], at_plane(q))
    for i in range(2):
        gone(cg.at[i], c_s.at[i], c_r.at[i], partner())
        gone(ra.at[i, pl.ds(0, AN - 1)], a1_s.at[i], a1_r.at[i], at_b(zz))
        gone(rb.at[i, pl.ds(0, BN - 1)], a2_s.at[i], a2_r.at[i], at_b(zz))
        gone(ra.at[i, pl.ds(0, AN - 1)], a3_s.at[i], a3_r.at[i], at_b(zz))
        gone(cg.at[i], f_s.at[i], f_r.at[i], partner())
    gone(sa.at[pl.ds(0, AN - 1)], s1_s, s1_r, at_a(a))
    gone(sb.at[pl.ds(0, 2 * BN - 1)], s2_s, s2_r, at_b(zz))
    gone(sf.at[pl.ds(0, AN - 1)], s3_s, s3_r, at_a(a))


def copy_kernel(*refs):
    ins, outs, held, sem = refs[:5], refs[5:10], refs[10:15], refs[15]
    parts = [(0, slice(v, v + 1)) for v in range(NV)] + [(i, slice(None)) for i in range(1, 5)]
    come = [pltpu.make_async_copy(ins[i].at[at], held[i].at[at], sem.at[0, n]) for n, (i, at) in enumerate(parts)]
    go = [pltpu.make_async_copy(held[i].at[at], outs[i].at[at], sem.at[1, n]) for n, (i, at) in enumerate(parts)]
    for copy in come:
        copy.start()
    for first, then in zip(come, go):
        first.wait()
        then.start()
    for copy in go:
        copy.wait()


def per_device(
    initial_state, target, features, coupling, in_weight, mid_weight, top_weight, out_weight, biases,
    block_count, connectivity, orientation, rotation,
):
    cells = lax.axis_size("op") * lax.axis_size("blk") * NS * BI * BJ
    loss_scale = 2.0 / math.sqrt(cells)
    vmem = pl.BlockSpec(memory_space=pltpu.VMEM)
    smem = pl.BlockSpec(memory_space=pltpu.SMEM)
    anywhere = pl.BlockSpec(memory_space=pl.ANY)
    dma = pltpu.SemaphoreType.DMA
    field = pltpu.VMEM((NV, NS, BI, BJ), f32)
    outs = pl.pallas_call(
        functools.partial(kernel, loss_scale),
        out_shape=(
            jax.ShapeDtypeStruct((NV, NS, BI, BJ), f32),
            jax.ShapeDtypeStruct((NF, HID), f32),
            jax.ShapeDtypeStruct((HID, HID), f32),
            jax.ShapeDtypeStruct((HID, HID), f32),
            jax.ShapeDtypeStruct((4, HID), f32),
        ),
        in_specs=[anywhere, anywhere, anywhere, smem, vmem, vmem, vmem, vmem, vmem, smem, smem, smem, smem],
        out_specs=(anywhere, vmem, vmem, vmem, vmem),
        scratch_shapes=[
            field, field, field, pltpu.VMEM((NF, NS, BI, BJ), bf16),
            pltpu.VMEM((NCH // 2, NF, CW), bf16),
            pltpu.VMEM((NCH // 2, NF, CW), bf16),
            pltpu.VMEM((NCH // 2, HID, CW), bf16),
            pltpu.VMEM((NCH // 2, HID, CW), bf16),
            pltpu.VMEM((NCH // 2, HID, CW), bf16),
            pltpu.VMEM((NCH // 2, HID, CW), bf16),
            pltpu.VMEM((NCH // 2, HID, CW), bf16),
            pltpu.VMEM((NCH // 2, HID, CW), bf16),
            pltpu.VMEM((NS, 2, NF * 16, BJ), f32),
            pltpu.VMEM((HID, NF), bf16),
            pltpu.VMEM((HID, HID), bf16),
            pltpu.VMEM((HID, HID), bf16),
            pltpu.VMEM((3, HID, BJ), f32),
            pltpu.VMEM((HID, BJ), f32),
            field, field, field, field,
            pltpu.VMEM((NS * BI, BJ), f32),
            pltpu.VMEM((NS * BI, BJ), f32),
            pltpu.VMEM((NS * BI, BJ), f32),
            pltpu.VMEM((NS * BI, BJ), f32),
            pltpu.VMEM((2, 2, 8, HALF), f32),
            pltpu.VMEM((2, PL, 8, HALF), f32),
            pltpu.VMEM((2, 2 * ZN, 8, HALF), f32),
            pltpu.VMEM((2, 2 * ZN, 8, HALF), f32),
            pltpu.VMEM((2, 8, HALF), f32),
            pltpu.VMEM((4, 8, BJ), f32),
            pltpu.VMEM((2 * ZN, 8, BJ), f32),
            pltpu.VMEM((2 * ZN * 8, PL * 8), bf16),
            pltpu.VMEM((PL * 8, 2 * ZN * 8), bf16),
            pltpu.VMEM((2, NV, 8, BJ), f32),
            pltpu.VMEM((2, 8, HALF), f32),
            pltpu.VMEM((2 * ZN, 8, HALF), f32),
            pltpu.VMEM((PL, 8, HALF), f32),
            pltpu.VMEM((PL, 8, HALF), f32),
            pltpu.VMEM((HID + 16, HID), f32),
            pltpu.VMEM((HID + 16, HID), f32),
            pltpu.VMEM((NF + 16, HID), f32),
            pltpu.VMEM((HID, BJ), f32),
            pltpu.VMEM((2, HID // 2, HID), f32),
            pltpu.VMEM((2, AN, HID // 2 // AN, HID), f32),
            pltpu.VMEM((2, AN, HID // 2 // AN, HID), f32),
            pltpu.VMEM((2, BN, HID // 2 // AN, HID), f32),
            pltpu.VMEM((2, 2, AN, HID // 2 // AN, HID), f32),
            pltpu.VMEM((AN, 2, HID), f32),
            pltpu.VMEM((AN, 2, HID), f32),
            pltpu.VMEM((2 * BN, 2, HID), f32),
            pltpu.VMEM((AN, 2, HID), f32),
            dma((2, PL)), dma((2, PL)), dma((2 * ZN,)), dma((2 * ZN,)), dma((2, 2 * ZN)), dma((2, 2 * ZN)),
            dma((2 * ZN,)), dma((2 * ZN,)), dma((PL,)), dma((PL,)),
            dma((4,)), dma((2,)), dma((2,)), dma((2,)), dma((2,)), dma((2,)), dma((2,)), dma((2,)), dma((2,)), dma((2,)), dma((2,)),
            dma, dma, dma, dma, dma, dma,
        ],
        compiler_params=pltpu.CompilerParams(
            collective_id=0, has_side_effects=True, vmem_limit_bytes=56 * 2**20
        ),
    )(
        initial_state[0], target[0], features[0], coupling, in_weight, mid_weight, top_weight,
        out_weight, biases, block_count, connectivity.T, orientation.T, rotation.T,
    )
    outs = pl.pallas_call(
        copy_kernel,
        out_shape=tuple(jax.ShapeDtypeStruct(x.shape, x.dtype) for x in outs),
        in_specs=[anywhere] * 5,
        out_specs=(anywhere,) * 5,
        scratch_shapes=[pltpu.VMEM(x.shape, x.dtype) for x in outs] + [dma((2, NV + 4))],
    )(*outs)
    return (outs[0][None],) + tuple(outs[1:])


def solution(mesh):
    wide = P("op", None, "blk", None, None)
    return jax.shard_map(
        per_device,
        mesh=mesh,
        in_specs=(wide, wide, wide) + (P(),) * 6 + (P("blk"),) + (P("blk", None),) * 3,
        out_specs=(wide, P(), P(), P(), P()),
        check_vma=False,
    )
```

```python
import functools
import math

import jax
import jax.numpy as jnp
from jax import lax
from jax.experimental import pallas as pl
from jax.experimental.pallas import tpu as pltpu
from jax.sharding import PartitionSpec as P

MESH = pl.DeviceIdType.MESH
tau = 0.2
passage_angle = 2.0 * math.pi / 36.0
cos_step = math.cos(passage_angle)
sin_step = math.sin(passage_angle)
f32 = jnp.float32
bf16 = jnp.bfloat16

NV, NS, BI, BJ, HID, NF = 6, 3, 32, 128, 256, 16
PL = 8
ZN = 4
NCH = 12
CW = 1024
EDGE = NCH - 1
AN = 16
BN = 8
HV = NV // 2
HALF = HV * BJ


def row_of(s, i):
    if i == 0 or i == BI - 1:
        return 8 * EDGE + 2 * s + (i != 0)
    inner = (BI - 2) * s + i - 1
    return inner if inner < 8 * EDGE else inner + 2 * NS


def runs(s):
    whole = (BI - 2) * s
    first = min(BI - 2, 8 * EDGE - whole)
    res = [(1, whole, first)]
    if first < BI - 2:
        res.append((1 + first, row_of(s, 1 + first), BI - 2 - first))
    return res


def nt(a, b):
    return lax.dot_general(a, b, (((1,), (1,)), ((), ())), preferred_element_type=f32)


def mm(a, b):
    return jnp.dot(a, b, preferred_element_type=f32)


def lanes_sum(u, lane):
    left = jnp.where(lane == 0, u, pltpu.roll(u, 1, 1))
    right = jnp.where(lane == BJ - 1, u, pltpu.roll(u, BJ - 1, 1))
    return left + right


def kernel(
    loss_scale,
    state_h, target_h, feat_h, coup, in_w, mid_w, top_w, out_w, biases, count, conn, orient, rot,
    out_h, out_in, out_mid, out_top, out_vec,
    out_state, state, target, feat, x0, x1, first0, first1, second0, second1, third0, third1,
    xs, win_t, wmid_t, wtop_t, bias_c, ow_c,
    mid_r, ts_r, tm_r, fc_r, beta_r, betan_r, bc_r, bcn_r,
    edge, gath, picked, arr, inner, tile_r, meta, sel_r, selt_r, ghost_r,
    cote, cz, tbl, ret,
    gtop, gmid, gin, gout,
    cg, gsum, ra, rb, full, sg, sa, sb, sf,
    pl_s, pl_r, me_s, me_r, zz_s, zz_r, cz_s, cz_r, rt_s, rt_r,
    in_s, c_s, c_r, a1_s, a1_r, a2_s, a2_r, a3_s, a3_r, f_s, f_r, s1_s, s1_r, s2_s, s2_r, s3_s, s3_r,
):
    x_r, first_r, second_r, third_r = (x0, x1), (first0, first1), (second0, second1), (third0, third1)
    b = lax.axis_index("blk")
    o = lax.axis_index("op")
    z = lax.div(b, PL)
    p = lax.rem(b, PL)

    plane_peers = [lax.rem(p + d, PL) for d in range(1, PL)]
    x_at = lax.div(o, 2)
    z_lo = lax.rem(o, 2)
    core = lax.rem(b, 2)
    mine = z * 2 + core
    tower = [lax.rem(mine + d, 2 * ZN) for d in range(1, 2 * ZN)]
    a = x_at * ZN + lax.div(p, 2)
    zz = z * 2 + z_lo

    def at_plane(q):
        return {"blk": z * PL + q}

    def at_tower(w):
        return {"blk": lax.div(w, 2) * PL + p - core + lax.rem(w, 2)}

    def at_a(q):
        return {"blk": z * PL + lax.rem(q, 4) * 2 + core, "op": lax.div(q, 4) * 2 + z_lo}

    def at_zc(w, c):
        return {"blk": lax.div(w, 2) * PL + p - core + c, "op": x_at * 2 + lax.rem(w, 2)}

    def partner():
        return {"blk": b + 1 - 2 * core}

    def at_b(w):
        return {"blk": lax.div(w, 2) * PL + p, "op": x_at * 2 + lax.rem(w, 2)}

    def send(src, dst, s_sem, r_sem, device):
        copy = pltpu.make_async_remote_copy(
            src_ref=src, dst_ref=dst, send_sem=s_sem, recv_sem=r_sem, device_id=device, device_id_type=MESH
        )
        copy.start()

    def got(dst, s_sem, r_sem, device):
        pltpu.make_async_remote_copy(
            src_ref=dst, dst_ref=dst, send_sem=s_sem, recv_sem=r_sem, device_id=device, device_id_type=MESH
        ).wait_recv()

    def gone(src, s_sem, r_sem, device):
        pltpu.make_async_remote_copy(
            src_ref=src, dst_ref=src, send_sem=s_sem, recv_sem=r_sem, device_id=device, device_id_type=MESH
        ).wait_send()

    barrier = pltpu.get_barrier_semaphore()
    def greet(device):
        pl.semaphore_signal(barrier, inc=1, device_id=device, device_id_type=MESH)

    for q in plane_peers:
        greet(at_plane(q))
    for d in range(4, AN):
        greet(at_a(lax.rem(x_at * 4 + d, AN)))
    for d in range(1, BN):
        for c in range(2):
            greet(at_zc(lax.rem(zz + d, BN), c))

    loads = [pltpu.make_async_copy(h, v, in_s.at[i]) for i, (h, v) in enumerate(((state_h, state), (feat_h, feat), (target_h, target)))]
    for load in loads:
        load.start()

    rowi = lax.broadcasted_iota(jnp.int32, (8, BJ), 0)
    lane8 = lax.broadcasted_iota(jnp.int32, (8, BJ), 1)
    meta_t = jnp.full((8, BJ), -1.0, f32)
    flip_t = jnp.zeros((8, BJ), f32)
    cos_t = jnp.ones((8, BJ), f32)
    sin_t = jnp.zeros((8, BJ), f32)
    live_t = jnp.zeros((8, BJ), f32)
    live = []
    for s in range(NS):
        live.append(jnp.where(s < count[0], 1.0, 0.0).astype(f32))
        for e in range(2):
            here = rowi == 2 * s + e
            idx = conn[e, s]
            idx = idx + 2 * ((idx * 10923) >> 16)
            meta_t = jnp.where(here, idx.astype(f32), meta_t)
            flip_t = jnp.where(here, orient[e, s].astype(f32), flip_t)
            turn = rot[e, s]
            cos_t = jnp.where(here, jnp.where(turn == 0, 1.0, cos_step).astype(f32), cos_t)
            sin_t = jnp.where(here, turn.astype(f32) * sin_step, sin_t)
            live_t = jnp.where(here, live[s], live_t)
    meta[mine] = meta_t
    tile_r[0] = flip_t
    tile_r[1] = cos_t
    tile_r[2] = sin_t
    tile_r[3] = live_t

    def part(ref, v):
        return ref.at[v // HV, :, v % HV * BJ:(v % HV + 1) * BJ]

    def pack(dst, field, rows):
        dst[...] = jnp.zeros((2, 8, HALF), f32)
        for v in range(NV):
            for s in range(NS):
                for e in range(2):
                    part(dst, v)[2 * s + e:2 * s + e + 1, :] = field[v, s, rows[e]:rows[e] + 1, :]

    def cut(ref):
        return [part(ref, v)[...] for v in range(NV)]

    def thirds(u):
        u1 = u.astype(bf16)
        u2 = (u - u1.astype(f32)).astype(bf16)
        u3 = (u - u1.astype(f32) - u2.astype(f32)).astype(bf16)
        return u1, u2, u3

    def by_rows(mask, u):
        r = mm(mask, jnp.concatenate(thirds(u), axis=1))
        return r[:, :HALF] + r[:, HALF:2 * HALF] + r[:, 2 * HALF:]

    loads[0].wait()
    pack(edge.at[0], state, (0, BI - 1))

    pl.semaphore_wait(barrier, PL - 1 + AN - 4 + 2 * (BN - 1))

    def send_plane(k):
        for q in plane_peers:
            send(edge.at[k, lax.rem(q, 2)], gath.at[k, p], pl_s.at[k, q], pl_r.at[k, p], at_plane(q))
        gath[k, p] = edge[k, core]

    for w in tower:
        send(meta.at[mine], meta.at[mine], me_s.at[w], me_r.at[mine], at_tower(w))
    send_plane(0)

    def pick(k):
        for q in plane_peers:
            got(gath.at[k, q], pl_s.at[k, q], pl_r.at[k, q], at_plane(q))
        chosen = by_rows(sel_r[...], gath[k].reshape(PL * 8, HALF))
        picked[k] = chosen.reshape(2 * ZN, 8, HALF)
        arr[k, mine] = picked[k, mine]
        for w in tower:
            send(picked.at[k, w], arr.at[k, mine], zz_s.at[k, w], zz_r.at[k, mine], at_tower(w))

    def make_sel():
        for w in tower:
            got(meta.at[w], me_s.at[w], me_r.at[w], at_tower(w))
        n = 2 * ZN * 8
        lane = lax.broadcasted_iota(jnp.int32, (n, BJ), 1)
        named = meta[...].reshape(n, BJ)
        local = named - (z * (PL * 8)).astype(f32)
        sel = jnp.where((local == lane.astype(f32)) & (lane < PL * 8), 1.0, 0.0).astype(f32)
        sel_r[...] = sel[:, :PL * 8].astype(bf16)
        wide = jnp.concatenate([sel, jnp.zeros((BJ - n, BJ), f32)], axis=0).T
        selt_r[...] = wide[:PL * 8, :n].astype(bf16)

    def turned(parts, sign):
        flip, cos, sin = tile_r[0], tile_r[1], tile_r[2] * sign
        r = lax.broadcasted_iota(jnp.int32, (BJ, BJ), 0)
        c = lax.broadcasted_iota(jnp.int32, (BJ, BJ), 1)
        anti = jnp.where(r + c == BJ - 1, 1.0, 0.0).astype(bf16)
        n = 8 * NV
        back = mm(jnp.concatenate(thirds(jnp.concatenate(parts, axis=0)), axis=0), anti)
        back = back[:n] + back[n:2 * n] + back[2 * n:]
        out = [jnp.where(flip > 0.5, back[8 * v:8 * v + 8], parts[v]) for v in range(NV)]
        c2 = cos * out[2] - sin * out[3]
        c3 = sin * out[2] + cos * out[3]
        return [out[0], out[1], c2, c3, out[4], out[5]]

    def ghosts(k):
        for w in tower:
            got(arr.at[k, w], zz_s.at[k, w], zz_r.at[k, w], at_tower(w))
        total = [(arr[k, h] + arr[k, 2 + h]) + (arr[k, 4 + h] + arr[k, 6 + h]) for h in range(2)]
        parts = turned([total[v // HV][:, v % HV * BJ:(v % HV + 1) * BJ] for v in range(NV)], 1.0)
        for v in range(NV):
            ghost_r[k, v] = parts[v]

    def edge_sweep(e, n, gh):
        res = []
        beta_e = jnp.where(rowi < 2 * NS, beta_r[8 * EDGE:8 * EDGE + 8, :], 0.0)
        for v in range(NV):
            lap = gh[v] + n[v] + lanes_sum(e[v], lane8) - 4.0 * e[v]
            coupled = coup[v, 0] * e[0]
            for w in range(1, NV):
                coupled = coupled + coup[v, w] * e[w]
            res.append(e[v] + tau * (lap - coupled + beta_e * jnp.tanh(e[v])))
        return res

    pad = jnp.zeros((BJ - NF, HID), f32)
    win_t[...] = jnp.concatenate([in_w[...].astype(f32), pad], axis=0).T[:, :NF].astype(bf16)
    wmid_t[...] = mid_w[...].astype(f32).T.astype(bf16)
    wtop_t[...] = top_w[...].astype(f32).T.astype(bf16)
    for k in range(3):
        bias_c[k] = jnp.broadcast_to(biases[k:k + 1, :], (BJ, HID)).T
    ow_c[...] = jnp.broadcast_to(out_w[...].astype(f32).reshape(1, HID), (BJ, HID)).T

    loads[1].wait()
    for s in range(NS):
        for h in range(2):
            xs[s, h] = feat[:, s, 16 * h:16 * h + 16, :].astype(f32).reshape(NF * 16, BJ)
    for s in range(NS):
        for h in range(2):
            for r in range(16):
                row = row_of(s, 16 * h + r)
                x_r[row // 8 % 2][row // 16, :, (row % 8) * BJ:(row % 8 + 1) * BJ] = xs[s, h, pl.ds(r, NF, stride=16), :].astype(bf16)

    SUB = 512

    weights = (win_t, wmid_t, wtop_t)
    acts = (x_r, first_r, second_r, third_r)
    SUBS = 2 * CW // SUB

    def forward(k, carry):
        pair = (lax.rem(k + EDGE // 2, NCH // 2), k)

        def place(j):
            half = j // (CW // SUB)
            return 1 - half, pair[half], slice((j % (CW // SUB)) * SUB, (j % (CW // SUB) + 1) * SUB)

        def product(layer, j):
            par, c, cols = place(j)
            return mm(weights[layer][...], acts[layer][par][c, :, cols])

        tiles = [jnp.zeros((8, BJ), f32), jnp.zeros((8, BJ), f32)]

        def activate(layer, j, d):
            par, c, cols = place(j)
            bias = bias_c[layer]
            for i in range(SUB // BJ):
                t = jnp.tanh(d[:, i * BJ:(i + 1) * BJ] + bias).astype(bf16)
                acts[layer + 1][par][c, :, cols.start + i * BJ:cols.start + (i + 1) * BJ] = t
                if layer == 2:
                    bt = jnp.sum(ow_c[...] * t.astype(f32), axis=0, keepdims=True) + 1.0
                    row = (j % (CW // SUB)) * (SUB // BJ) + i
                    half = j // (CW // SUB)
                    tiles[half] = jnp.where(rowi == row, bt, tiles[half])

        tasks = [(layer, j) for layer in range(3) for j in range(SUBS)]
        held = None
        for task in tasks:
            d = product(*task)
            if held is not None:
                activate(*held)
            held = task + (d,)
        activate(*held)
        for half in range(2):
            beta_r[pl.ds(pl.multiple_of((2 * pair[half] + 1 - half) * 8, 8), 8), :] = tiles[half]

        @pl.when(k == 0)
        def _():
            make_sel()
            pick(0)

        @pl.when(k == 2)
        def _():
            ghosts(0)
            pack(inner, state, (1, BI - 2))
            res = edge_sweep(cut(edge.at[0]), cut(inner), [ghost_r[0, v] for v in range(NV)])
            for v in range(NV):
                part(edge.at[1], v)[...] = res[v]
            send_plane(1)

        @pl.when(k == 4)
        def _():
            pick(1)

        return carry

    lax.fori_loop(0, NCH // 2, forward, 0)

    for s in range(NS):
        for e in range(2):
            g = 8 * EDGE + 2 * s + e
            row = s * BI + e * (BI - 1)
            betan_r[row:row + 1, :] = beta_r[g:g + 1, :]
        for first, place, length in runs(s):
            betan_r[s * BI + first:s * BI + first + length, :] = beta_r[place:place + length, :]

    rows32 = lax.broadcasted_iota(jnp.int32, (BI, BJ), 0)
    lane32 = lax.broadcasted_iota(jnp.int32, (BI, BJ), 1)

    def stencil(u, low, high):
        up = jnp.where(rows32 == 0, low, pltpu.roll(u, 1, 0))
        down = jnp.where(rows32 == BI - 1, high, pltpu.roll(u, BI - 1, 0))
        return up + down + lanes_sum(u, lane32) - 4.0 * u

    def low_high(k, s, v):
        return ghost_r[k, v, pl.ds(2 * s, 1), :], ghost_r[k, v, pl.ds(2 * s + 1, 1), :]

    def rows_of(s):
        return pl.ds(pl.multiple_of(s * BI, BI), BI)

    def first_sweep(s, carry):
        us = [state[v, s] for v in range(NV)]
        beta = betan_r[rows_of(s), :]
        for v in range(NV):
            t = jnp.tanh(us[v])
            ts_r[v, s] = t
            low, high = low_high(0, s, v)
            coupled = coup[v, 0] * us[0]
            for w in range(1, NV):
                coupled = coupled + coup[v, w] * us[w]
            mid_r[v, s] = us[v] + tau * (stencil(us[v], low, high) - coupled + beta * t)
        return carry

    lax.fori_loop(0, NS, first_sweep, 0)

    ghosts(1)
    pack(inner, mid_r, (1, BI - 2))
    final_e = edge_sweep(cut(edge.at[1]), cut(inner), [ghost_r[1, v] for v in range(NV)])
    loads[2].wait()
    pack(inner, target, (0, BI - 1))
    goal_e = cut(inner)
    cot_e = [tau * (loss_scale * tile_r[3] * (final_e[v] - goal_e[v])) for v in range(NV)]
    cot_e = turned(cot_e, -1.0)
    for v in range(NV):
        part(cote, v)[...] = cot_e[v]
    cz[mine] = cote[core]
    for w in tower:
        send(cote.at[lax.rem(w, 2)], cz.at[mine], cz_s.at[w], cz_r.at[mine], at_tower(w))

    def second_sweep(s, carry):
        alive = jnp.where(s < count[0], 1.0, 0.0).astype(f32)
        us = [mid_r[v, s] for v in range(NV)]
        beta = betan_r[rows_of(s), :]
        for v in range(NV):
            t = jnp.tanh(us[v])
            tm_r[v, s] = t
            low, high = low_high(1, s, v)
            coupled = coup[v, 0] * us[0]
            for w in range(1, NV):
                coupled = coupled + coup[v, w] * us[w]
            final = us[v] + tau * (stencil(us[v], low, high) - coupled + beta * t)
            out_state[v, s] = alive * final
            fc_r[v, s] = loss_scale * alive * (final - target[v, s])
        return carry

    lax.fori_loop(0, NS, second_sweep, 0)

    def back_sweep(s, carry):
        gs = [fc_r[v, s] for v in range(NV)]
        beta = betan_r[rows_of(s), :]
        acc = jnp.zeros((BI, BJ), f32)
        for v in range(NV):
            t = tm_r[v, s]
            coupled = coup[0, v] * gs[0]
            for w in range(1, NV):
                coupled = coupled + coup[w, v] * gs[w]
            mc = gs[v] + tau * (stencil(gs[v], 0.0, 0.0) - coupled + beta * (1.0 - t * t) * gs[v])
            acc = acc + (gs[v] * t + mc * ts_r[v, s])
        bcn_r[rows_of(s), :] = tau * acc
        return carry

    lax.fori_loop(0, NS, back_sweep, 0)
    for s in range(NS):
        for first, place, length in runs(s):
            bc_r[place:place + length, :] = bcn_r[s * BI + first:s * BI + first + length, :]

    leave = pltpu.make_async_copy(out_state, out_h, in_s.at[3])
    leave.start()

    def table():
        for w in tower:
            got(cz.at[w], cz_s.at[w], cz_r.at[w], at_tower(w))
        sums = by_rows(selt_r[...], cz[...].reshape(2 * ZN * 8, HALF))
        tbl[...] = sums.reshape(PL, 8, HALF)
        ret[p] = tbl[p]
        for q in plane_peers:
            send(tbl.at[q], ret.at[p], rt_s.at[q], rt_r.at[p], at_plane(q))

    def returned():
        for q in plane_peers:
            got(ret.at[q], rt_s.at[q], rt_r.at[q], at_plane(q))
        extra = jnp.zeros((8, BJ), f32)
        for h in range(2):
            total = (ret[h] + ret[2 + h]) + (ret[4 + h] + ret[6 + h])
            for v in range(HV):
                cols = slice(v * BJ, (v + 1) * BJ)
                extra = extra + total[:, cols] * jnp.tanh(edge[0, h, :, cols])
        for s in range(NS):
            for e in range(2):
                g = 2 * s + e
                row = s * BI + e * (BI - 1)
                bc_r[8 * EDGE + g:8 * EDGE + g + 1, :] = bcn_r[row:row + 1, :] + tau * extra[g:g + 1]

    ones = jnp.ones((16, CW), bf16)
    gout[...] = jnp.zeros((HID, BJ), f32)
    gtop[...] = jnp.zeros((HID + 16, HID), f32)
    gmid[...] = jnp.zeros((HID + 16, HID), f32)
    gin[...] = jnp.zeros((NF + 16, HID), f32)

    def weigh(par, k, acc, left, right, fresh=None):
        part = nt(jnp.concatenate([left[par][k], ones], axis=0), right[par][k])
        if fresh is not None:
            part = jnp.where(fresh, part, 0.0)
        acc[...] = acc[...] + part

    def before(k):
        return lax.rem(k + NCH // 2 - 1, NCH // 2)

    RB = 64

    def top_delta(par, k):
        third = third_r[par]
        bc = bc_r[pl.ds(pl.multiple_of((2 * k + par) * 8, 8), 8), :]
        ch = bc.astype(bf16).astype(f32)
        for i in range(HID // RB):
            rows = slice(i * RB, (i + 1) * RB)
            ow = ow_c[rows]
            acc = gout[rows]
            for j in range(CW // BJ):
                cols = slice(j * BJ, (j + 1) * BJ)
                t = third[k, rows, cols].astype(f32)
                acc = acc + t * ch[j:j + 1]
                third[k, rows, cols] = (ow * bc[j:j + 1] * (1.0 - t * t)).astype(bf16)
            gout[rows] = acc

    def back_top(k, carry):
        @pl.when(k == 2)
        def _():
            table()

        @pl.when(k == NCH // 2 - 1)
        def _():
            returned()

        weigh(1, before(k), gtop, second_r, third_r, k > 0)
        top_delta(0, k)
        weigh(0, k, gtop, second_r, third_r)
        top_delta(1, k)
        return carry

    def layer_back(k, weight, source, act, acc, left, fresh=None):
        held = None

        def put(par, cols, d):
            for i in range(SUB // BJ):
                here = slice(cols.start + i * BJ, cols.start + (i + 1) * BJ)
                t = act[par][k, :, here].astype(f32)
                act[par][k, :, here] = (d[:, i * BJ:(i + 1) * BJ] * (1.0 - t * t)).astype(bf16)

        for par in range(2):
            for j in range(CW // SUB):
                cols = slice(j * SUB, (j + 1) * SUB)
                d = mm(weight[...], source[par][k, :, cols])
                if held is not None:
                    put(*held)
                held = (par, cols, d)
                if j == 0:
                    if par == 0:
                        weigh(1, before(k), acc, left, act, fresh)
                    else:
                        put(*held)
                        held = None
                        weigh(0, k, acc, left, act)
        put(*held)

    grads = (gtop, gmid)
    HR = HID // 2
    R = HR // AN

    def hand(i):
        other = pl.ds(pl.multiple_of((1 - core) * HR, HR), HR)
        send(grads[i].at[other], cg.at[i], c_s.at[i], c_r.at[i], partner())

    def ar_1(i):
        got(cg.at[i], c_s.at[i], c_r.at[i], partner())
        half = grads[i][pl.ds(pl.multiple_of(core * HR, HR), HR), :] + cg[i]
        gsum[i] = half.reshape(AN, R, HID)
        for d in range(1, AN):
            q = lax.rem(a + d, AN)
            send(gsum.at[i, q], ra.at[i, a], a1_s.at[i], a1_r.at[i], at_a(q))
        ra[i, a] = gsum[i, a]

    def ar_2(i):
        got(ra.at[i, pl.ds(0, AN - 1)], a1_s.at[i], a1_r.at[i], at_b(zz))
        total = ra[i, 0]
        for q in range(1, AN):
            total = total + ra[i, q]
        rb[i, zz] = total
        for d in range(1, BN):
            send(rb.at[i, zz], rb.at[i, zz], a2_s.at[i], a2_r.at[i], at_b(lax.rem(zz + d, BN)))

    def ar_3(i):
        got(rb.at[i, pl.ds(0, BN - 1)], a2_s.at[i], a2_r.at[i], at_b(zz))
        total = rb[i, 0]
        for w in range(1, BN):
            total = total + rb[i, w]
        full[i, core, a] = total
        for d in range(1, AN):
            send(full.at[i, core, a], full.at[i, core, a], a3_s.at[i], a3_r.at[i], at_a(lax.rem(a + d, AN)))

    def ar_4(i):
        got(full.at[i, core, pl.ds(0, AN - 1)], a3_s.at[i], a3_r.at[i], at_b(zz))
        send(full.at[i, core], full.at[i, core], f_s.at[i], f_r.at[i], partner())

    def ar_5(i, out):
        got(full.at[i, 1 - core], f_s.at[i], f_r.at[i], partner())
        out[...] = full[i].reshape(HID, HID)

    def small_1():
        for r in range(NF):
            sg[r // 2, r % 2:r % 2 + 1] = gin[r:r + 1]
        sg[NF // 2, 0:1] = jnp.sum(gout[...].T, axis=0, keepdims=True)
        sg[NF // 2, 1:2] = gin[NF:NF + 1]
        sg[NF // 2 + 1, 0:1] = gmid[HID:HID + 1]
        sg[NF // 2 + 1, 1:2] = gtop[HID:HID + 1]
        sg[NF // 2 + 2:] = jnp.zeros((AN - NF // 2 - 2, 2, HID), f32)
        for d in range(1, AN):
            q = lax.rem(a + d, AN)
            send(sg.at[q], sa.at[a], s1_s, s1_r, at_a(q))
        sa[a] = sg[a]

    def small_2():
        got(sa.at[pl.ds(0, AN - 1)], s1_s, s1_r, at_a(a))
        total = sa[0]
        for q in range(1, AN):
            total = total + sa[q]
        own = 2 * zz + core
        sb[own] = total
        send(sb.at[own], sb.at[own], s2_s, s2_r, partner())
        for d in range(1, BN):
            for c in range(2):
                send(sb.at[own], sb.at[own], s2_s, s2_r, at_zc(lax.rem(zz + d, BN), c))

    def small_3():
        got(sb.at[pl.ds(0, 2 * BN - 1)], s2_s, s2_r, at_b(zz))
        total = sb[0]
        for w in range(1, 2 * BN):
            total = total + sb[w]
        sf[a] = total
        for d in range(1, AN):
            send(sf.at[a], sf.at[a], s3_s, s3_r, at_a(lax.rem(a + d, AN)))

    def small_4():
        got(sf.at[pl.ds(0, AN - 1)], s3_s, s3_r, at_a(a))
        for r in range(NF):
            out_in[r:r + 1] = sf[r // 2, r % 2:r % 2 + 1]
        for r in range(4):
            out_vec[r:r + 1] = sf[(NF + r) // 2, r % 2:r % 2 + 1]

    PAIRS = NCH // 2
    lax.fori_loop(0, PAIRS, back_top, 0)
    weigh(1, PAIRS - 1, gtop, second_r, third_r)
    hand(0)

    def back_mid(k, carry):
        layer_back(k, top_w, third_r, second_r, gmid, first_r, k > 0)

        @pl.when(k == 1)
        def _():
            ar_1(0)

        @pl.when(k == 4)
        def _():
            ar_2(0)

        return carry

    lax.fori_loop(0, PAIRS, back_mid, 0)
    weigh(1, PAIRS - 1, gmid, first_r, second_r)
    hand(1)

    def back_first(k, carry):
        layer_back(k, mid_w, second_r, first_r, gin, x_r, k > 0)

        @pl.when(k == 1)
        def _():
            ar_1(1)
            ar_3(0)

        @pl.when(k == 4)
        def _():
            ar_2(1)
            ar_4(0)

        return carry

    lax.fori_loop(0, PAIRS, back_first, 0)
    weigh(1, PAIRS - 1, gin, x_r, first_r)

    small_1()
    ar_3(1)
    small_2()
    ar_5(0, out_top)
    small_3()
    ar_4(1)
    small_4()
    ar_5(1, out_mid)

    leave.wait()
    for k in range(2):
        for q in plane_peers:
            gone(edge.at[k, core], pl_s.at[k, q], pl_r.at[k, p], at_plane(q))
        for w in tower:
            gone(picked.at[k, w], zz_s.at[k, w], zz_r.at[k, mine], at_tower(w))
    for w in tower:
        gone(meta.at[mine], me_s.at[w], me_r.at[mine], at_tower(w))
        gone(cote.at[core], cz_s.at[w], cz_r.at[mine], at_tower(w))
    for q in plane_peers:
        gone(tbl.at[q], rt_s.at[q], rt_r.at[p], at_plane(q))
    for i in range(2):
        gone(cg.at[i], c_s.at[i], c_r.at[i], partner())
        gone(ra.at[i, pl.ds(0, AN - 1)], a1_s.at[i], a1_r.at[i], at_b(zz))
        gone(rb.at[i, pl.ds(0, BN - 1)], a2_s.at[i], a2_r.at[i], at_b(zz))
        gone(ra.at[i, pl.ds(0, AN - 1)], a3_s.at[i], a3_r.at[i], at_b(zz))
        gone(cg.at[i], f_s.at[i], f_r.at[i], partner())
    gone(sa.at[pl.ds(0, AN - 1)], s1_s, s1_r, at_a(a))
    gone(sb.at[pl.ds(0, 2 * BN - 1)], s2_s, s2_r, at_b(zz))
    gone(sf.at[pl.ds(0, AN - 1)], s3_s, s3_r, at_a(a))


def copy_kernel(*refs):
    ins, outs, held, sem = refs[:5], refs[5:10], refs[10:15], refs[15]
    parts = [(0, slice(v, v + 1)) for v in range(NV)] + [(i, slice(None)) for i in range(1, 5)]
    come = [pltpu.make_async_copy(ins[i].at[at], held[i].at[at], sem.at[0, n]) for n, (i, at) in enumerate(parts)]
    go = [pltpu.make_async_copy(held[i].at[at], outs[i].at[at], sem.at[1, n]) for n, (i, at) in enumerate(parts)]
    for copy in come:
        copy.start()
    for first, then in zip(come, go):
        first.wait()
        then.start()
    for copy in go:
        copy.wait()


def per_device(
    initial_state, target, features, coupling, in_weight, mid_weight, top_weight, out_weight, biases,
    block_count, connectivity, orientation, rotation,
):
    cells = lax.axis_size("op") * lax.axis_size("blk") * NS * BI * BJ
    loss_scale = 2.0 / math.sqrt(cells)
    vmem = pl.BlockSpec(memory_space=pltpu.VMEM)
    smem = pl.BlockSpec(memory_space=pltpu.SMEM)
    anywhere = pl.BlockSpec(memory_space=pl.ANY)
    dma = pltpu.SemaphoreType.DMA
    field = pltpu.VMEM((NV, NS, BI, BJ), f32)
    outs = pl.pallas_call(
        functools.partial(kernel, loss_scale),
        out_shape=(
            jax.ShapeDtypeStruct((NV, NS, BI, BJ), f32),
            jax.ShapeDtypeStruct((NF, HID), f32),
            jax.ShapeDtypeStruct((HID, HID), f32),
            jax.ShapeDtypeStruct((HID, HID), f32),
            jax.ShapeDtypeStruct((4, HID), f32),
        ),
        in_specs=[anywhere, anywhere, anywhere, smem, vmem, vmem, vmem, vmem, vmem, smem, smem, smem, smem],
        out_specs=(anywhere, vmem, vmem, vmem, vmem),
        scratch_shapes=[
            field, field, field, pltpu.VMEM((NF, NS, BI, BJ), bf16),
            pltpu.VMEM((NCH // 2, NF, CW), bf16),
            pltpu.VMEM((NCH // 2, NF, CW), bf16),
            pltpu.VMEM((NCH // 2, HID, CW), bf16),
            pltpu.VMEM((NCH // 2, HID, CW), bf16),
            pltpu.VMEM((NCH // 2, HID, CW), bf16),
            pltpu.VMEM((NCH // 2, HID, CW), bf16),
            pltpu.VMEM((NCH // 2, HID, CW), bf16),
            pltpu.VMEM((NCH // 2, HID, CW), bf16),
            pltpu.VMEM((NS, 2, NF * 16, BJ), f32),
            pltpu.VMEM((HID, NF), bf16),
            pltpu.VMEM((HID, HID), bf16),
            pltpu.VMEM((HID, HID), bf16),
            pltpu.VMEM((3, HID, BJ), f32),
            pltpu.VMEM((HID, BJ), f32),
            field, field, field, field,
            pltpu.VMEM((NS * BI, BJ), f32),
            pltpu.VMEM((NS * BI, BJ), f32),
            pltpu.VMEM((NS * BI, BJ), f32),
            pltpu.VMEM((NS * BI, BJ), f32),
            pltpu.VMEM((2, 2, 8, HALF), f32),
            pltpu.VMEM((2, PL, 8, HALF), f32),
            pltpu.VMEM((2, 2 * ZN, 8, HALF), f32),
            pltpu.VMEM((2, 2 * ZN, 8, HALF), f32),
            pltpu.VMEM((2, 8, HALF), f32),
            pltpu.VMEM((4, 8, BJ), f32),
            pltpu.VMEM((2 * ZN, 8, BJ), f32),
            pltpu.VMEM((2 * ZN * 8, PL * 8), bf16),
            pltpu.VMEM((PL * 8, 2 * ZN * 8), bf16),
            pltpu.VMEM((2, NV, 8, BJ), f32),
            pltpu.VMEM((2, 8, HALF), f32),
            pltpu.VMEM((2 * ZN, 8, HALF), f32),
            pltpu.VMEM((PL, 8, HALF), f32),
            pltpu.VMEM((PL, 8, HALF), f32),
            pltpu.VMEM((HID + 16, HID), f32),
            pltpu.VMEM((HID + 16, HID), f32),
            pltpu.VMEM((NF + 16, HID), f32),
            pltpu.VMEM((HID, BJ), f32),
            pltpu.VMEM((2, HID // 2, HID), f32),
            pltpu.VMEM((2, AN, HID // 2 // AN, HID), f32),
            pltpu.VMEM((2, AN, HID // 2 // AN, HID), f32),
            pltpu.VMEM((2, BN, HID // 2 // AN, HID), f32),
            pltpu.VMEM((2, 2, AN, HID // 2 // AN, HID), f32),
            pltpu.VMEM((AN, 2, HID), f32),
            pltpu.VMEM((AN, 2, HID), f32),
            pltpu.VMEM((2 * BN, 2, HID), f32),
            pltpu.VMEM((AN, 2, HID), f32),
            dma((2, PL)), dma((2, PL)), dma((2 * ZN,)), dma((2 * ZN,)), dma((2, 2 * ZN)), dma((2, 2 * ZN)),
            dma((2 * ZN,)), dma((2 * ZN,)), dma((PL,)), dma((PL,)),
            dma((4,)), dma((2,)), dma((2,)), dma((2,)), dma((2,)), dma((2,)), dma((2,)), dma((2,)), dma((2,)), dma((2,)), dma((2,)),
            dma, dma, dma, dma, dma, dma,
        ],
        compiler_params=pltpu.CompilerParams(
            collective_id=0, has_side_effects=True, vmem_limit_bytes=56 * 2**20
        ),
    )(
        initial_state[0], target[0], features[0], coupling, in_weight, mid_weight, top_weight,
        out_weight, biases, block_count, connectivity.T, orientation.T, rotation.T,
    )
    outs = pl.pallas_call(
        copy_kernel,
        out_shape=tuple(jax.ShapeDtypeStruct(x.shape, x.dtype) for x in outs),
        in_specs=[anywhere] * 5,
        out_specs=(anywhere,) * 5,
        scratch_shapes=[pltpu.VMEM(x.shape, x.dtype) for x in outs] + [dma((2, NV + 4))],
    )(*outs)
    return (outs[0][None],) + tuple(outs[1:])


def solution(mesh):
    wide = P("op", None, "blk", None, None)
    return jax.shard_map(
        per_device,
        mesh=mesh,
        in_specs=(wide, wide, wide) + (P(),) * 6 + (P("blk"),) + (P("blk", None),) * 3,
        out_specs=(wide, P(), P(), P(), P()),
        check_vma=False,
    )
```

```python
import functools
import math

import jax
import jax.numpy as jnp
from jax import lax
from jax.experimental import pallas as pl
from jax.experimental.pallas import tpu as pltpu
from jax.sharding import PartitionSpec as P

MESH = pl.DeviceIdType.MESH
tau = 0.2
passage_angle = 2.0 * math.pi / 36.0
cos_step = math.cos(passage_angle)
sin_step = math.sin(passage_angle)
f32 = jnp.float32
bf16 = jnp.bfloat16

NV, NS, BI, BJ, HID, NF = 6, 3, 32, 128, 256, 16
PL = 8
ZN = 4
NCH = 12
CW = 1024
EDGE = NCH - 1
AN = 16
BN = 8
HV = NV // 2
HALF = HV * BJ
FH = NF // 2
FROW = FH * BJ
GHOST = NCH // 2


def row_of(s, i):
    if i == 0 or i == BI - 1:
        return 8 * EDGE + 2 * s + (i != 0)
    inner = (BI - 2) * s + i - 1
    return inner if inner < 8 * EDGE else inner + 2 * NS


def runs(s):
    whole = (BI - 2) * s
    first = min(BI - 2, 8 * EDGE - whole)
    res = [(1, whole, first)]
    if first < BI - 2:
        res.append((1 + first, row_of(s, 1 + first), BI - 2 - first))
    return res


def nt(a, b):
    return lax.dot_general(a, b, (((1,), (1,)), ((), ())), preferred_element_type=f32)


def mm(a, b):
    return jnp.dot(a, b, preferred_element_type=f32)


def lanes_sum(u, lane):
    left = jnp.where(lane == 0, u, pltpu.roll(u, 1, 1))
    right = jnp.where(lane == BJ - 1, u, pltpu.roll(u, BJ - 1, 1))
    return left + right


def kernel(
    loss_scale,
    state_h, target_h, feat_h, coup, in_w, mid_w, top_w, out_w, biases, count, conn, orient, rot,
    out_h, out_in, out_mid, out_top, out_vec,
    out_state, state, target, feat, x0, x1, first0, first1, second0, second1, third0, third1,
    xs, win_t, wmid_t, wtop_t, bias_c, ow_c,
    mid_r, ts_r, tm_r, fc_r, beta_r, betan_r, bc_r, bcn_r,
    edge, gath, picked, arr, inner, tile_r, meta, sel_r, ghost_r, rawt,
    fedge, fgath, fpicked, farr, xg,
    gtop, gmid, gin, gout,
    cg, gsum, ra, rb, full, sg, sa, sb, sf,
    pl_s, pl_r, me_s, me_r, zz_s, zz_r, fz_s, fz_r, fp_s, fp_r,
    in_s, c_s, c_r, a1_s, a1_r, a2_s, a2_r, a3_s, a3_r, f_s, f_r, s1_s, s1_r, s2_s, s2_r, s3_s, s3_r,
):
    x_r, first_r, second_r, third_r = (x0, x1), (first0, first1), (second0, second1), (third0, third1)
    b = lax.axis_index("blk")
    o = lax.axis_index("op")
    z = lax.div(b, PL)
    p = lax.rem(b, PL)

    plane_peers = [lax.rem(p + d, PL) for d in range(1, PL)]
    x_at = lax.div(o, 2)
    z_lo = lax.rem(o, 2)
    core = lax.rem(b, 2)
    mine = z * 2 + core
    tower = [lax.rem(mine + d, 2 * ZN) for d in range(1, 2 * ZN)]
    a = x_at * ZN + lax.div(p, 2)
    zz = z * 2 + z_lo

    def at_plane(q):
        return {"blk": z * PL + q}

    def at_tower(w):
        return {"blk": lax.div(w, 2) * PL + p - core + lax.rem(w, 2)}

    def at_a(q):
        return {"blk": z * PL + lax.rem(q, 4) * 2 + core, "op": lax.div(q, 4) * 2 + z_lo}

    def at_zc(w, c):
        return {"blk": lax.div(w, 2) * PL + p - core + c, "op": x_at * 2 + lax.rem(w, 2)}

    def partner():
        return {"blk": b + 1 - 2 * core}

    def at_b(w):
        return {"blk": lax.div(w, 2) * PL + p, "op": x_at * 2 + lax.rem(w, 2)}

    def send(src, dst, s_sem, r_sem, device):
        copy = pltpu.make_async_remote_copy(
            src_ref=src, dst_ref=dst, send_sem=s_sem, recv_sem=r_sem, device_id=device, device_id_type=MESH
        )
        copy.start()

    def got(dst, s_sem, r_sem, device):
        pltpu.make_async_remote_copy(
            src_ref=dst, dst_ref=dst, send_sem=s_sem, recv_sem=r_sem, device_id=device, device_id_type=MESH
        ).wait_recv()

    def gone(src, s_sem, r_sem, device):
        pltpu.make_async_remote_copy(
            src_ref=src, dst_ref=src, send_sem=s_sem, recv_sem=r_sem, device_id=device, device_id_type=MESH
        ).wait_send()

    barrier = pltpu.get_barrier_semaphore()
    def greet(device):
        pl.semaphore_signal(barrier, inc=1, device_id=device, device_id_type=MESH)

    for q in plane_peers:
        greet(at_plane(q))
    for d in range(4, AN):
        greet(at_a(lax.rem(x_at * 4 + d, AN)))
    for d in range(1, BN):
        for c in range(2):
            greet(at_zc(lax.rem(zz + d, BN), c))

    loads = [pltpu.make_async_copy(h, v, in_s.at[i]) for i, (h, v) in enumerate(((state_h, state), (feat_h, feat), (target_h, target)))]
    for load in loads:
        load.start()

    rowi = lax.broadcasted_iota(jnp.int32, (8, BJ), 0)
    lane8 = lax.broadcasted_iota(jnp.int32, (8, BJ), 1)
    meta_t = jnp.full((8, BJ), -1.0, f32)
    flip_t = jnp.zeros((8, BJ), f32)
    cos_t = jnp.ones((8, BJ), f32)
    sin_t = jnp.zeros((8, BJ), f32)
    live_t = jnp.zeros((8, BJ), f32)
    live = []
    for s in range(NS):
        live.append(jnp.where(s < count[0], 1.0, 0.0).astype(f32))
        for e in range(2):
            here = rowi == 2 * s + e
            idx = conn[e, s]
            idx = idx + 2 * ((idx * 10923) >> 16)
            meta_t = jnp.where(here, idx.astype(f32), meta_t)
            flip_t = jnp.where(here, orient[e, s].astype(f32), flip_t)
            turn = rot[e, s]
            cos_t = jnp.where(here, jnp.where(turn == 0, 1.0, cos_step).astype(f32), cos_t)
            sin_t = jnp.where(here, turn.astype(f32) * sin_step, sin_t)
            live_t = jnp.where(here, live[s], live_t)
    meta[mine] = meta_t
    tile_r[0] = flip_t
    tile_r[1] = cos_t
    tile_r[2] = sin_t
    tile_r[3] = live_t

    def part(ref, v):
        return ref.at[v // HV, :, v % HV * BJ:(v % HV + 1) * BJ]

    def pack(dst, field, rows):
        dst[...] = jnp.zeros((2, 8, HALF), f32)
        for v in range(NV):
            for s in range(NS):
                for e in range(2):
                    part(dst, v)[2 * s + e:2 * s + e + 1, :] = field[v, s, rows[e]:rows[e] + 1, :]

    def cut(ref):
        return [part(ref, v)[...] for v in range(NV)]

    def thirds(u):
        u1 = u.astype(bf16)
        u2 = (u - u1.astype(f32)).astype(bf16)
        u3 = (u - u1.astype(f32) - u2.astype(f32)).astype(bf16)
        return u1, u2, u3

    def by_rows(mask, u):
        r = mm(mask, jnp.concatenate(thirds(u), axis=1))
        return r[:, :HALF] + r[:, HALF:2 * HALF] + r[:, 2 * HALF:]

    loads[0].wait()
    pack(edge.at[0], state, (0, BI - 1))

    pl.semaphore_wait(barrier, PL - 1 + AN - 4 + 2 * (BN - 1))

    def send_plane(k):
        for q in plane_peers:
            send(edge.at[k, lax.rem(q, 2)], gath.at[k, p], pl_s.at[k, q], pl_r.at[k, p], at_plane(q))
        gath[k, p] = edge[k, core]

    for w in tower:
        send(meta.at[mine], meta.at[mine], me_s.at[w], me_r.at[mine], at_tower(w))
    send_plane(0)

    def pick(k):
        for q in plane_peers:
            got(gath.at[k, q], pl_s.at[k, q], pl_r.at[k, q], at_plane(q))
        chosen = by_rows(sel_r[...], gath[k].reshape(PL * 8, HALF))
        picked[k] = chosen.reshape(2 * ZN, 8, HALF)
        arr[k, mine] = picked[k, mine]
        for w in tower:
            send(picked.at[k, w], arr.at[k, mine], zz_s.at[k, w], zz_r.at[k, mine], at_tower(w))

    def make_sel():
        for w in tower:
            got(meta.at[w], me_s.at[w], me_r.at[w], at_tower(w))
        n = 2 * ZN * 8
        lane = lax.broadcasted_iota(jnp.int32, (n, BJ), 1)
        named = meta[...].reshape(n, BJ)
        local = named - (z * (PL * 8)).astype(f32)
        sel = jnp.where((local == lane.astype(f32)) & (lane < PL * 8), 1.0, 0.0).astype(f32)
        sel_r[...] = sel[:, :PL * 8].astype(bf16)

    def pick_features():
        for q in plane_peers:
            got(fgath.at[q], fp_s.at[q], fp_r.at[q], at_plane(q))
        chosen = mm(sel_r[...], fgath[...].reshape(PL * 8, FROW).astype(bf16))
        fpicked[...] = chosen.reshape(2 * ZN, 8, FROW)
        farr[mine] = fpicked[mine]
        for w in tower:
            send(fpicked.at[w], farr.at[mine], fz_s.at[w], fz_r.at[mine], at_tower(w))

    def ghost_features():
        for w in tower:
            got(farr.at[w], fz_s.at[w], fz_r.at[w], at_tower(w))
        for h in range(2):
            total = (farr[h] + farr[2 + h]) + (farr[4 + h] + farr[6 + h])
            for f in range(FH):
                for g in range(8):
                    xg[h * FH + f:h * FH + f + 1, g * BJ:(g + 1) * BJ] = total[g:g + 1, f * BJ:(f + 1) * BJ]
        x0[GHOST] = xg[...].astype(bf16)

    def turned(parts, sign):
        flip, cos, sin = tile_r[0], tile_r[1], tile_r[2] * sign
        r = lax.broadcasted_iota(jnp.int32, (BJ, BJ), 0)
        c = lax.broadcasted_iota(jnp.int32, (BJ, BJ), 1)
        anti = jnp.where(r + c == BJ - 1, 1.0, 0.0).astype(bf16)
        n = 8 * NV
        back = mm(jnp.concatenate(thirds(jnp.concatenate(parts, axis=0)), axis=0), anti)
        back = back[:n] + back[n:2 * n] + back[2 * n:]
        out = [jnp.where(flip > 0.5, back[8 * v:8 * v + 8], parts[v]) for v in range(NV)]
        c2 = cos * out[2] - sin * out[3]
        c3 = sin * out[2] + cos * out[3]
        return [out[0], out[1], c2, c3, out[4], out[5]]

    def ghosts(k):
        for w in tower:
            got(arr.at[k, w], zz_s.at[k, w], zz_r.at[k, w], at_tower(w))
        total = [(arr[k, h] + arr[k, 2 + h]) + (arr[k, 4 + h] + arr[k, 6 + h]) for h in range(2)]
        if k == 0:
            for v in range(NV):
                rawt[v] = jnp.tanh(total[v // HV][:, v % HV * BJ:(v % HV + 1) * BJ])
        parts = turned([total[v // HV][:, v % HV * BJ:(v % HV + 1) * BJ] for v in range(NV)], 1.0)
        for v in range(NV):
            ghost_r[k, v] = parts[v]

    def edge_sweep(e, n, gh):
        res = []
        beta_e = jnp.where(rowi < 2 * NS, beta_r[8 * EDGE:8 * EDGE + 8, :], 0.0)
        for v in range(NV):
            lap = gh[v] + n[v] + lanes_sum(e[v], lane8) - 4.0 * e[v]
            coupled = coup[v, 0] * e[0]
            for w in range(1, NV):
                coupled = coupled + coup[v, w] * e[w]
            res.append(e[v] + tau * (lap - coupled + beta_e * jnp.tanh(e[v])))
        return res

    pad = jnp.zeros((BJ - NF, HID), f32)
    win_t[...] = jnp.concatenate([in_w[...].astype(f32), pad], axis=0).T[:, :NF].astype(bf16)
    wmid_t[...] = mid_w[...].astype(f32).T.astype(bf16)
    wtop_t[...] = top_w[...].astype(f32).T.astype(bf16)
    for k in range(3):
        bias_c[k] = jnp.broadcast_to(biases[k:k + 1, :], (BJ, HID)).T
    ow_c[...] = jnp.broadcast_to(out_w[...].astype(f32).reshape(1, HID), (BJ, HID)).T

    loads[1].wait()
    for s in range(NS):
        for h in range(2):
            xs[s, h] = feat[:, s, 16 * h:16 * h + 16, :].astype(f32).reshape(NF * 16, BJ)
    fedge[...] = jnp.zeros((2, 8, FROW), f32)
    for s in range(NS):
        for e in range(2):
            for f in range(NF):
                at = f * 16 + 15 * e
                fedge[f // FH, 2 * s + e:2 * s + e + 1, f % FH * BJ:(f % FH + 1) * BJ] = xs[s, e, at:at + 1, :]
    for q in plane_peers:
        send(fedge.at[lax.rem(q, 2)], fgath.at[p], fp_s.at[q], fp_r.at[p], at_plane(q))
    fgath[p] = fedge[core]

    for s in range(NS):
        for h in range(2):
            for r in range(16):
                row = row_of(s, 16 * h + r)
                x_r[row // 8 % 2][row // 16, :, (row % 8) * BJ:(row % 8 + 1) * BJ] = xs[s, h, pl.ds(r, NF, stride=16), :].astype(bf16)

    SUB = 512

    weights = (win_t, wmid_t, wtop_t)
    acts = (x_r, first_r, second_r, third_r)
    SUBS = 2 * CW // SUB

    def forward(k, carry):
        pair = (lax.rem(k + EDGE // 2, NCH // 2), k)

        def place(j):
            half = j // (CW // SUB)
            return 1 - half, pair[half], slice((j % (CW // SUB)) * SUB, (j % (CW // SUB) + 1) * SUB)

        def product(layer, j):
            par, c, cols = place(j)
            return mm(weights[layer][...], acts[layer][par][c, :, cols])

        tiles = [jnp.zeros((8, BJ), f32), jnp.zeros((8, BJ), f32)]

        def activate(layer, j, d):
            par, c, cols = place(j)
            bias = bias_c[layer]
            for i in range(SUB // BJ):
                t = jnp.tanh(d[:, i * BJ:(i + 1) * BJ] + bias).astype(bf16)
                acts[layer + 1][par][c, :, cols.start + i * BJ:cols.start + (i + 1) * BJ] = t
                if layer == 2:
                    bt = jnp.sum(ow_c[...] * t.astype(f32), axis=0, keepdims=True) + 1.0
                    row = (j % (CW // SUB)) * (SUB // BJ) + i
                    half = j // (CW // SUB)
                    tiles[half] = jnp.where(rowi == row, bt, tiles[half])

        tasks = [(layer, j) for layer in range(3) for j in range(SUBS)]
        held = None
        for task in tasks:
            d = product(*task)
            if held is not None:
                activate(*held)
            held = task + (d,)
        activate(*held)
        for half in range(2):
            beta_r[pl.ds(pl.multiple_of((2 * pair[half] + 1 - half) * 8, 8), 8), :] = tiles[half]

        @pl.when(k == 0)
        def _():
            make_sel()
            pick(0)

        @pl.when(k == 2)
        def _():
            ghosts(0)
            pack(inner, state, (1, BI - 2))
            res = edge_sweep(cut(edge.at[0]), cut(inner), [ghost_r[0, v] for v in range(NV)])
            for v in range(NV):
                part(edge.at[1], v)[...] = res[v]
            send_plane(1)

        @pl.when(k == 4)
        def _():
            pick(1)
            pick_features()

        return carry

    lax.fori_loop(0, NCH // 2, forward, 0)

    for s in range(NS):
        for e in range(2):
            g = 8 * EDGE + 2 * s + e
            row = s * BI + e * (BI - 1)
            betan_r[row:row + 1, :] = beta_r[g:g + 1, :]
        for first, place, length in runs(s):
            betan_r[s * BI + first:s * BI + first + length, :] = beta_r[place:place + length, :]

    rows32 = lax.broadcasted_iota(jnp.int32, (BI, BJ), 0)
    lane32 = lax.broadcasted_iota(jnp.int32, (BI, BJ), 1)

    def stencil(u, low, high):
        up = jnp.where(rows32 == 0, low, pltpu.roll(u, 1, 0))
        down = jnp.where(rows32 == BI - 1, high, pltpu.roll(u, BI - 1, 0))
        return up + down + lanes_sum(u, lane32) - 4.0 * u

    def low_high(k, s, v):
        return ghost_r[k, v, 2 * s:2 * s + 1, :], ghost_r[k, v, 2 * s + 1:2 * s + 2, :]

    for s in range(NS):
        us = [state[v, s] for v in range(NV)]
        beta = betan_r[s * BI:(s + 1) * BI, :]
        for v in range(NV):
            t = jnp.tanh(us[v])
            ts_r[v, s] = t
            low, high = low_high(0, s, v)
            coupled = coup[v, 0] * us[0]
            for w in range(1, NV):
                coupled = coupled + coup[v, w] * us[w]
            mid_r[v, s] = us[v] + tau * (stencil(us[v], low, high) - coupled + beta * t)

    ghosts(1)
    pack(inner, mid_r, (1, BI - 2))
    final_e = edge_sweep(cut(edge.at[1]), cut(inner), [ghost_r[1, v] for v in range(NV)])
    loads[2].wait()
    pack(inner, target, (0, BI - 1))
    goal_e = cut(inner)
    cot_e = [tau * (loss_scale * tile_r[3] * (final_e[v] - goal_e[v])) for v in range(NV)]
    cot_e = turned(cot_e, -1.0)
    gained = cot_e[0] * rawt[0]
    for v in range(1, NV):
        gained = gained + cot_e[v] * rawt[v]
    bc_r[8 * NCH:8 * NCH + 8, :] = tau * gained

    for s in range(NS):
        us = [mid_r[v, s] for v in range(NV)]
        beta = betan_r[s * BI:(s + 1) * BI, :]
        for v in range(NV):
            t = jnp.tanh(us[v])
            tm_r[v, s] = t
            low, high = low_high(1, s, v)
            coupled = coup[v, 0] * us[0]
            for w in range(1, NV):
                coupled = coupled + coup[v, w] * us[w]
            final = us[v] + tau * (stencil(us[v], low, high) - coupled + beta * t)
            out_state[v, s] = live[s] * final
            fc_r[v, s] = loss_scale * live[s] * (final - target[v, s])

    for s in range(NS):
        gs = [fc_r[v, s] for v in range(NV)]
        beta = betan_r[s * BI:(s + 1) * BI, :]
        acc = jnp.zeros((BI, BJ), f32)
        for v in range(NV):
            t = tm_r[v, s]
            coupled = coup[0, v] * gs[0]
            for w in range(1, NV):
                coupled = coupled + coup[w, v] * gs[w]
            mc = gs[v] + tau * (stencil(gs[v], 0.0, 0.0) - coupled + beta * (1.0 - t * t) * gs[v])
            acc = acc + (gs[v] * t + mc * ts_r[v, s])
        bcn_r[s * BI:(s + 1) * BI, :] = tau * acc
        for e in range(2):
            g = 8 * EDGE + 2 * s + e
            row = s * BI + e * (BI - 1)
            bc_r[g:g + 1, :] = bcn_r[row:row + 1, :]
        for first, place, length in runs(s):
            bc_r[place:place + length, :] = bcn_r[s * BI + first:s * BI + first + length, :]

    leave = pltpu.make_async_copy(out_state, out_h, in_s.at[3])
    leave.start()

    def forward_ghost():
        ghost_features()
        for layer in range(3):
            for j in range(CW // SUB):
                cols = slice(j * SUB, (j + 1) * SUB)
                d = mm(weights[layer][...], acts[layer][0][GHOST, :, cols])
                for i in range(SUB // BJ):
                    here = slice(cols.start + i * BJ, cols.start + (i + 1) * BJ)
                    acts[layer + 1][0][GHOST, :, here] = jnp.tanh(d[:, i * BJ:(i + 1) * BJ] + bias_c[layer]).astype(bf16)

    ones = jnp.ones((16, CW), bf16)
    gout[...] = jnp.zeros((HID, BJ), f32)
    gtop[...] = jnp.zeros((HID + 16, HID), f32)
    gmid[...] = jnp.zeros((HID + 16, HID), f32)
    gin[...] = jnp.zeros((NF + 16, HID), f32)

    def weigh(par, k, acc, left, right, fresh=None):
        part = nt(jnp.concatenate([left[par][k], ones], axis=0), right[par][k])
        if fresh is not None:
            part = jnp.where(fresh, part, 0.0)
        acc[...] = acc[...] + part

    def before(k):
        return lax.rem(k + NCH // 2 - 1, NCH // 2)

    RB = 64

    def top_delta(par, k):
        third = third_r[par]
        bc = bc_r[pl.ds(pl.multiple_of((2 * k + par) * 8, 8), 8), :]
        ch = bc.astype(bf16).astype(f32)
        for i in range(HID // RB):
            rows = slice(i * RB, (i + 1) * RB)
            ow = ow_c[rows]
            acc = gout[rows]
            for j in range(CW // BJ):
                cols = slice(j * BJ, (j + 1) * BJ)
                t = third[k, rows, cols].astype(f32)
                acc = acc + t * ch[j:j + 1]
                third[k, rows, cols] = (ow * bc[j:j + 1] * (1.0 - t * t)).astype(bf16)
            gout[rows] = acc

    def back_top(k, carry):
        weigh(1, before(k), gtop, second_r, third_r, k > 0)
        top_delta(0, k)
        weigh(0, k, gtop, second_r, third_r)
        top_delta(1, k)
        return carry

    def layer_back(k, weight, source, act, acc, left, fresh=None):
        held = None

        def put(par, cols, d):
            for i in range(SUB // BJ):
                here = slice(cols.start + i * BJ, cols.start + (i + 1) * BJ)
                t = act[par][k, :, here].astype(f32)
                act[par][k, :, here] = (d[:, i * BJ:(i + 1) * BJ] * (1.0 - t * t)).astype(bf16)

        for par in range(2):
            for j in range(CW // SUB):
                cols = slice(j * SUB, (j + 1) * SUB)
                d = mm(weight[...], source[par][k, :, cols])
                if held is not None:
                    put(*held)
                held = (par, cols, d)
                if j == 0:
                    if par == 0:
                        weigh(1, before(k), acc, left, act, fresh)
                    else:
                        put(*held)
                        held = None
                        weigh(0, k, acc, left, act)
        put(*held)

    def back_mid(k, carry):
        layer_back(k, top_w, third_r, second_r, gmid, first_r, k > 0)
        return carry

    def layer_ghost(weight, source, act, acc, left):
        for j in range(CW // SUB):
            cols = slice(j * SUB, (j + 1) * SUB)
            d = mm(weight[...], source[0][GHOST, :, cols])
            t = act[0][GHOST, :, cols].astype(f32)
            act[0][GHOST, :, cols] = (d * (1.0 - t * t)).astype(bf16)
        weigh(0, GHOST, acc, left, act)

    grads = (gtop, gmid)
    HR = HID // 2
    R = HR // AN

    def hand(i):
        other = pl.ds(pl.multiple_of((1 - core) * HR, HR), HR)
        send(grads[i].at[other], cg.at[i], c_s.at[i], c_r.at[i], partner())

    def ar_1(i):
        got(cg.at[i], c_s.at[i], c_r.at[i], partner())
        half = grads[i][pl.ds(pl.multiple_of(core * HR, HR), HR), :] + cg[i]
        gsum[i] = half.reshape(AN, R, HID)
        for d in range(1, AN):
            q = lax.rem(a + d, AN)
            send(gsum.at[i, q], ra.at[i, a], a1_s.at[i], a1_r.at[i], at_a(q))
        ra[i, a] = gsum[i, a]

    def ar_2(i):
        got(ra.at[i, pl.ds(0, AN - 1)], a1_s.at[i], a1_r.at[i], at_b(zz))
        total = ra[i, 0]
        for q in range(1, AN):
            total = total + ra[i, q]
        rb[i, zz] = total
        for d in range(1, BN):
            send(rb.at[i, zz], rb.at[i, zz], a2_s.at[i], a2_r.at[i], at_b(lax.rem(zz + d, BN)))

    def ar_3(i):
        got(rb.at[i, pl.ds(0, BN - 1)], a2_s.at[i], a2_r.at[i], at_b(zz))
        total = rb[i, 0]
        for w in range(1, BN):
            total = total + rb[i, w]
        full[i, core, a] = total
        for d in range(1, AN):
            send(full.at[i, core, a], full.at[i, core, a], a3_s.at[i], a3_r.at[i], at_a(lax.rem(a + d, AN)))

    def ar_4(i):
        got(full.at[i, core, pl.ds(0, AN - 1)], a3_s.at[i], a3_r.at[i], at_b(zz))
        send(full.at[i, core], full.at[i, core], f_s.at[i], f_r.at[i], partner())

    def ar_5(i, out):
        got(full.at[i, 1 - core], f_s.at[i], f_r.at[i], partner())
        out[...] = full[i].reshape(HID, HID)

    def small_1():
        for r in range(NF):
            sg[r // 2, r % 2:r % 2 + 1] = gin[r:r + 1]
        sg[NF // 2, 0:1] = jnp.sum(gout[...].T, axis=0, keepdims=True)
        sg[NF // 2, 1:2] = gin[NF:NF + 1]
        sg[NF // 2 + 1, 0:1] = gmid[HID:HID + 1]
        sg[NF // 2 + 1, 1:2] = gtop[HID:HID + 1]
        sg[NF // 2 + 2:] = jnp.zeros((AN - NF // 2 - 2, 2, HID), f32)
        for d in range(1, AN):
            q = lax.rem(a + d, AN)
            send(sg.at[q], sa.at[a], s1_s, s1_r, at_a(q))
        sa[a] = sg[a]

    def small_2():
        got(sa.at[pl.ds(0, AN - 1)], s1_s, s1_r, at_a(a))
        total = sa[0]
        for q in range(1, AN):
            total = total + sa[q]
        own = 2 * zz + core
        sb[own] = total
        send(sb.at[own], sb.at[own], s2_s, s2_r, partner())
        for d in range(1, BN):
            for c in range(2):
                send(sb.at[own], sb.at[own], s2_s, s2_r, at_zc(lax.rem(zz + d, BN), c))

    def small_3():
        got(sb.at[pl.ds(0, 2 * BN - 1)], s2_s, s2_r, at_b(zz))
        total = sb[0]
        for w in range(1, 2 * BN):
            total = total + sb[w]
        sf[a] = total
        for d in range(1, AN):
            send(sf.at[a], sf.at[a], s3_s, s3_r, at_a(lax.rem(a + d, AN)))

    def small_4():
        got(sf.at[pl.ds(0, AN - 1)], s3_s, s3_r, at_a(a))
        for r in range(NF):
            out_in[r:r + 1] = sf[r // 2, r % 2:r % 2 + 1]
        for r in range(4):
            out_vec[r:r + 1] = sf[(NF + r) // 2, r % 2:r % 2 + 1]

    LAST = NCH // 2 - 1
    lax.fori_loop(0, LAST, back_top, 0)
    weigh(1, LAST - 1, gtop, second_r, third_r)
    top_delta(0, LAST)
    weigh(0, LAST, gtop, second_r, third_r)
    lax.fori_loop(0, LAST, back_mid, 0)
    forward_ghost()
    top_delta(1, LAST)
    weigh(1, LAST, gtop, second_r, third_r)
    top_delta(0, GHOST)
    weigh(0, GHOST, gtop, second_r, third_r)
    hand(0)
    layer_back(LAST, top_w, third_r, second_r, gmid, first_r)
    weigh(1, LAST, gmid, first_r, second_r)
    layer_ghost(top_w, third_r, second_r, gmid, first_r)
    hand(1)
    ar_1(0)

    def back_first(k, carry):
        layer_back(k, mid_w, second_r, first_r, gin, x_r, k > 0)

        @pl.when(k == 1)
        def _():
            ar_1(1)

        @pl.when(k == 3)
        def _():
            ar_2(0)

        @pl.when(k == 5)
        def _():
            ar_2(1)

        return carry

    lax.fori_loop(0, LAST + 1, back_first, 0)
    weigh(1, LAST, gin, x_r, first_r)
    layer_ghost(mid_w, second_r, first_r, gin, x_r)

    small_1()
    ar_3(0)
    ar_3(1)
    small_2()
    ar_4(0)
    ar_4(1)
    small_3()
    ar_5(0, out_top)
    ar_5(1, out_mid)
    small_4()

    leave.wait()
    for k in range(2):
        for q in plane_peers:
            gone(edge.at[k, core], pl_s.at[k, q], pl_r.at[k, p], at_plane(q))
        for w in tower:
            gone(picked.at[k, w], zz_s.at[k, w], zz_r.at[k, mine], at_tower(w))
    for w in tower:
        gone(meta.at[mine], me_s.at[w], me_r.at[mine], at_tower(w))
        gone(fpicked.at[w], fz_s.at[w], fz_r.at[mine], at_tower(w))
    for q in plane_peers:
        gone(fedge.at[core], fp_s.at[q], fp_r.at[p], at_plane(q))
    for i in range(2):
        gone(cg.at[i], c_s.at[i], c_r.at[i], partner())
        gone(ra.at[i, pl.ds(0, AN - 1)], a1_s.at[i], a1_r.at[i], at_b(zz))
        gone(rb.at[i, pl.ds(0, BN - 1)], a2_s.at[i], a2_r.at[i], at_b(zz))
        gone(ra.at[i, pl.ds(0, AN - 1)], a3_s.at[i], a3_r.at[i], at_b(zz))
        gone(cg.at[i], f_s.at[i], f_r.at[i], partner())
    gone(sa.at[pl.ds(0, AN - 1)], s1_s, s1_r, at_a(a))
    gone(sb.at[pl.ds(0, 2 * BN - 1)], s2_s, s2_r, at_b(zz))
    gone(sf.at[pl.ds(0, AN - 1)], s3_s, s3_r, at_a(a))


def copy_kernel(*refs):
    ins, outs, held, sem = refs[:5], refs[5:10], refs[10:15], refs[15]
    parts = [(0, slice(v, v + 1)) for v in range(NV)] + [(i, slice(None)) for i in range(1, 5)]
    come = [pltpu.make_async_copy(ins[i].at[at], held[i].at[at], sem.at[0, n]) for n, (i, at) in enumerate(parts)]
    go = [pltpu.make_async_copy(held[i].at[at], outs[i].at[at], sem.at[1, n]) for n, (i, at) in enumerate(parts)]
    for copy in come:
        copy.start()
    for first, then in zip(come, go):
        first.wait()
        then.start()
    for copy in go:
        copy.wait()


def per_device(
    initial_state, target, features, coupling, in_weight, mid_weight, top_weight, out_weight, biases,
    block_count, connectivity, orientation, rotation,
):
    cells = lax.axis_size("op") * lax.axis_size("blk") * NS * BI * BJ
    loss_scale = 2.0 / math.sqrt(cells)
    vmem = pl.BlockSpec(memory_space=pltpu.VMEM)
    smem = pl.BlockSpec(memory_space=pltpu.SMEM)
    anywhere = pl.BlockSpec(memory_space=pl.ANY)
    dma = pltpu.SemaphoreType.DMA
    field = pltpu.VMEM((NV, NS, BI, BJ), f32)
    outs = pl.pallas_call(
        functools.partial(kernel, loss_scale),
        out_shape=(
            jax.ShapeDtypeStruct((NV, NS, BI, BJ), f32),
            jax.ShapeDtypeStruct((NF, HID), f32),
            jax.ShapeDtypeStruct((HID, HID), f32),
            jax.ShapeDtypeStruct((HID, HID), f32),
            jax.ShapeDtypeStruct((4, HID), f32),
        ),
        in_specs=[anywhere, anywhere, anywhere, smem, vmem, vmem, vmem, vmem, vmem, smem, smem, smem, smem],
        out_specs=(anywhere, vmem, vmem, vmem, vmem),
        scratch_shapes=[
            field, field, field, pltpu.VMEM((NF, NS, BI, BJ), bf16),
            pltpu.VMEM((NCH // 2 + 1, NF, CW), bf16),
            pltpu.VMEM((NCH // 2, NF, CW), bf16),
            pltpu.VMEM((NCH // 2 + 1, HID, CW), bf16),
            pltpu.VMEM((NCH // 2, HID, CW), bf16),
            pltpu.VMEM((NCH // 2 + 1, HID, CW), bf16),
            pltpu.VMEM((NCH // 2, HID, CW), bf16),
            pltpu.VMEM((NCH // 2 + 1, HID, CW), bf16),
            pltpu.VMEM((NCH // 2, HID, CW), bf16),
            pltpu.VMEM((NS, 2, NF * 16, BJ), f32),
            pltpu.VMEM((HID, NF), bf16),
            pltpu.VMEM((HID, HID), bf16),
            pltpu.VMEM((HID, HID), bf16),
            pltpu.VMEM((3, HID, BJ), f32),
            pltpu.VMEM((HID, BJ), f32),
            field, field, field, field,
            pltpu.VMEM((NS * BI, BJ), f32),
            pltpu.VMEM((NS * BI, BJ), f32),
            pltpu.VMEM((NS * BI + 8, BJ), f32),
            pltpu.VMEM((NS * BI, BJ), f32),
            pltpu.VMEM((2, 2, 8, HALF), f32),
            pltpu.VMEM((2, PL, 8, HALF), f32),
            pltpu.VMEM((2, 2 * ZN, 8, HALF), f32),
            pltpu.VMEM((2, 2 * ZN, 8, HALF), f32),
            pltpu.VMEM((2, 8, HALF), f32),
            pltpu.VMEM((4, 8, BJ), f32),
            pltpu.VMEM((2 * ZN, 8, BJ), f32),
            pltpu.VMEM((2 * ZN * 8, PL * 8), bf16),
            pltpu.VMEM((2, NV, 8, BJ), f32),
            pltpu.VMEM((NV, 8, BJ), f32),
            pltpu.VMEM((2, 8, FROW), f32),
            pltpu.VMEM((PL, 8, FROW), f32),
            pltpu.VMEM((2 * ZN, 8, FROW), f32),
            pltpu.VMEM((2 * ZN, 8, FROW), f32),
            pltpu.VMEM((NF, CW), f32),
            pltpu.VMEM((HID + 16, HID), f32),
            pltpu.VMEM((HID + 16, HID), f32),
            pltpu.VMEM((NF + 16, HID), f32),
            pltpu.VMEM((HID, BJ), f32),
            pltpu.VMEM((2, HID // 2, HID), f32),
            pltpu.VMEM((2, AN, HID // 2 // AN, HID), f32),
            pltpu.VMEM((2, AN, HID // 2 // AN, HID), f32),
            pltpu.VMEM((2, BN, HID // 2 // AN, HID), f32),
            pltpu.VMEM((2, 2, AN, HID // 2 // AN, HID), f32),
            pltpu.VMEM((AN, 2, HID), f32),
            pltpu.VMEM((AN, 2, HID), f32),
            pltpu.VMEM((2 * BN, 2, HID), f32),
            pltpu.VMEM((AN, 2, HID), f32),
            dma((2, PL)), dma((2, PL)), dma((2 * ZN,)), dma((2 * ZN,)), dma((2, 2 * ZN)), dma((2, 2 * ZN)),
            dma((2 * ZN,)), dma((2 * ZN,)), dma((PL,)), dma((PL,)),
            dma((4,)), dma((2,)), dma((2,)), dma((2,)), dma((2,)), dma((2,)), dma((2,)), dma((2,)), dma((2,)), dma((2,)), dma((2,)),
            dma, dma, dma, dma, dma, dma,
        ],
        compiler_params=pltpu.CompilerParams(
            collective_id=0, has_side_effects=True, vmem_limit_bytes=56 * 2**20
        ),
    )(
        initial_state[0], target[0], features[0], coupling, in_weight, mid_weight, top_weight,
        out_weight, biases, block_count, connectivity.T, orientation.T, rotation.T,
    )
    outs = pl.pallas_call(
        copy_kernel,
        out_shape=tuple(jax.ShapeDtypeStruct(x.shape, x.dtype) for x in outs),
        in_specs=[anywhere] * 5,
        out_specs=(anywhere,) * 5,
        scratch_shapes=[pltpu.VMEM(x.shape, x.dtype) for x in outs] + [dma((2, NV + 4))],
    )(*outs)
    return (outs[0][None],) + tuple(outs[1:])


def solution(mesh):
    wide = P("op", None, "blk", None, None)
    return jax.shard_map(
        per_device,
        mesh=mesh,
        in_specs=(wide, wide, wide) + (P(),) * 6 + (P("blk"),) + (P("blk", None),) * 3,
        out_specs=(wide, P(), P(), P(), P()),
        check_vma=False,
    )
```

```python
import functools
import math

import jax
import jax.numpy as jnp
from jax import lax
from jax.experimental import pallas as pl
from jax.experimental.pallas import tpu as pltpu
from jax.sharding import PartitionSpec as P

MESH = pl.DeviceIdType.MESH
tau = 0.2
passage_angle = 2.0 * math.pi / 36.0
cos_step = math.cos(passage_angle)
sin_step = math.sin(passage_angle)
f32 = jnp.float32
bf16 = jnp.bfloat16

NV, NS, BI, BJ, HID, NF = 6, 3, 32, 128, 256, 16
PL = 8
ZN = 4
NCH = 12
CW = 1024
EDGE = NCH - 1
AN = 16
BN = 8
HV = NV // 2
HALF = HV * BJ


def row_of(s, i):
    if i == 0 or i == BI - 1:
        return 8 * EDGE + 2 * s + (i != 0)
    inner = (BI - 2) * s + i - 1
    return inner if inner < 8 * EDGE else inner + 2 * NS


def runs(s):
    whole = (BI - 2) * s
    first = min(BI - 2, 8 * EDGE - whole)
    res = [(1, whole, first)]
    if first < BI - 2:
        res.append((1 + first, row_of(s, 1 + first), BI - 2 - first))
    return res


def nt(a, b):
    return lax.dot_general(a, b, (((1,), (1,)), ((), ())), preferred_element_type=f32)


def mm(a, b):
    return jnp.dot(a, b, preferred_element_type=f32)


def lanes_sum(u, lane):
    left = jnp.where(lane == 0, u, pltpu.roll(u, 1, 1))
    right = jnp.where(lane == BJ - 1, u, pltpu.roll(u, BJ - 1, 1))
    return left + right


def kernel(
    loss_scale,
    state_h, target_h, feat_h, coup, in_w, mid_w, top_w, out_w, biases, count, conn, orient, rot,
    out_h, out_in, out_mid, out_top, out_vec,
    out_state, state, target, feat, x0, x1, first0, first1, second0, second1, third0, third1,
    xs, win_t, wmid_t, wtop_t, bias_c, ow_c,
    mid_r, ts_r, tm_r, fc_r, beta_r, betan_r, bc_r, bcn_r,
    edge, gath, picked, arr, inner, tile_r, meta, sel_r, selt_r, ghost_r,
    cote, cz, tbl, ret,
    gtop, gmid, gin, gout,
    cg, gsum, ra, rb, full, sg, sa, sb, sf,
    pl_s, pl_r, me_s, me_r, zz_s, zz_r, cz_s, cz_r, rt_s, rt_r,
    in_s, c_s, c_r, a1_s, a1_r, a2_s, a2_r, a3_s, a3_r, f_s, f_r, s1_s, s1_r, s2_s, s2_r, s3_s, s3_r,
):
    x_r, first_r, second_r, third_r = (x0, x1), (first0, first1), (second0, second1), (third0, third1)
    b = lax.axis_index("blk")
    o = lax.axis_index("op")
    z = lax.div(b, PL)
    p = lax.rem(b, PL)

    plane_peers = [lax.rem(p + d, PL) for d in range(1, PL)]
    x_at = lax.div(o, 2)
    z_lo = lax.rem(o, 2)
    core = lax.rem(b, 2)
    mine = z * 2 + core
    tower = [lax.rem(mine + d, 2 * ZN) for d in range(1, 2 * ZN)]
    a = x_at * ZN + lax.div(p, 2)
    zz = z * 2 + z_lo

    def at_plane(q):
        return {"blk": z * PL + q}

    def at_tower(w):
        return {"blk": lax.div(w, 2) * PL + p - core + lax.rem(w, 2)}

    def at_a(q):
        return {"blk": z * PL + lax.rem(q, 4) * 2 + core, "op": lax.div(q, 4) * 2 + z_lo}

    def at_zc(w, c):
        return {"blk": lax.div(w, 2) * PL + p - core + c, "op": x_at * 2 + lax.rem(w, 2)}

    def partner():
        return {"blk": b + 1 - 2 * core}

    def at_b(w):
        return {"blk": lax.div(w, 2) * PL + p, "op": x_at * 2 + lax.rem(w, 2)}

    def send(src, dst, s_sem, r_sem, device):
        copy = pltpu.make_async_remote_copy(
            src_ref=src, dst_ref=dst, send_sem=s_sem, recv_sem=r_sem, device_id=device, device_id_type=MESH
        )
        copy.start()

    def got(dst, s_sem, r_sem, device):
        pltpu.make_async_remote_copy(
            src_ref=dst, dst_ref=dst, send_sem=s_sem, recv_sem=r_sem, device_id=device, device_id_type=MESH
        ).wait_recv()

    def gone(src, s_sem, r_sem, device):
        pltpu.make_async_remote_copy(
            src_ref=src, dst_ref=src, send_sem=s_sem, recv_sem=r_sem, device_id=device, device_id_type=MESH
        ).wait_send()

    barrier = pltpu.get_barrier_semaphore()
    def greet(device):
        pl.semaphore_signal(barrier, inc=1, device_id=device, device_id_type=MESH)

    for q in plane_peers:
        greet(at_plane(q))
    for d in range(4, AN):
        greet(at_a(lax.rem(x_at * 4 + d, AN)))
    for d in range(1, BN):
        for c in range(2):
            greet(at_zc(lax.rem(zz + d, BN), c))

    loads = [pltpu.make_async_copy(h, v, in_s.at[i]) for i, (h, v) in enumerate(((state_h, state), (feat_h, feat), (target_h, target)))]
    for load in loads:
        load.start()

    rowi = lax.broadcasted_iota(jnp.int32, (8, BJ), 0)
    lane8 = lax.broadcasted_iota(jnp.int32, (8, BJ), 1)
    meta_t = jnp.full((8, BJ), -1.0, f32)
    flip_t = jnp.zeros((8, BJ), f32)
    cos_t = jnp.ones((8, BJ), f32)
    sin_t = jnp.zeros((8, BJ), f32)
    live_t = jnp.zeros((8, BJ), f32)
    live = []
    for s in range(NS):
        live.append(jnp.where(s < count[0], 1.0, 0.0).astype(f32))
        for e in range(2):
            here = rowi == 2 * s + e
            idx = conn[e, s]
            idx = idx + 2 * ((idx * 10923) >> 16)
            meta_t = jnp.where(here, idx.astype(f32), meta_t)
            flip_t = jnp.where(here, orient[e, s].astype(f32), flip_t)
            turn = rot[e, s]
            cos_t = jnp.where(here, jnp.where(turn == 0, 1.0, cos_step).astype(f32), cos_t)
            sin_t = jnp.where(here, turn.astype(f32) * sin_step, sin_t)
            live_t = jnp.where(here, live[s], live_t)
    meta[mine] = meta_t
    tile_r[0] = flip_t
    tile_r[1] = cos_t
    tile_r[2] = sin_t
    tile_r[3] = live_t

    def part(ref, v):
        return ref.at[v // HV, :, v % HV * BJ:(v % HV + 1) * BJ]

    def pack(dst, field, rows):
        dst[...] = jnp.zeros((2, 8, HALF), f32)
        for v in range(NV):
            for s in range(NS):
                for e in range(2):
                    part(dst, v)[2 * s + e:2 * s + e + 1, :] = field[v, s, rows[e]:rows[e] + 1, :]

    def cut(ref):
        return [part(ref, v)[...] for v in range(NV)]

    def thirds(u):
        u1 = u.astype(bf16)
        u2 = (u - u1.astype(f32)).astype(bf16)
        u3 = (u - u1.astype(f32) - u2.astype(f32)).astype(bf16)
        return u1, u2, u3

    def by_rows(mask, u):
        r = mm(mask, jnp.concatenate(thirds(u), axis=1))
        return r[:, :HALF] + r[:, HALF:2 * HALF] + r[:, 2 * HALF:]

    loads[0].wait()
    pack(edge.at[0], state, (0, BI - 1))

    pl.semaphore_wait(barrier, PL - 1 + AN - 4 + 2 * (BN - 1))

    def send_plane(k):
        for q in plane_peers:
            send(edge.at[k, lax.rem(q, 2)], gath.at[k, p], pl_s.at[k, q], pl_r.at[k, p], at_plane(q))
        gath[k, p] = edge[k, core]

    for w in tower:
        send(meta.at[mine], meta.at[mine], me_s.at[w], me_r.at[mine], at_tower(w))
    send_plane(0)

    def pick(k):
        for q in plane_peers:
            got(gath.at[k, q], pl_s.at[k, q], pl_r.at[k, q], at_plane(q))
        chosen = by_rows(sel_r[...], gath[k].reshape(PL * 8, HALF))
        picked[k] = chosen.reshape(2 * ZN, 8, HALF)
        arr[k, mine] = picked[k, mine]
        for w in tower:
            send(picked.at[k, w], arr.at[k, mine], zz_s.at[k, w], zz_r.at[k, mine], at_tower(w))

    def make_sel():
        for w in tower:
            got(meta.at[w], me_s.at[w], me_r.at[w], at_tower(w))
        n = 2 * ZN * 8
        lane = lax.broadcasted_iota(jnp.int32, (n, BJ), 1)
        named = meta[...].reshape(n, BJ)
        local = named - (z * (PL * 8)).astype(f32)
        sel = jnp.where((local == lane.astype(f32)) & (lane < PL * 8), 1.0, 0.0).astype(f32)
        sel_r[...] = sel[:, :PL * 8].astype(bf16)
        wide = jnp.concatenate([sel, jnp.zeros((BJ - n, BJ), f32)], axis=0).T
        selt_r[...] = wide[:PL * 8, :n].astype(bf16)

    def turned(parts, sign):
        flip, cos, sin = tile_r[0], tile_r[1], tile_r[2] * sign
        r = lax.broadcasted_iota(jnp.int32, (BJ, BJ), 0)
        c = lax.broadcasted_iota(jnp.int32, (BJ, BJ), 1)
        anti = jnp.where(r + c == BJ - 1, 1.0, 0.0).astype(bf16)
        n = 8 * NV
        back = mm(jnp.concatenate(thirds(jnp.concatenate(parts, axis=0)), axis=0), anti)
        back = back[:n] + back[n:2 * n] + back[2 * n:]
        out = [jnp.where(flip > 0.5, back[8 * v:8 * v + 8], parts[v]) for v in range(NV)]
        c2 = cos * out[2] - sin * out[3]
        c3 = sin * out[2] + cos * out[3]
        return [out[0], out[1], c2, c3, out[4], out[5]]

    def ghosts(k):
        for w in tower:
            got(arr.at[k, w], zz_s.at[k, w], zz_r.at[k, w], at_tower(w))
        total = [(arr[k, h] + arr[k, 2 + h]) + (arr[k, 4 + h] + arr[k, 6 + h]) for h in range(2)]
        parts = turned([total[v // HV][:, v % HV * BJ:(v % HV + 1) * BJ] for v in range(NV)], 1.0)
        for v in range(NV):
            ghost_r[k, v] = parts[v]

    def edge_sweep(e, n, gh):
        res = []
        beta_e = jnp.where(rowi < 2 * NS, beta_r[8 * EDGE:8 * EDGE + 8, :], 0.0)
        for v in range(NV):
            lap = gh[v] + n[v] + lanes_sum(e[v], lane8) - 4.0 * e[v]
            coupled = coup[v, 0] * e[0]
            for w in range(1, NV):
                coupled = coupled + coup[v, w] * e[w]
            res.append(e[v] + tau * (lap - coupled + beta_e * jnp.tanh(e[v])))
        return res

    pad = jnp.zeros((BJ - NF, HID), f32)
    win_t[...] = jnp.concatenate([in_w[...].astype(f32), pad], axis=0).T[:, :NF].astype(bf16)
    wmid_t[...] = mid_w[...].astype(f32).T.astype(bf16)
    wtop_t[...] = top_w[...].astype(f32).T.astype(bf16)
    for k in range(3):
        bias_c[k] = jnp.broadcast_to(biases[k:k + 1, :], (BJ, HID)).T
    ow_c[...] = jnp.broadcast_to(out_w[...].astype(f32).reshape(1, HID), (BJ, HID)).T

    loads[1].wait()
    for s in range(NS):
        for h in range(2):
            xs[s, h] = feat[:, s, 16 * h:16 * h + 16, :].astype(f32).reshape(NF * 16, BJ)
    for s in range(NS):
        for h in range(2):
            for r in range(16):
                row = row_of(s, 16 * h + r)
                x_r[row // 8 % 2][row // 16, :, (row % 8) * BJ:(row % 8 + 1) * BJ] = xs[s, h, pl.ds(r, NF, stride=16), :].astype(bf16)

    SUB = 512

    weights = (win_t, wmid_t, wtop_t)
    acts = (x_r, first_r, second_r, third_r)
    SUBS = 2 * CW // SUB

    def forward(k, carry):
        pair = (lax.rem(k + EDGE // 2, NCH // 2), k)

        def place(j):
            half = j // (CW // SUB)
            return 1 - half, pair[half], slice((j % (CW // SUB)) * SUB, (j % (CW // SUB) + 1) * SUB)

        def product(layer, j):
            par, c, cols = place(j)
            return mm(weights[layer][...], acts[layer][par][c, :, cols])

        tiles = [jnp.zeros((8, BJ), f32), jnp.zeros((8, BJ), f32)]

        def activate(layer, j, d):
            par, c, cols = place(j)
            bias = bias_c[layer]
            for i in range(SUB // BJ):
                t = jnp.tanh(d[:, i * BJ:(i + 1) * BJ] + bias).astype(bf16)
                acts[layer + 1][par][c, :, cols.start + i * BJ:cols.start + (i + 1) * BJ] = t
                if layer == 2:
                    bt = jnp.sum(ow_c[...] * t.astype(f32), axis=0, keepdims=True) + 1.0
                    row = (j % (CW // SUB)) * (SUB // BJ) + i
                    half = j // (CW // SUB)
                    tiles[half] = jnp.where(rowi == row, bt, tiles[half])

        tasks = [(layer, j) for layer in range(3) for j in range(SUBS)]
        held = None
        for task in tasks:
            d = product(*task)
            if held is not None:
                activate(*held)
            held = task + (d,)
        activate(*held)
        for half in range(2):
            beta_r[pl.ds(pl.multiple_of((2 * pair[half] + 1 - half) * 8, 8), 8), :] = tiles[half]

        @pl.when(k == 0)
        def _():
            make_sel()
            pick(0)

        @pl.when(k == 2)
        def _():
            ghosts(0)
            pack(inner, state, (1, BI - 2))
            res = edge_sweep(cut(edge.at[0]), cut(inner), [ghost_r[0, v] for v in range(NV)])
            for v in range(NV):
                part(edge.at[1], v)[...] = res[v]
            send_plane(1)

        @pl.when(k == 4)
        def _():
            pick(1)

        return carry

    lax.fori_loop(0, NCH // 2, forward, 0)

    for s in range(NS):
        for e in range(2):
            g = 8 * EDGE + 2 * s + e
            row = s * BI + e * (BI - 1)
            betan_r[row:row + 1, :] = beta_r[g:g + 1, :]
        for first, place, length in runs(s):
            betan_r[s * BI + first:s * BI + first + length, :] = beta_r[place:place + length, :]

    rows32 = lax.broadcasted_iota(jnp.int32, (BI, BJ), 0)
    lane32 = lax.broadcasted_iota(jnp.int32, (BI, BJ), 1)

    def stencil(u, low, high):
        up = jnp.where(rows32 == 0, low, pltpu.roll(u, 1, 0))
        down = jnp.where(rows32 == BI - 1, high, pltpu.roll(u, BI - 1, 0))
        return up + down + lanes_sum(u, lane32) - 4.0 * u

    def low_high(k, s, v):
        return ghost_r[k, v, 2 * s:2 * s + 1, :], ghost_r[k, v, 2 * s + 1:2 * s + 2, :]

    for s in range(NS):
        us = [state[v, s] for v in range(NV)]
        beta = betan_r[s * BI:(s + 1) * BI, :]
        for v in range(NV):
            t = jnp.tanh(us[v])
            ts_r[v, s] = t
            low, high = low_high(0, s, v)
            coupled = coup[v, 0] * us[0]
            for w in range(1, NV):
                coupled = coupled + coup[v, w] * us[w]
            mid_r[v, s] = us[v] + tau * (stencil(us[v], low, high) - coupled + beta * t)

    ghosts(1)
    pack(inner, mid_r, (1, BI - 2))
    final_e = edge_sweep(cut(edge.at[1]), cut(inner), [ghost_r[1, v] for v in range(NV)])
    loads[2].wait()
    pack(inner, target, (0, BI - 1))
    goal_e = cut(inner)
    cot_e = [tau * (loss_scale * tile_r[3] * (final_e[v] - goal_e[v])) for v in range(NV)]
    cot_e = turned(cot_e, -1.0)
    for v in range(NV):
        part(cote, v)[...] = cot_e[v]
    cz[mine] = cote[core]
    for w in tower:
        send(cote.at[lax.rem(w, 2)], cz.at[mine], cz_s.at[w], cz_r.at[mine], at_tower(w))

    for s in range(NS):
        us = [mid_r[v, s] for v in range(NV)]
        beta = betan_r[s * BI:(s + 1) * BI, :]
        for v in range(NV):
            t = jnp.tanh(us[v])
            tm_r[v, s] = t
            low, high = low_high(1, s, v)
            coupled = coup[v, 0] * us[0]
            for w in range(1, NV):
                coupled = coupled + coup[v, w] * us[w]
            final = us[v] + tau * (stencil(us[v], low, high) - coupled + beta * t)
            out_state[v, s] = live[s] * final
            fc_r[v, s] = loss_scale * live[s] * (final - target[v, s])

    for s in range(NS):
        gs = [fc_r[v, s] for v in range(NV)]
        beta = betan_r[s * BI:(s + 1) * BI, :]
        acc = jnp.zeros((BI, BJ), f32)
        for v in range(NV):
            t = tm_r[v, s]
            coupled = coup[0, v] * gs[0]
            for w in range(1, NV):
                coupled = coupled + coup[w, v] * gs[w]
            mc = gs[v] + tau * (stencil(gs[v], 0.0, 0.0) - coupled + beta * (1.0 - t * t) * gs[v])
            acc = acc + (gs[v] * t + mc * ts_r[v, s])
        bcn_r[s * BI:(s + 1) * BI, :] = tau * acc
        for first, place, length in runs(s):
            bc_r[place:place + length, :] = bcn_r[s * BI + first:s * BI + first + length, :]

    leave = pltpu.make_async_copy(out_state, out_h, in_s.at[3])
    leave.start()

    def table():
        for w in tower:
            got(cz.at[w], cz_s.at[w], cz_r.at[w], at_tower(w))
        sums = by_rows(selt_r[...], cz[...].reshape(2 * ZN * 8, HALF))
        tbl[...] = sums.reshape(PL, 8, HALF)
        ret[p] = tbl[p]
        for q in plane_peers:
            send(tbl.at[q], ret.at[p], rt_s.at[q], rt_r.at[p], at_plane(q))

    def returned():
        for q in plane_peers:
            got(ret.at[q], rt_s.at[q], rt_r.at[q], at_plane(q))
        extra = jnp.zeros((8, BJ), f32)
        for h in range(2):
            total = (ret[h] + ret[2 + h]) + (ret[4 + h] + ret[6 + h])
            for v in range(HV):
                cols = slice(v * BJ, (v + 1) * BJ)
                extra = extra + total[:, cols] * jnp.tanh(edge[0, h, :, cols])
        for s in range(NS):
            for e in range(2):
                g = 2 * s + e
                row = s * BI + e * (BI - 1)
                bc_r[8 * EDGE + g:8 * EDGE + g + 1, :] = bcn_r[row:row + 1, :] + tau * extra[g:g + 1]

    ones = jnp.ones((16, CW), bf16)
    gout[...] = jnp.zeros((HID, BJ), f32)
    gtop[...] = jnp.zeros((HID + 16, HID), f32)
    gmid[...] = jnp.zeros((HID + 16, HID), f32)
    gin[...] = jnp.zeros((NF + 16, HID), f32)

    def weigh(par, k, acc, left, right, fresh=None):
        part = nt(jnp.concatenate([left[par][k], ones], axis=0), right[par][k])
        if fresh is not None:
            part = jnp.where(fresh, part, 0.0)
        acc[...] = acc[...] + part

    def before(k):
        return lax.rem(k + NCH // 2 - 1, NCH // 2)

    RB = 64

    def top_delta(par, k):
        third = third_r[par]
        bc = bc_r[pl.ds(pl.multiple_of((2 * k + par) * 8, 8), 8), :]
        ch = bc.astype(bf16).astype(f32)
        for i in range(HID // RB):
            rows = slice(i * RB, (i + 1) * RB)
            ow = ow_c[rows]
            acc = gout[rows]
            for j in range(CW // BJ):
                cols = slice(j * BJ, (j + 1) * BJ)
                t = third[k, rows, cols].astype(f32)
                acc = acc + t * ch[j:j + 1]
                third[k, rows, cols] = (ow * bc[j:j + 1] * (1.0 - t * t)).astype(bf16)
            gout[rows] = acc

    def back_top(k, carry):
        weigh(1, before(k), gtop, second_r, third_r, k > 0)
        top_delta(0, k)
        weigh(0, k, gtop, second_r, third_r)
        top_delta(1, k)
        return carry

    def layer_back(k, weight, source, act, acc, left, fresh=None):
        held = None

        def put(par, cols, d):
            for i in range(SUB // BJ):
                here = slice(cols.start + i * BJ, cols.start + (i + 1) * BJ)
                t = act[par][k, :, here].astype(f32)
                act[par][k, :, here] = (d[:, i * BJ:(i + 1) * BJ] * (1.0 - t * t)).astype(bf16)

        for par in range(2):
            for j in range(CW // SUB):
                cols = slice(j * SUB, (j + 1) * SUB)
                d = mm(weight[...], source[par][k, :, cols])
                if held is not None:
                    put(*held)
                held = (par, cols, d)
                if j == 0:
                    if par == 0:
                        weigh(1, before(k), acc, left, act, fresh)
                    else:
                        put(*held)
                        held = None
                        weigh(0, k, acc, left, act)
        put(*held)

    def back_mid(k, carry):
        layer_back(k, top_w, third_r, second_r, gmid, first_r, k > 0)
        return carry

    grads = (gtop, gmid)
    HR = HID // 2
    R = HR // AN

    def hand(i):
        other = pl.ds(pl.multiple_of((1 - core) * HR, HR), HR)
        send(grads[i].at[other], cg.at[i], c_s.at[i], c_r.at[i], partner())

    def ar_1(i):
        got(cg.at[i], c_s.at[i], c_r.at[i], partner())
        half = grads[i][pl.ds(pl.multiple_of(core * HR, HR), HR), :] + cg[i]
        gsum[i] = half.reshape(AN, R, HID)
        for d in range(1, AN):
            q = lax.rem(a + d, AN)
            send(gsum.at[i, q], ra.at[i, a], a1_s.at[i], a1_r.at[i], at_a(q))
        ra[i, a] = gsum[i, a]

    def ar_2(i):
        got(ra.at[i, pl.ds(0, AN - 1)], a1_s.at[i], a1_r.at[i], at_b(zz))
        total = ra[i, 0]
        for q in range(1, AN):
            total = total + ra[i, q]
        rb[i, zz] = total
        for d in range(1, BN):
            send(rb.at[i, zz], rb.at[i, zz], a2_s.at[i], a2_r.at[i], at_b(lax.rem(zz + d, BN)))

    def ar_3(i):
        got(rb.at[i, pl.ds(0, BN - 1)], a2_s.at[i], a2_r.at[i], at_b(zz))
        total = rb[i, 0]
        for w in range(1, BN):
            total = total + rb[i, w]
        full[i, core, a] = total
        for d in range(1, AN):
            send(full.at[i, core, a], full.at[i, core, a], a3_s.at[i], a3_r.at[i], at_a(lax.rem(a + d, AN)))

    def ar_4(i):
        got(full.at[i, core, pl.ds(0, AN - 1)], a3_s.at[i], a3_r.at[i], at_b(zz))
        send(full.at[i, core], full.at[i, core], f_s.at[i], f_r.at[i], partner())

    def ar_5(i, out):
        got(full.at[i, 1 - core], f_s.at[i], f_r.at[i], partner())
        out[...] = full[i].reshape(HID, HID)

    def small_1():
        for r in range(NF):
            sg[r // 2, r % 2:r % 2 + 1] = gin[r:r + 1]
        sg[NF // 2, 0:1] = jnp.sum(gout[...].T, axis=0, keepdims=True)
        sg[NF // 2, 1:2] = gin[NF:NF + 1]
        sg[NF // 2 + 1, 0:1] = gmid[HID:HID + 1]
        sg[NF // 2 + 1, 1:2] = gtop[HID:HID + 1]
        sg[NF // 2 + 2:] = jnp.zeros((AN - NF // 2 - 2, 2, HID), f32)
        for d in range(1, AN):
            q = lax.rem(a + d, AN)
            send(sg.at[q], sa.at[a], s1_s, s1_r, at_a(q))
        sa[a] = sg[a]

    def small_2():
        got(sa.at[pl.ds(0, AN - 1)], s1_s, s1_r, at_a(a))
        total = sa[0]
        for q in range(1, AN):
            total = total + sa[q]
        own = 2 * zz + core
        sb[own] = total
        send(sb.at[own], sb.at[own], s2_s, s2_r, partner())
        for d in range(1, BN):
            for c in range(2):
                send(sb.at[own], sb.at[own], s2_s, s2_r, at_zc(lax.rem(zz + d, BN), c))

    def small_3():
        got(sb.at[pl.ds(0, 2 * BN - 1)], s2_s, s2_r, at_b(zz))
        total = sb[0]
        for w in range(1, 2 * BN):
            total = total + sb[w]
        sf[a] = total
        for d in range(1, AN):
            send(sf.at[a], sf.at[a], s3_s, s3_r, at_a(lax.rem(a + d, AN)))

    def small_4():
        got(sf.at[pl.ds(0, AN - 1)], s3_s, s3_r, at_a(a))
        for r in range(NF):
            out_in[r:r + 1] = sf[r // 2, r % 2:r % 2 + 1]
        for r in range(4):
            out_vec[r:r + 1] = sf[(NF + r) // 2, r % 2:r % 2 + 1]

    LAST = NCH // 2 - 1
    lax.fori_loop(0, LAST, back_top, 0)
    weigh(1, LAST - 1, gtop, second_r, third_r)
    table()
    top_delta(0, LAST)
    weigh(0, LAST, gtop, second_r, third_r)
    def back_mid_first(k, carry):
        @pl.when(k == 3)
        def _():
            returned()
            top_delta(1, LAST)
            weigh(1, LAST, gtop, second_r, third_r)
            hand(0)

        return back_mid(k, carry)

    lax.fori_loop(0, LAST, back_mid_first, 0)
    layer_back(LAST, top_w, third_r, second_r, gmid, first_r)
    weigh(1, LAST, gmid, first_r, second_r)
    hand(1)
    ar_1(0)

    def back_first(k, carry):
        layer_back(k, mid_w, second_r, first_r, gin, x_r, k > 0)

        @pl.when(k == 1)
        def _():
            ar_1(1)

        @pl.when(k == 3)
        def _():
            ar_2(0)

        @pl.when(k == 5)
        def _():
            ar_2(1)

        return carry

    lax.fori_loop(0, LAST + 1, back_first, 0)
    weigh(1, LAST, gin, x_r, first_r)

    small_1()
    ar_3(0)
    ar_3(1)
    small_2()
    ar_4(0)
    ar_4(1)
    small_3()
    ar_5(0, out_top)
    ar_5(1, out_mid)
    small_4()

    leave.wait()
    for k in range(2):
        for q in plane_peers:
            gone(edge.at[k, core], pl_s.at[k, q], pl_r.at[k, p], at_plane(q))
        for w in tower:
            gone(picked.at[k, w], zz_s.at[k, w], zz_r.at[k, mine], at_tower(w))
    for w in tower:
        gone(meta.at[mine], me_s.at[w], me_r.at[mine], at_tower(w))
        gone(cote.at[core], cz_s.at[w], cz_r.at[mine], at_tower(w))
    for q in plane_peers:
        gone(tbl.at[q], rt_s.at[q], rt_r.at[p], at_plane(q))
    for i in range(2):
        gone(cg.at[i], c_s.at[i], c_r.at[i], partner())
        gone(ra.at[i, pl.ds(0, AN - 1)], a1_s.at[i], a1_r.at[i], at_b(zz))
        gone(rb.at[i, pl.ds(0, BN - 1)], a2_s.at[i], a2_r.at[i], at_b(zz))
        gone(ra.at[i, pl.ds(0, AN - 1)], a3_s.at[i], a3_r.at[i], at_b(zz))
        gone(cg.at[i], f_s.at[i], f_r.at[i], partner())
    gone(sa.at[pl.ds(0, AN - 1)], s1_s, s1_r, at_a(a))
    gone(sb.at[pl.ds(0, 2 * BN - 1)], s2_s, s2_r, at_b(zz))
    gone(sf.at[pl.ds(0, AN - 1)], s3_s, s3_r, at_a(a))


def copy_kernel(*refs):
    ins, outs, held, sem = refs[:5], refs[5:10], refs[10:15], refs[15]
    parts = [(0, slice(v, v + 1)) for v in range(NV)] + [(i, slice(None)) for i in range(1, 5)]
    come = [pltpu.make_async_copy(ins[i].at[at], held[i].at[at], sem.at[0, n]) for n, (i, at) in enumerate(parts)]
    go = [pltpu.make_async_copy(held[i].at[at], outs[i].at[at], sem.at[1, n]) for n, (i, at) in enumerate(parts)]
    for copy in come:
        copy.start()
    for first, then in zip(come, go):
        first.wait()
        then.start()
    for copy in go:
        copy.wait()


def per_device(
    initial_state, target, features, coupling, in_weight, mid_weight, top_weight, out_weight, biases,
    block_count, connectivity, orientation, rotation,
):
    cells = lax.axis_size("op") * lax.axis_size("blk") * NS * BI * BJ
    loss_scale = 2.0 / math.sqrt(cells)
    vmem = pl.BlockSpec(memory_space=pltpu.VMEM)
    smem = pl.BlockSpec(memory_space=pltpu.SMEM)
    anywhere = pl.BlockSpec(memory_space=pl.ANY)
    dma = pltpu.SemaphoreType.DMA
    field = pltpu.VMEM((NV, NS, BI, BJ), f32)
    outs = pl.pallas_call(
        functools.partial(kernel, loss_scale),
        out_shape=(
            jax.ShapeDtypeStruct((NV, NS, BI, BJ), f32),
            jax.ShapeDtypeStruct((NF, HID), f32),
            jax.ShapeDtypeStruct((HID, HID), f32),
            jax.ShapeDtypeStruct((HID, HID), f32),
            jax.ShapeDtypeStruct((4, HID), f32),
        ),
        in_specs=[anywhere, anywhere, anywhere, smem, vmem, vmem, vmem, vmem, vmem, smem, smem, smem, smem],
        out_specs=(anywhere, vmem, vmem, vmem, vmem),
        scratch_shapes=[
            field, field, field, pltpu.VMEM((NF, NS, BI, BJ), bf16),
            pltpu.VMEM((NCH // 2, NF, CW), bf16),
            pltpu.VMEM((NCH // 2, NF, CW), bf16),
            pltpu.VMEM((NCH // 2, HID, CW), bf16),
            pltpu.VMEM((NCH // 2, HID, CW), bf16),
            pltpu.VMEM((NCH // 2, HID, CW), bf16),
            pltpu.VMEM((NCH // 2, HID, CW), bf16),
            pltpu.VMEM((NCH // 2, HID, CW), bf16),
            pltpu.VMEM((NCH // 2, HID, CW), bf16),
            pltpu.VMEM((NS, 2, NF * 16, BJ), f32),
            pltpu.VMEM((HID, NF), bf16),
            pltpu.VMEM((HID, HID), bf16),
            pltpu.VMEM((HID, HID), bf16),
            pltpu.VMEM((3, HID, BJ), f32),
            pltpu.VMEM((HID, BJ), f32),
            field, field, field, field,
            pltpu.VMEM((NS * BI, BJ), f32),
            pltpu.VMEM((NS * BI, BJ), f32),
            pltpu.VMEM((NS * BI, BJ), f32),
            pltpu.VMEM((NS * BI, BJ), f32),
            pltpu.VMEM((2, 2, 8, HALF), f32),
            pltpu.VMEM((2, PL, 8, HALF), f32),
            pltpu.VMEM((2, 2 * ZN, 8, HALF), f32),
            pltpu.VMEM((2, 2 * ZN, 8, HALF), f32),
            pltpu.VMEM((2, 8, HALF), f32),
            pltpu.VMEM((4, 8, BJ), f32),
            pltpu.VMEM((2 * ZN, 8, BJ), f32),
            pltpu.VMEM((2 * ZN * 8, PL * 8), bf16),
            pltpu.VMEM((PL * 8, 2 * ZN * 8), bf16),
            pltpu.VMEM((2, NV, 8, BJ), f32),
            pltpu.VMEM((2, 8, HALF), f32),
            pltpu.VMEM((2 * ZN, 8, HALF), f32),
            pltpu.VMEM((PL, 8, HALF), f32),
            pltpu.VMEM((PL, 8, HALF), f32),
            pltpu.VMEM((HID + 16, HID), f32),
            pltpu.VMEM((HID + 16, HID), f32),
            pltpu.VMEM((NF + 16, HID), f32),
            pltpu.VMEM((HID, BJ), f32),
            pltpu.VMEM((2, HID // 2, HID), f32),
            pltpu.VMEM((2, AN, HID // 2 // AN, HID), f32),
            pltpu.VMEM((2, AN, HID // 2 // AN, HID), f32),
            pltpu.VMEM((2, BN, HID // 2 // AN, HID), f32),
            pltpu.VMEM((2, 2, AN, HID // 2 // AN, HID), f32),
            pltpu.VMEM((AN, 2, HID), f32),
            pltpu.VMEM((AN, 2, HID), f32),
            pltpu.VMEM((2 * BN, 2, HID), f32),
            pltpu.VMEM((AN, 2, HID), f32),
            dma((2, PL)), dma((2, PL)), dma((2 * ZN,)), dma((2 * ZN,)), dma((2, 2 * ZN)), dma((2, 2 * ZN)),
            dma((2 * ZN,)), dma((2 * ZN,)), dma((PL,)), dma((PL,)),
            dma((4,)), dma((2,)), dma((2,)), dma((2,)), dma((2,)), dma((2,)), dma((2,)), dma((2,)), dma((2,)), dma((2,)), dma((2,)),
            dma, dma, dma, dma, dma, dma,
        ],
        compiler_params=pltpu.CompilerParams(
            collective_id=0, has_side_effects=True, vmem_limit_bytes=56 * 2**20
        ),
    )(
        initial_state[0], target[0], features[0], coupling, in_weight, mid_weight, top_weight,
        out_weight, biases, block_count, connectivity.T, orientation.T, rotation.T,
    )
    outs = pl.pallas_call(
        copy_kernel,
        out_shape=tuple(jax.ShapeDtypeStruct(x.shape, x.dtype) for x in outs),
        in_specs=[anywhere] * 5,
        out_specs=(anywhere,) * 5,
        scratch_shapes=[pltpu.VMEM(x.shape, x.dtype) for x in outs] + [dma((2, NV + 4))],
    )(*outs)
    return (outs[0][None],) + tuple(outs[1:])


def solution(mesh):
    wide = P("op", None, "blk", None, None)
    return jax.shard_map(
        per_device,
        mesh=mesh,
        in_specs=(wide, wide, wide) + (P(),) * 6 + (P("blk"),) + (P("blk", None),) * 3,
        out_specs=(wide, P(), P(), P(), P()),
        check_vma=False,
    )
```
